128 devices in a mesh: fsdp: 8 (over y, z_lo), seq: 16 (over x, z_hi, core).
Axes of the slice: x: 4, y: 4, z: 4 (z_hi: 2, z_lo: 2; z = z_hi * 2 + z_lo), core: 2. Of those that a mesh axis runs over, the one named last changes fastest.
Arguments:
- inputs: bfloat16 [32768, 1024], P(('fsdp', 'seq')), may hold values from -6 to 6
- cotangent: bfloat16 [32768, 1024], P(('fsdp', 'seq')), may hold values from -6 to 6
- ln_attn_gain: bfloat16 [1024], P('fsdp'), may hold values from 0.099609375 to 1.8984375
- ln_attn_bias: bfloat16 [1024], P('fsdp'), may hold values from -3 to 3
- ln_mlp_gain: bfloat16 [1024], P('fsdp'), may hold values from 0.099609375 to 1.8984375
- ln_mlp_bias: bfloat16 [1024], P('fsdp'), may hold values from -3 to 3
- qkv_weight: bfloat16 [1024, 3072], P('fsdp'), may hold values from -0.25 to 0.25
- qkv_bias: bfloat16 [3072], P('fsdp'), may hold values from -3 to 3
- dense_weight: bfloat16 [1024, 1024], P('fsdp'), may hold values from -1.5 to 1.5
- dense_bias: bfloat16 [1024], P('fsdp'), may hold values from -3 to 3
- hidden_weight: bfloat16 [1024, 4096], P('fsdp'), may hold values from -0.1875 to 0.1875
- hidden_bias: bfloat16 [4096], P('fsdp'), may hold values from -3 to 3
- output_weight: bfloat16 [4096, 1024], P('fsdp'), may hold values from -0.09375 to 0.09375
- output_bias: bfloat16 [1024], P('fsdp'), may hold values from -3 to 3
Outputs:
- outputs: bfloat16 [32768, 1024], P(('fsdp', 'seq'))
- input_grad: float32 [32768, 1024], P(('fsdp', 'seq'))
- ln_attn_gain_grad: float32 [1024], P('fsdp')
- ln_attn_bias_grad: float32 [1024], P('fsdp')
- ln_mlp_gain_grad: float32 [1024], P('fsdp')
- ln_mlp_bias_grad: float32 [1024], P('fsdp')
- qkv_weight_grad: float32 [1024, 3072], P('fsdp')
- qkv_bias_grad: float32 [3072], P('fsdp')
- dense_weight_grad: float32 [1024, 1024], P('fsdp')
- dense_bias_grad: float32 [1024], P('fsdp')
- hidden_weight_grad: float32 [1024, 4096], P('fsdp')
- hidden_bias_grad: float32 [4096], P('fsdp')
- output_weight_grad: float32 [4096, 1024], P('fsdp')
- output_bias_grad: float32 [1024], P('fsdp')
The draws below stay inside these ranges and needn't reach their ends.
All inputs are finite; a program needn't handle non-finite values.
Results may differ from the reference program's by a relative error of at most 0.023.
Values may be sent and summed in bfloat16 or wider, within the bound.
A program may use at most 256 MiB of HBM per device.

```python
import math
import jax
import jax.numpy as jnp
from jax import lax

D = 1024
FF = 4096
HEADS = 16
HEAD = 64
ROT = 16
LENGTH = 4096
SEQS = 8
TOKENS = 32768


def block_levels(own_key, extent, pieces, low, largest):
    gain = 1.0
    for axis_at, blocks in pieces:
        heights = jax.random.uniform(jax.random.fold_in(jax.random.fold_in(own_key, 6), axis_at), (blocks,), jnp.float32, low / len(pieces), largest / len(pieces))
        gain = gain * jnp.repeat(jnp.exp(heights), extent[axis_at] // blocks).reshape((-1,) + (1,) * (len(extent) - 1 - axis_at))
    return gain


def normal_values(rng, shape, deviation, most, cuts=(), kind=jnp.bfloat16):
    gain = block_levels(rng, shape, cuts, -0.22, 0.18) if cuts else 1.0
    entries = jax.random.normal(rng, shape, jnp.float32) * deviation * gain
    return jnp.minimum(jnp.maximum(entries, -most), most).astype(kind)


def setup_inputs(seed: int = 0) -> dict:
    key_list = jax.random.split(jax.random.key(seed), 15)
    return {
        "inputs": normal_values(key_list[0], (TOKENS, D), 1.0, 6.0, ((0, 128),)),
        "cotangent": normal_values(key_list[1], (TOKENS, D), 1.0, 6.0, ((0, 128),)),
        "ln_attn_gain": jnp.clip(1.0 + 0.18 * jax.random.normal(key_list[2], (D,), jnp.float32), 0.099609375, 1.8984375).astype(jnp.bfloat16),
        "ln_attn_bias": normal_values(key_list[3], (D,), 0.5, 3.0, ((0, 8),)),
        "ln_mlp_gain": jnp.clip(1.0 + 0.18 * jax.random.normal(key_list[4], (D,), jnp.float32), 0.099609375, 1.8984375).astype(jnp.bfloat16),
        "ln_mlp_bias": normal_values(key_list[5], (D,), 0.5, 3.0, ((0, 8),)),
        "qkv_weight": normal_values(key_list[6], (D, 3 * D), (D // 2) ** -0.5, 0.25, ((0, 8),)),
        "qkv_bias": normal_values(key_list[7], (3 * D,), 0.5, 3.0, ((0, 8),)),
        "dense_weight": normal_values(key_list[8], (D, D), (D // 64) ** -0.5, 1.5, ((0, 8),)),
        "dense_bias": normal_values(key_list[9], (D,), 0.5, 3.0, ((0, 8),)),
        "hidden_weight": normal_values(key_list[10], (D, FF), D ** -0.5, 0.1875, ((0, 8),)),
        "hidden_bias": normal_values(key_list[11], (FF,), 0.5, 3.0, ((0, 8),)),
        "output_weight": normal_values(key_list[12], (FF, D), FF ** -0.5, 0.09375, ((0, 8),)),
        "output_bias": normal_values(key_list[13], (D,), 0.5, 3.0, ((0, 8),)),
    }


@jax.custom_vjp
def low(v):
    return lax.optimization_barrier(v.astype(jnp.bfloat16)).astype(jnp.float32)

@jax.custom_vjp
def low_back(v):
    return v

def low_keep(v):
    return (low(v), None)

def low_pass(kept, grad):
    return (grad,)

def back_keep(v):
    return (v, None)

def back_low(kept, grad):
    return (low(grad),)
low.defvjp(low_keep, low_pass)
low_back.defvjp(back_keep, back_low)
epsilon = 1e-05
negative_fill = -1e+30
highest = lax.Precision.HIGHEST

def layer_norm(values, gain_vector, offset):
    centered = values - lax.optimization_barrier(jnp.mean(values, axis=-1, keepdims=True))
    variance = lax.optimization_barrier(jnp.mean(centered * centered, axis=-1, keepdims=True))
    return centered * lax.rsqrt(variance + epsilon) * gain_vector + offset

def rotary_tables(positions, rotary_width):
    half_width = rotary_width // 2
    frequency = 10000.0 ** (-2.0 * jnp.arange(half_width, dtype=jnp.float32) / rotary_width)
    angles = positions.astype(jnp.float32)[:, None] * frequency[None, :]
    angles = jnp.concatenate([angles, angles], axis=-1)
    return (jnp.cos(angles), jnp.sin(angles))

def rotate(head_data, cosine_table, sine_table, rotary_width):
    turned = head_data[:, :, :2, :rotary_width]
    leading = turned[..., :rotary_width // 2]
    trailing = turned[..., rotary_width // 2:]
    swapped = jnp.concatenate([-trailing, leading], axis=-1)
    turned = turned * cosine_table[:, None, None, :] + swapped * sine_table[:, None, None, :]
    return head_data.at[:, :, :2, :rotary_width].set(turned)

def attention(head_data):
    length = head_data.shape[0]
    queries = head_data[:, :, 0]
    key_rows = head_data[:, :, 1]
    value_rows = head_data[:, :, 2]
    block_rows = min(length, max(512, length // 8))
    score_scale = 1.0 / math.sqrt(HEAD)
    col_ids = jnp.arange(length, dtype=jnp.int32)

    def one_block(block_index):
        begin_row = block_index * block_rows
        block_queries = lax.dynamic_slice_in_dim(queries, begin_row, block_rows, 0)
        scores = low_back(jnp.einsum('qhd,khd->hqk', block_queries, key_rows, precision=highest) * score_scale)
        row_ids = begin_row + jnp.arange(block_rows, dtype=jnp.int32)
        causal_mask = col_ids[None, None, :] <= row_ids[None, :, None]
        scores = jnp.where(causal_mask, scores, negative_fill)
        row_max = lax.optimization_barrier(jnp.max(scores, axis=-1, keepdims=True))
        exponent = jnp.exp(scores - row_max)
        probabilities = exponent / lax.optimization_barrier(jnp.sum(exponent, axis=-1, keepdims=True))
        return jnp.einsum('hqk,khd->qhd', low(probabilities), value_rows, precision=highest)
    blocks = lax.map(jax.checkpoint(one_block), jnp.arange(length // block_rows, dtype=jnp.int32))
    return blocks.reshape(length, HEADS, HEAD)

def sequence_forward(sequence, params):
    attn_gain, attn_offset, mlp_gain, mlp_offset, qkv_matrix, qkv_offset, dense_matrix, dense_offset, hidden_matrix, hidden_offset, output_matrix, output_offset = params
    length = sequence.shape[0]
    attn_normed = low(layer_norm(sequence, attn_gain, attn_offset))
    mlp_normed = low(layer_norm(sequence, mlp_gain, mlp_offset))
    projected = low_back(jnp.dot(attn_normed, qkv_matrix, precision=highest) + qkv_offset)
    cosine_table, sine_table = rotary_tables(jnp.arange(length, dtype=jnp.int32), ROT)
    head_data = rotate(projected.reshape(length, HEADS, 3, HEAD), cosine_table, sine_table, ROT)
    head_data = low_back(low(head_data))
    attended = low_back(low(attention(head_data))).reshape(length, D)
    hidden = low_back(jnp.dot(mlp_normed, hidden_matrix, precision=highest) + hidden_offset)
    active = low(jax.nn.gelu(hidden, approximate=False))
    attn_branch = jnp.dot(attended, dense_matrix, precision=highest) + dense_offset
    mlp_branch = jnp.dot(active, output_matrix, precision=highest) + output_offset
    return sequence + attn_branch + mlp_branch

def reference(inputs, cotangent, ln_attn_gain, ln_attn_bias, ln_mlp_gain, ln_mlp_bias, qkv_weight, qkv_bias, dense_weight, dense_bias, hidden_weight, hidden_bias, output_weight, output_bias):
    params = (ln_attn_gain.astype(jnp.float32), ln_attn_bias.astype(jnp.float32), ln_mlp_gain.astype(jnp.float32), ln_mlp_bias.astype(jnp.float32), qkv_weight.astype(jnp.float32), qkv_bias.astype(jnp.float32), dense_weight.astype(jnp.float32), dense_bias.astype(jnp.float32), hidden_weight.astype(jnp.float32), hidden_bias.astype(jnp.float32), output_weight.astype(jnp.float32), output_bias.astype(jnp.float32))

    def forward(residual, weights):
        sequences = residual.reshape(SEQS, LENGTH, D)
        results = lax.map(jax.checkpoint(lambda sequence: sequence_forward(sequence, weights)), sequences)
        return results.reshape(SEQS * LENGTH, D)
    result, pullback = jax.vjp(forward, inputs.astype(jnp.float32), params)
    input_grad, gradients = pullback(cotangent.astype(jnp.float32))
    return (result.astype(jnp.bfloat16), input_grad, gradients[0], gradients[1], gradients[2], gradients[3], gradients[4], gradients[5], gradients[6], gradients[7], gradients[8], gradients[9], gradients[10], gradients[11])
```

```python
import functools
import math

import jax
import jax.numpy as jnp
from jax import lax
from jax.experimental import pallas as pl
from jax.experimental.pallas import tpu as pltpu
from jax.sharding import PartitionSpec as P

D = 1024
FF = 4096
HEADS = 16
HEAD = 64
ROT = 16
CHIP_TOKENS = 512
FSDP = 8
CHIPS = 8

epsilon = 1e-05
F32 = jnp.float32
BF16 = jnp.bfloat16
NT = (((1,), (1,)), ((), ()))
TN = (((0,), (0,)), ((), ()))
MIB = 2**20
HBM = pl.BlockSpec(memory_space=pl.ANY)
VMEM = pl.BlockSpec(memory_space=pltpu.VMEM)


def place():
    f = lax.axis_index("fsdp")
    s = lax.axis_index("seq")
    return f, s, (f // 2, f % 2, s // 4, (s // 2) % 2, s % 2)


def device(y, z, x, core):
    return {"fsdp": y * 2 + z % 2, "seq": x * 4 + (z // 2) * 2 + core}


def barrier(devices):
    sem = pltpu.get_barrier_semaphore()
    for d in devices:
        pl.semaphore_signal(sem, inc=1, device_id=d, device_id_type=pl.DeviceIdType.MESH)
    pl.semaphore_wait(sem, len(devices))


def remote(src, dst, send, recv, target):
    return pltpu.make_async_remote_copy(
        src_ref=src,
        dst_ref=dst,
        send_sem=send,
        recv_sem=recv,
        device_id=target,
        device_id_type=pl.DeviceIdType.MESH,
    )


def gather_kernel(wq, wd, wh, wo, small, x, ct, gq, gd, gh, go, gs, gx, gc, send, recv, local_sem):
    f, s, (y, zl, px, zh, core) = place()
    z = zh * 2 + zl
    sibling = device(y, z, px, 1 - core)
    yp = device((y + 1) % 4, z, px, core)
    ym = device((y + 3) % 4, z, px, core)
    zp = device(y, (z + 1) % 4, px, core)
    zm = device(y, (z + 3) % 4, px, core)
    others = [{"fsdp": (f + k) % 8, "seq": s} for k in range(1, 8)]
    zother = device(y, 2 * (1 - zh) + 1 - zl, px, core)
    barrier(others + [sibling, zother])

    def started(src, dst, k, target):
        copy = remote(src, dst, send.at[k], recv.at[k], target)
        copy.start()
        return copy

    def arrived(ref, k):
        remote(ref, ref, send.at[k], recv.at[k], sibling).wait_recv()

    base = 4 * 14
    sends = [
        started(x, gx.at[core], base, sibling),
        started(ct, gc.at[core], base + 1, sibling),
    ]
    for k in range(1, 8):
        sends.append(started(small, gs.at[f], base + 1 + k, others[k - 1]))
    own = [
        wq,
        wd.at[pl.ds(pl.multiple_of(core * 64, 64), 64)],
        wh,
        wo.at[pl.ds(pl.multiple_of(core * 256, 256), 256)],
    ]
    full = [gq, gd, gh, go]
    locals_ = [
        (x, gx.at[core]),
        (ct, gc.at[core]),
        (small, gs.at[f]),
        *[(o, g.at[f]) for o, g in zip(own, full)],
    ]
    keeps = []
    for k, (a, b) in enumerate(locals_):
        copy = pltpu.make_async_copy(a, b, local_sem.at[k])
        copy.start()
        keeps.append(copy)

    def part(ref, h):
        rows = ref.shape[0] // 2
        return ref.at[pl.ds(h * rows, rows)]

    slots = [f, (f + 6) % 8, (f + 2) % 8, (f + 4) % 8]
    flip = f + 1 - 2 * zl
    far = [flip, (flip + 6) % 8, (flip + 2) % 8, (flip + 4) % 8]
    for n, (o, g) in enumerate(zip(own, full)):
        b = 14 * n
        sends.append(started(part(o, 0), part(g.at[f], 0), b, yp))
        sends.append(started(part(o, 1), part(g.at[f], 1), b + 3, ym))
        sends.append(started(part(o, 0), part(g.at[f], 0), b + 6, zp))
        sends.append(started(part(o, 1), part(g.at[f], 1), b + 10, zm))
        sends.append(started(part(o, 0), part(g.at[f], 0), b + 2, ym))
        sends.append(started(part(o, 1), part(g.at[f], 1), b + 1, yp))

    def pass_on(g, b, k, slot, h, targets):
        ref = part(g.at[slot], h)
        arrived(ref, b + k)
        for kk, target in targets:
            sends.append(started(ref, ref, b + kk, target))

    for n, g in enumerate(full):
        b = 14 * n
        pass_on(g, b, 0, slots[1], 0, [(4, yp), (7, zp)])
        pass_on(g, b, 3, slots[2], 1, [(5, ym), (12, zm)])
        pass_on(g, b, 2, slots[2], 0, [(8, zp)])
        pass_on(g, b, 1, slots[1], 1, [(11, zm)])
    for n, g in enumerate(full):
        b = 14 * n
        pass_on(g, b, 4, slots[3], 0, [(9, zp)])
        pass_on(g, b, 5, slots[3], 1, [(13, zm)])
    for n, g in enumerate(full):
        for j in range(4):
            arrived(part(g.at[far[j]], 0), 14 * n + 6 + j)
            arrived(part(g.at[far[j]], 1), 14 * n + 10 + j)
    arrived(gx.at[1 - core], base)
    arrived(gc.at[1 - core], base + 1)
    for k in range(1, 8):
        arrived(gs.at[(f + 8 - k) % 8], base + 1 + k)
    for copy in sends:
        copy.wait_send()
    for copy in keeps:
        copy.wait()


def gather(wq, wd, wh, wo, small, x, ct):
    def shape(*dims):
        return jax.ShapeDtypeStruct(dims, BF16)

    return pl.pallas_call(
        gather_kernel,
        out_shape=(
            shape(8, 128, 1536),
            shape(8, 64, 1024),
            shape(8, 128, 2048),
            shape(8, 256, 1024),
            shape(8, 16, 128),
            shape(2, 256, 1024),
            shape(2, 256, 1024),
        ),
        in_specs=[HBM] * 7,
        out_specs=(HBM,) * 7,
        scratch_shapes=[
            pltpu.SemaphoreType.DMA((65,)),
            pltpu.SemaphoreType.DMA((65,)),
            pltpu.SemaphoreType.DMA((7,)),
        ],
        compiler_params=pltpu.CompilerParams(collective_id=0, has_side_effects=True),
    )(wq, wd, wh, wo, small, x, ct)


def exchange_kernel(a, b, send, recv, local_sem):
    f, s, _ = place()
    me, core = s // 2, s % 2
    targets = [{"fsdp": f, "seq": ((me + k) % CHIPS) * 2 + core} for k in range(1, CHIPS)]
    barrier(targets)
    copies = []
    for k in range(1, CHIPS):
        copy = remote(a.at[(me + k) % CHIPS], b.at[me], send.at[k], recv.at[k], targets[k - 1])
        copy.start()
        copies.append(copy)
    keep = pltpu.make_async_copy(a.at[me], b.at[me], local_sem)
    keep.start()
    for k in range(1, CHIPS):
        ref = b.at[(me + CHIPS - k) % CHIPS]
        remote(ref, ref, send.at[k], recv.at[k], targets[k - 1]).wait_recv()
    for copy in copies:
        copy.wait_send()
    keep.wait()


def exchange(a, collective_id):
    return pl.pallas_call(
        exchange_kernel,
        out_shape=jax.ShapeDtypeStruct(a.shape, a.dtype),
        in_specs=[HBM],
        out_specs=HBM,
        scratch_shapes=[
            pltpu.SemaphoreType.DMA((CHIPS,)),
            pltpu.SemaphoreType.DMA((CHIPS,)),
            pltpu.SemaphoreType.DMA,
        ],
        compiler_params=pltpu.CompilerParams(collective_id=collective_id, has_side_effects=True),
    )(a)


def fold(op, a):
    result = a[:, :128]
    for j in range(128, a.shape[1], 128):
        result = op(result, a[:, j : j + 128])
    return result


def attention_kernel(
    B, hd, out, q_s, k_s, v_s, d_s, s_s, p_s, dk_s, dv_s, mx_s, l_s, o_s, dq_s
):
    n = hd.shape[0] // B
    scale = 1.0 / math.sqrt(HEAD)

    def block(i):
        return pl.ds(pl.multiple_of(i * B, B), B)

    def prepare(i, _):
        rows = block(i)
        piece = hd[rows, :]
        q_s[rows, :] = piece[:, 0:64] * jnp.asarray(scale, BF16)
        k_s[rows, :] = piece[:, 64:128]
        v_s[rows, :] = piece[:, 128:192]
        d_s[rows, :] = piece[:, 192:256]
        return 0

    lax.fori_loop(0, n, prepare, 0)
    dk_s[...] = jnp.zeros_like(dk_s)
    dv_s[...] = jnp.zeros_like(dv_s)
    keep = lax.broadcasted_iota(jnp.int32, (B, B), 1) <= lax.broadcasted_iota(
        jnp.int32, (B, B), 0
    )

    def query_block(t, _):
        i = n - 1 - t
        rows = block(i)
        qi = q_s[rows, :]
        mx_s[...] = jnp.full(mx_s.shape, -1e30, F32)

        def score(kb):
            return lax.dot_general(qi, k_s[block(kb), :], NT, preferred_element_type=F32)

        def first(kb, _):
            scores = score(kb)
            s_s[kb] = scores
            mx_s[...] = jnp.maximum(mx_s[...], fold(jnp.maximum, scores))
            return 0

        lax.fori_loop(0, i, first, 0)
        scores = jnp.where(keep, score(i), -1e30)
        s_s[i] = scores
        row_max = jnp.max(
            jnp.maximum(mx_s[...], fold(jnp.maximum, scores)), axis=1, keepdims=True
        )
        l_s[...] = jnp.zeros_like(l_s)
        o_s[...] = jnp.zeros_like(o_s)
        dq_s[...] = jnp.zeros_like(dq_s)

        def second(kb, _):
            p = jnp.exp(s_s[kb] - row_max)
            l_s[...] += fold(jnp.add, p)
            pb = p.astype(BF16)
            p_s[kb] = pb
            o_s[...] += jnp.dot(pb, v_s[block(kb), :], preferred_element_type=F32)
            return 0

        lax.fori_loop(0, i + 1, second, 0)
        inverse = 1.0 / jnp.sum(l_s[...], axis=1, keepdims=True)
        o = o_s[...] * inverse
        d = (d_s[rows, :].astype(F32) * inverse).astype(BF16)
        delta = jnp.sum(o * d.astype(F32), axis=1, keepdims=True)
        q_t = qi.T
        d_t = d.T

        def third(kb, _):
            cols = block(kb)
            pb = p_s[kb]
            dp = lax.dot_general(d, v_s[cols, :], NT, preferred_element_type=F32)
            ds = (pb.astype(F32) * (dp - delta)).astype(BF16)
            dq_s[...] += jnp.dot(ds, k_s[cols, :], preferred_element_type=F32)
            dk_s[:, cols] += jnp.dot(q_t, ds, preferred_element_type=F32)
            dv_s[:, cols] += jnp.dot(d_t, pb, preferred_element_type=F32)
            return 0

        lax.fori_loop(0, i + 1, third, 0)
        out[rows, 0:64] = (dq_s[...] * scale).astype(BF16)
        out[rows, 64:128] = dk_s[:, rows].T.astype(BF16)
        out[rows, 128:192] = dv_s[:, rows].T.astype(BF16)
        out[rows, 192:256] = o.astype(BF16)
        return 0

    lax.fori_loop(0, n, query_block, 0)


def attention(hd, B=512):
    L = hd.shape[0]
    return pl.pallas_call(
        functools.partial(attention_kernel, B),
        out_shape=jax.ShapeDtypeStruct((L, 4 * HEAD), BF16),
        in_specs=[VMEM],
        out_specs=VMEM,
        scratch_shapes=[
            *[pltpu.VMEM((L, HEAD), BF16)] * 4,
            pltpu.VMEM((L // B, B, B), F32),
            pltpu.VMEM((L // B, B, B), BF16),
            *[pltpu.VMEM((HEAD, L), F32)] * 2,
            *[pltpu.VMEM((B, 128), F32)] * 2,
            *[pltpu.VMEM((B, HEAD), F32)] * 2,
        ],
        compiler_params=pltpu.CompilerParams(vmem_limit_bytes=56 * MIB),
    )(hd)


ORDERS = ("yzx", "zxy", "xyz")
LEADS = ((2, 4), (2, 4), (4, 2))


def from_input(n, ref, t, h):
    if n == 0:
        return ref.at[t, h]
    if n == 1:
        return ref.at[pl.ds(2 * h, 2), t % 2, t // 2]
    return ref.at[:, h, :, t]


def from_own(n, stage, own, t, h, where):
    y, zl, zh, px = where
    if stage == 1:
        if n == 0:
            return own.at[t % 2, t // 2, pl.ds(2 * h, 2)]
        if n == 1:
            return own.at[h, :, t]
        return own.at[h, t]
    half = own.shape[-1] // 2
    columns = pl.ds(h * half, half)
    if n == 0:
        return own.at[zl, zh, t, :, columns]
    if n == 1:
        return own.at[t // 2, t % 2, px, :, columns]
    return own.at[t % 2, y, t // 2, :, columns]


def add_into(dst, terms):
    lead = tuple(dst.shape[:-2])

    def body(k, _):
        at = []
        for extent in reversed(lead):
            at.insert(0, k % extent)
            k = k // extent
        at = (*at, slice(None), slice(None))
        total = dst[at].astype(F32)
        for t in terms:
            total = total + t[at].astype(F32)
        dst[at] = total.astype(BF16)
        return 0

    lax.fori_loop(0, math.prod(lead), body, 0)


def reduce_kernel(*refs):
    ins, small, outs, small_out = refs[0:3], refs[3], refs[4:7], refs[7]
    scratch = refs[8:]
    bufs = [scratch[9 * n : 9 * n + 9] for n in range(3)]
    (sm_a, sm_b, send, recv, local_sem, sm_send, sm_recv) = scratch[27:]
    f, s, (y, zl, px, zh, core) = place()
    z = zh * 2 + zl
    coordinate = {"y": y, "z": z, "x": px}
    where = (y, zl, zh, px)

    def along(axis, step):
        t = dict(coordinate)
        t[axis] = (t[axis] + step) % 4
        return device(t["y"], t["z"], t["x"], core)

    plus = {a: along(a, 1) for a in "yzx"}
    minus = {a: along(a, 3) for a in "yzx"}
    same_seq = [{"fsdp": (f + k) % 8, "seq": s} for k in range(1, 8)]
    same_fsdp = [{"fsdp": f, "seq": (s + k) % 16} for k in range(1, 16)]
    zother = device(y, 2 * (1 - zh) + 1 - zl, px, core)
    sibling = device(y, z, px, 1 - core)
    barrier(same_seq + same_fsdp + [zother])
    sends = []

    def started(src, dst, k, target):
        copy = remote(src, dst, send.at[k], recv.at[k], target)
        copy.start()
        sends.append(copy)

    def arrived(ref, k):
        remote(ref, ref, send.at[k], recv.at[k], sibling).wait_recv()

    def small_sent(src, dst, k, target):
        copy = remote(src, dst, sm_send.at[k], sm_recv.at[k], target)
        copy.start()
        sends.append(copy)

    def small_arrived(ref, k):
        remote(ref, ref, sm_send.at[k], sm_recv.at[k], sibling).wait_recv()

    for k in range(1, 8):
        small_sent(small.at[(f + k) % 8], sm_a.at[k], k, same_seq[k - 1])

    keeps = []
    for n in range(3):
        axis = ORDERS[n][0]
        p = coordinate[axis]
        src = ins[n]
        opp, fin, mid, own = bufs[n][0:4]
        b = 26 * n
        started(from_input(n, src, (p + 2) % 4, 0), opp.at[0], b, plus[axis])
        started(from_input(n, src, (p + 2) % 4, 1), opp.at[1], b + 1, minus[axis])
        pairs = [
            (from_input(n, src, (p + 1) % 4, 0), mid.at[0]),
            (from_input(n, src, (p + 3) % 4, 1), mid.at[1]),
            (from_input(n, src, p, 0), own.at[0]),
            (from_input(n, src, p, 1), own.at[1]),
        ]
        for k, (a, dst) in enumerate(pairs):
            copy = pltpu.make_async_copy(a, dst, local_sem.at[4 * n + k])
            copy.start()
            keeps.append(copy)
        started(from_input(n, src, (p + 1) % 4, 1), fin.at[0, 1], b + 2, plus[axis])
        started(from_input(n, src, (p + 3) % 4, 0), fin.at[1, 0], b + 3, minus[axis])

    def buffers(n, stage):
        if stage == 0:
            return bufs[n][0], bufs[n][1]
        return bufs[n][2 + 2 * stage], bufs[n][3 + 2 * stage]

    def begin(n, stage):
        axis = ORDERS[n][stage]
        p = coordinate[axis]
        own = bufs[n][3]
        opp, fin = buffers(n, stage)
        b = 26 * n + 6 * stage

        def view(t, h):
            return from_own(n, stage, own, t % 4, h, where)

        started(view(p + 2, 0), opp.at[0], b, plus[axis])
        started(view(p + 2, 1), opp.at[1], b + 1, minus[axis])
        started(view(p + 1, 1), fin.at[0, 1], b + 2, plus[axis])
        started(view(p + 3, 0), fin.at[1, 0], b + 3, minus[axis])

    def relay(n, stage):
        axis = ORDERS[n][stage]
        p = coordinate[axis]
        opp, fin = buffers(n, stage)
        b = 26 * n + 6 * stage
        if stage == 0:
            mids = bufs[n][2].at[0], bufs[n][2].at[1]
        else:
            own = bufs[n][3]
            mids = (
                from_own(n, stage, own, (p + 1) % 4, 0, where),
                from_own(n, stage, own, (p + 3) % 4, 1, where),
            )
        arrived(opp.at[0], b)
        add_into(mids[0], [opp.at[0]])
        started(mids[0], fin.at[0, 0], b + 4, plus[axis])
        arrived(opp.at[1], b + 1)
        add_into(mids[1], [opp.at[1]])
        started(mids[1], fin.at[1, 1], b + 5, minus[axis])

    def finish(n, stage):
        p = coordinate[ORDERS[n][stage]]
        own = bufs[n][3]
        _, fin = buffers(n, stage)
        b = 26 * n + 6 * stage
        arrived(fin.at[0, 1], b + 2)
        arrived(fin.at[1, 0], b + 3)
        arrived(fin.at[0, 0], b + 4)
        arrived(fin.at[1, 1], b + 5)
        for h in range(2):
            mine = own.at[h] if stage == 0 else from_own(n, stage, own, p, h, where)
            add_into(mine, [fin.at[0, h], fin.at[1, h]])

    for n in range(3):
        keeps[4 * n].wait()
        keeps[4 * n + 1].wait()
        relay(n, 0)

    for k in range(1, 8):
        small_arrived(sm_a.at[k], k)
    total = small[f]
    for k in range(1, 8):
        total = total + sm_a[k]
    sm_b[0] = total
    for k in range(1, 16):
        small_sent(sm_b.at[0], sm_b.at[k], 7 + k, same_fsdp[k - 1])

    for n in range(3):
        keeps[4 * n + 2].wait()
        keeps[4 * n + 3].wait()
        finish(n, 0)
        begin(n, 1)
    for n in range(3):
        relay(n, 1)
    for n in range(3):
        finish(n, 1)
        begin(n, 2)
    for n in range(3):
        relay(n, 2)

    chip = px * 2 + zh
    mine = zh * 4 + px
    gathers = []
    for n in range(3):
        finish(n, 2)
        own, out = bufs[n][3], outs[n]
        done = [own.at[zl, zh, px], own.at[y // 2, y % 2, px], own.at[zl, y, zh]][n]
        keep = pltpu.make_async_copy(done, out.at[core, mine], local_sem.at[12 + n])
        keep.start()
        gathers.append(keep)
        for k in range(1, 8):
            j = (chip + k) % 8
            started(done, out.at[core, mine], 26 * n + 17 + k, {"fsdp": f, "seq": j * 2 + core})
    for n in range(3):
        out = outs[n]
        for k in range(1, 8):
            j = (chip + 8 - k) % 8
            arrived(out.at[core, (j % 2) * 4 + j // 2], 26 * n + 17 + k)
        gathers[n].wait()
        started(out.at[core], out.at[core], 26 * n + 25, sibling)
    for k in range(1, 16):
        small_arrived(sm_b.at[k], 7 + k)
    total = sm_b[0]
    for k in range(1, 16):
        total = total + sm_b[k]
    small_out[...] = total
    for n in range(3):
        arrived(outs[n].at[1 - core], 26 * n + 25)
    for copy in sends:
        copy.wait_send()


def reduce_all(parts, small, collective_id):
    scratch = []
    for part, lead in zip(parts, LEADS):
        R, C = part.shape[-2:]
        for dims in (
            (2, *lead, R, C),
            (2, 2, *lead, R, C),
            (2, *lead, R, C),
            (2, *lead, R, C),
            (2, 2, R, C),
            (2, 2, 2, R, C),
            (2, R, C // 2),
            (2, 2, R, C // 2),
        ):
            scratch.append(pltpu.VMEM(dims, BF16))
        scratch.append(pltpu.SemaphoreType.DMA)
    outs = [jax.ShapeDtypeStruct((2, 8, *p.shape[-2:]), BF16) for p in parts]
    return pl.pallas_call(
        reduce_kernel,
        out_shape=(*outs, jax.ShapeDtypeStruct((16, 128), F32)),
        in_specs=[HBM, HBM, HBM, VMEM],
        out_specs=(HBM, HBM, HBM, VMEM),
        scratch_shapes=[
            *scratch,
            pltpu.VMEM((8, 16, 128), F32),
            pltpu.VMEM((16, 16, 128), F32),
            pltpu.SemaphoreType.DMA((78,)),
            pltpu.SemaphoreType.DMA((78,)),
            pltpu.SemaphoreType.DMA((15,)),
            pltpu.SemaphoreType.DMA((23,)),
            pltpu.SemaphoreType.DMA((23,)),
        ],
        compiler_params=pltpu.CompilerParams(
            collective_id=collective_id, has_side_effects=True, vmem_limit_bytes=48 * MIB
        ),
    )(*parts, small)


def turn(values, tables, sign):
    cosine, ahead, behind = tables
    moved = pltpu.roll(values, 120, 1) * ahead + pltpu.roll(values, 8, 1) * behind
    return values * cosine + sign * moved


def front_kernel(x, ct, wq, wd, vectors, bias, tables, packed, attn_out, mlp_out):
    values = x[...].astype(F32)
    centered = values - jnp.mean(values, axis=-1, keepdims=True)
    variance = jnp.mean(centered * centered, axis=-1, keepdims=True)
    normed = centered * lax.rsqrt(variance + epsilon)
    attn_out[...] = (normed * vectors[0:1, :] + vectors[1:2, :]).astype(BF16)
    mlp_out[...] = (normed * vectors[2:3, :] + vectors[3:4, :]).astype(BF16)
    low = lax.broadcasted_iota(jnp.int32, (CHIP_TOKENS, 128), 1) < HEAD
    rotary = (tables[0], tables[1], tables[2])
    for pair in range(4):
        a = attn_out[...]
        qk = slice(pair * 256, pair * 256 + 256)
        vs = slice(1024 + pair * 128, 1024 + pair * 128 + 128)
        projected = jnp.dot(a, wq[:, qk], preferred_element_type=F32) + bias[0:1, qk]
        for j in range(2):
            turned = turn(projected[:, j * 128 : j * 128 + 128], rotary, 1.0)
            packed[2 * pair + j, :, 0:128] = turned.astype(BF16)
        v = jnp.dot(a, wq[:, vs], preferred_element_type=F32) + bias[0:1, vs]
        rows = slice(pair * 128, pair * 128 + 128)
        d = lax.dot_general(ct[...], wd[rows, :], NT, preferred_element_type=F32)
        packed[2 * pair, :, 128:256] = jnp.where(low, v, pltpu.roll(d, 64, 1)).astype(BF16)
        packed[2 * pair + 1, :, 128:256] = jnp.where(low, pltpu.roll(v, 64, 1), d).astype(BF16)


def front(x, ct, wq, wd, vectors, bias, tables):
    T = CHIP_TOKENS
    return pl.pallas_call(
        front_kernel,
        out_shape=(
            jax.ShapeDtypeStruct((8, T, 256), BF16),
            jax.ShapeDtypeStruct((T, D), BF16),
            jax.ShapeDtypeStruct((T, D), BF16),
        ),
        in_specs=[VMEM] * 7,
        out_specs=(VMEM,) * 3,
        compiler_params=pltpu.CompilerParams(vmem_limit_bytes=48 * MIB),
    )(x, ct, wq, wd, vectors, bias, tables)


def back_kernel(packed, tables, grad, attended, bias):
    low = lax.broadcasted_iota(jnp.int32, (CHIP_TOKENS, 128), 1) < HEAD
    rotary = (tables[0], tables[1], tables[2])
    for pair in range(4):
        for j in range(2):
            at = slice((2 * pair + j) * 128, (2 * pair + j) * 128 + 128)
            turned = turn(packed[2 * pair + j, :, 0:128].astype(F32), rotary, -1.0).astype(BF16)
            grad[:, at] = turned
            bias[0:1, at] = jnp.sum(turned.astype(F32), axis=0, keepdims=True)
        a = packed[2 * pair, :, 128:256].astype(F32)
        b = packed[2 * pair + 1, :, 128:256].astype(F32)
        at = slice(1024 + pair * 128, 1024 + pair * 128 + 128)
        v = jnp.where(low, a, pltpu.roll(b, 64, 1))
        grad[:, at] = v.astype(BF16)
        bias[0:1, at] = jnp.sum(v, axis=0, keepdims=True)
        o = jnp.where(low, pltpu.roll(a, 64, 1), b)
        attended[:, pair * 128 : pair * 128 + 128] = o.astype(BF16)


def back(packed, tables):
    T = CHIP_TOKENS
    return pl.pallas_call(
        back_kernel,
        out_shape=(
            jax.ShapeDtypeStruct((T, 1536), BF16),
            jax.ShapeDtypeStruct((T, 512), BF16),
            jax.ShapeDtypeStruct((1, 1536), F32),
        ),
        in_specs=[VMEM] * 2,
        out_specs=(VMEM,) * 3,
        compiler_params=pltpu.CompilerParams(vmem_limit_bytes=48 * MIB),
    )(packed, tables)


def rotary_tables(first_position):
    half = ROT // 2
    frequency = 10000.0 ** (-2.0 * jnp.arange(half, dtype=F32) / ROT)
    positions = first_position + jnp.arange(CHIP_TOKENS, dtype=jnp.int32)
    angles = positions.astype(F32)[:, None] * frequency[None, :]
    cosine, sine = jnp.cos(angles), jnp.sin(angles)
    rest = HEAD - ROT
    one = jnp.ones((CHIP_TOKENS, rest), F32)
    zero = jnp.zeros((CHIP_TOKENS, rest), F32)
    none = jnp.zeros((CHIP_TOKENS, half), F32)
    rows = [
        jnp.concatenate([cosine, cosine, one] * 2, axis=1),
        jnp.concatenate([-sine, none, zero] * 2, axis=1),
        jnp.concatenate([none, sine, zero] * 2, axis=1),
    ]
    return jnp.stack(rows)


def gelu_and_slope(h):
    below = 0.5 * lax.erfc(-h * math.sqrt(0.5))
    density = jnp.exp(-0.5 * h * h) * (1.0 / math.sqrt(2.0 * math.pi))
    return h * below, below + h * density


def local(
    inputs,
    cotangent,
    ln_attn_gain,
    ln_attn_bias,
    ln_mlp_gain,
    ln_mlp_bias,
    qkv_weight,
    qkv_bias,
    dense_weight,
    dense_bias,
    hidden_weight,
    hidden_bias,
    output_weight,
    output_bias,
):
    seq = lax.axis_index("seq")
    core = seq % 2
    small = jnp.concatenate(
        [
            ln_attn_gain.reshape(1, 128),
            ln_attn_bias.reshape(1, 128),
            ln_mlp_gain.reshape(1, 128),
            ln_mlp_bias.reshape(1, 128),
            qkv_bias.reshape(3, 128),
            dense_bias.reshape(1, 128),
            hidden_bias.reshape(4, 128),
            output_bias.reshape(1, 128),
            jnp.zeros((3, 128), BF16),
        ]
    )
    own_qkv = lax.dynamic_index_in_dim(
        qkv_weight.reshape(128, 8, 2, 192), core, axis=2, keepdims=False
    )
    own_qkv = jnp.concatenate(
        [own_qkv[:, :, :128].reshape(128, 1024), own_qkv[:, :, 128:].reshape(128, 512)], axis=1
    )
    own_hidden = lax.dynamic_index_in_dim(
        hidden_weight.reshape(128, 8, 2, 256), core, axis=2, keepdims=False
    ).reshape(128, 2048)
    wq, wd, wh, wo, vectors, x, ct = gather(
        own_qkv, dense_weight, own_hidden, output_weight, small, inputs, cotangent
    )
    wq = wq.reshape(D, 1536)
    wd = wd.reshape(512, D)
    wh = wh.reshape(D, 2048)
    wo = wo.reshape(2048, D)
    x = x.reshape(CHIP_TOKENS, D)
    ct = ct.reshape(CHIP_TOKENS, D)
    vectors = vectors.astype(F32)
    norms = vectors[:, 0:4].transpose(1, 0, 2).reshape(4, D)
    head_bias = lax.dynamic_index_in_dim(
        vectors[:, 4:7].reshape(8, 2, 192), core, axis=1, keepdims=False
    )
    head_bias = jnp.concatenate(
        [head_bias[:, :128].reshape(1, 1024), head_bias[:, 128:].reshape(1, 512)], axis=1
    )
    out_bias = (vectors[:, 7] + vectors[:, 12]).reshape(1, D)
    unit_bias = lax.dynamic_index_in_dim(
        vectors[:, 8:12].reshape(8, 2, 256), core, axis=1, keepdims=False
    ).reshape(1, 2048)

    tables = rotary_tables((seq // 2) * CHIP_TOKENS)
    packed, attn_normed, mlp_normed = front(x, ct, wq, wd, norms, head_bias, tables)
    head_data = exchange(packed, 1).reshape(CHIPS * CHIP_TOKENS, 4 * HEAD)
    result = attention(head_data)
    tokens = exchange(result.reshape(CHIPS, CHIP_TOKENS, 4 * HEAD), 2)
    projected_grad, attended, head_bias_grad = back(tokens, tables)

    hidden = jnp.dot(mlp_normed, wh, preferred_element_type=F32) + unit_bias
    active, slope = gelu_and_slope(hidden)
    active = active.astype(BF16)
    active_grad = lax.dot_general(ct, wo, NT, preferred_element_type=F32)
    hidden_grad = (active_grad * slope).astype(BF16)
    output_weight_grad = lax.dot_general(active, ct, TN, preferred_element_type=F32)
    hidden_weight_grad = lax.dot_general(mlp_normed, hidden_grad, TN, preferred_element_type=F32)
    mlp_norm_grad = lax.dot_general(hidden_grad, wh, NT, preferred_element_type=F32)
    hidden_bias_grad = jnp.sum(hidden_grad.astype(F32), axis=0)

    branches = jnp.dot(attended, wd, preferred_element_type=F32) + jnp.dot(
        active, wo, preferred_element_type=F32
    )
    attn_norm_grad = lax.dot_general(projected_grad, wq, NT, preferred_element_type=F32)
    weighted = attn_norm_grad * norms[0:1] + mlp_norm_grad * norms[2:3]
    qkv_weight_grad = lax.dot_general(attn_normed, projected_grad, TN, preferred_element_type=F32)
    dense_weight_grad = lax.dot_general(attended, ct, TN, preferred_element_type=F32)

    values = x.astype(F32)
    centered = values - jnp.mean(values, axis=-1, keepdims=True)
    variance = jnp.mean(centered * centered, axis=-1, keepdims=True)
    scale = lax.rsqrt(variance + epsilon)
    normed = centered * scale
    attn_gain_grad = jnp.sum(attn_norm_grad * normed, axis=0)
    attn_bias_grad = jnp.sum(attn_norm_grad, axis=0)
    mlp_gain_grad = jnp.sum(mlp_norm_grad * normed, axis=0)
    mlp_bias_grad = jnp.sum(mlp_norm_grad, axis=0)

    def rows(a, c):
        return lax.dynamic_slice_in_dim(a, c * 256, 256, 0)

    swap = [(i, i + 1 - 2 * (i % 2)) for i in range(16)]
    given = jnp.concatenate(
        [rows(branches, 1 - core).astype(BF16), rows(weighted, 1 - core).astype(BF16)]
    )
    taken = lax.ppermute(given, "seq", swap).astype(F32)
    outputs = inputs.astype(F32) + rows(branches, core) + taken[:256] + out_bias
    w = rows(weighted, core) + taken[256:]
    n = rows(normed, core)
    input_grad = cotangent.astype(F32) + rows(scale, core) * (
        w - jnp.mean(w, axis=-1, keepdims=True) - n * jnp.mean(w * n, axis=-1, keepdims=True)
    )

    mine = (jnp.arange(2) == core).astype(F32)
    cotangent_sum = jnp.sum(cotangent.astype(F32), axis=0)
    per_head = jnp.concatenate(
        [head_bias_grad[0, :1024].reshape(8, 128), head_bias_grad[0, 1024:].reshape(8, 64)], axis=1
    )
    small_grads = jnp.concatenate(
        [
            attn_gain_grad.reshape(8, 1, 128),
            attn_bias_grad.reshape(8, 1, 128),
            mlp_gain_grad.reshape(8, 1, 128),
            mlp_bias_grad.reshape(8, 1, 128),
            (per_head[:, None, :] * mine[None, :, None]).reshape(8, 3, 128),
            cotangent_sum.reshape(8, 1, 128),
            (hidden_bias_grad.reshape(8, 1, 256) * mine[None, :, None]).reshape(8, 4, 128),
            jnp.zeros((8, 4, 128), F32),
        ],
        axis=1,
    )
    dense_part = dense_weight_grad.astype(BF16).reshape(8, 64, 2, 512).transpose(0, 2, 1, 3)
    heads_part = jnp.concatenate(
        [qkv_weight_grad.astype(BF16).reshape(8, 128, 1536), dense_part.reshape(8, 128, 512)],
        axis=2,
    )
    hidden_sum, output_sum, heads_sum, small_sum = reduce_all(
        (
            hidden_weight_grad.astype(BF16).reshape(4, 2, 2, 4, 16, 2048),
            output_weight_grad.astype(BF16).reshape(4, 2, 2, 4, 32, 1024),
            heads_part.reshape(4, 2, 2, 4, 16, 2048),
        ),
        small_grads,
        3,
    )
    hidden_total = (
        hidden_sum.reshape(2, 128, 8, 256).transpose(1, 2, 0, 3).reshape(128, FF).astype(F32)
    )
    output_total = output_sum.reshape(512, D).astype(F32)
    heads_sum = heads_sum.reshape(2, 128, 2048)
    qkv_total = jnp.concatenate(
        [
            heads_sum[:, :, :1024].reshape(2, 128, 8, 128),
            heads_sum[:, :, 1024:1536].reshape(2, 128, 8, 64),
        ],
        axis=3,
    )
    qkv_total = qkv_total.transpose(1, 2, 0, 3).reshape(128, 3 * D).astype(F32)
    dense_total = heads_sum[:, :, 1536:].reshape(2, 2, 64, 512).transpose(0, 2, 1, 3)
    dense_total = dense_total.reshape(128, D).astype(F32)
    return (
        outputs.astype(BF16),
        input_grad,
        small_sum[0],
        small_sum[1],
        small_sum[2],
        small_sum[3],
        qkv_total,
        small_sum[4:7].reshape(384),
        dense_total,
        small_sum[7],
        hidden_total,
        small_sum[8:12].reshape(512),
        output_total,
        small_sum[7],
    )


def solution(mesh):
    rows = P(("fsdp", "seq"), None)
    vector = P("fsdp")
    matrix = P("fsdp", None)
    shared = (vector,) * 4 + (matrix, vector) * 4
    return jax.shard_map(
        local,
        mesh=mesh,
        in_specs=(rows, rows, *shared),
        out_specs=(rows, rows, *shared),
        check_vma=False,
    )
```

```python
import functools
import math

import jax
import jax.numpy as jnp
from jax import lax
from jax.experimental import pallas as pl
from jax.experimental.pallas import tpu as pltpu
from jax.sharding import PartitionSpec as P

D = 1024
FF = 4096
HEADS = 16
HEAD = 64
ROT = 16
CHIP_TOKENS = 512
FSDP = 8
CHIPS = 8

epsilon = 1e-05
F32 = jnp.float32
BF16 = jnp.bfloat16
NT = (((1,), (1,)), ((), ()))
TN = (((0,), (0,)), ((), ()))
MIB = 2**20
HBM = pl.BlockSpec(memory_space=pl.ANY)
VMEM = pl.BlockSpec(memory_space=pltpu.VMEM)


def place():
    f = lax.axis_index("fsdp")
    s = lax.axis_index("seq")
    return f, s, (f // 2, f % 2, s // 4, (s // 2) % 2, s % 2)


def device(y, z, x, core):
    return {"fsdp": y * 2 + z % 2, "seq": x * 4 + (z // 2) * 2 + core}


def barrier(devices):
    sem = pltpu.get_barrier_semaphore()
    for d in devices:
        pl.semaphore_signal(sem, inc=1, device_id=d, device_id_type=pl.DeviceIdType.MESH)
    pl.semaphore_wait(sem, len(devices))


def remote(src, dst, send, recv, target):
    return pltpu.make_async_remote_copy(
        src_ref=src,
        dst_ref=dst,
        send_sem=send,
        recv_sem=recv,
        device_id=target,
        device_id_type=pl.DeviceIdType.MESH,
    )


class Gather:
    def __init__(self, own, full, send, recv):
        f, s, (y, zl, px, zh, core) = place()
        z = zh * 2 + zl
        self.own, self.full, self.send, self.recv = own, full, send, recv
        self.yp = device((y + 1) % 4, z, px, core)
        self.ym = device((y + 3) % 4, z, px, core)
        self.zp = device(y, (z + 1) % 4, px, core)
        self.zm = device(y, (z + 3) % 4, px, core)
        self.f = f
        self.slots = [f, (f + 6) % 8, (f + 2) % 8, (f + 4) % 8]
        flip = f + 1 - 2 * zl
        self.far = [flip, (flip + 6) % 8, (flip + 2) % 8, (flip + 4) % 8]
        self.sends = []

    def neighbours(self):
        return [self.yp, self.ym, self.zp, self.zm]

    def started(self, src, dst, k, target):
        copy = remote(src, dst, self.send.at[k], self.recv.at[k], target)
        copy.start()
        self.sends.append(copy)

    def arrived(self, ref, k):
        remote(ref, ref, self.send.at[k], self.recv.at[k], self.yp).wait_recv()

    @staticmethod
    def part(ref, h):
        rows = ref.shape[0] // 2
        return ref.at[pl.ds(h * rows, rows)]

    def own_y(self):
        for n, (o, g) in enumerate(zip(self.own, self.full)):
            for k, h, target in ((0, 0, self.yp), (3, 1, self.ym), (2, 0, self.ym), (1, 1, self.yp)):
                self.started(self.part(o, h), self.part(g.at[self.f], h), 14 * n + k, target)

    def own_z(self):
        for n, (o, g) in enumerate(zip(self.own, self.full)):
            for k, h, target in ((6, 0, self.zp), (10, 1, self.zm)):
                self.started(self.part(o, h), self.part(g.at[self.f], h), 14 * n + k, target)

    def pass_on(self, n, k, slot, h, targets):
        ref = self.part(self.full[n].at[slot], h)
        self.arrived(ref, 14 * n + k)
        for kk, target in targets:
            self.started(ref, ref, 14 * n + kk, target)

    def near(self):
        for n in range(len(self.full)):
            self.pass_on(n, 0, self.slots[1], 0, [(4, self.yp), (7, self.zp)])
            self.pass_on(n, 3, self.slots[2], 1, [(5, self.ym), (12, self.zm)])
            self.pass_on(n, 2, self.slots[2], 0, [(8, self.zp)])
            self.pass_on(n, 1, self.slots[1], 1, [(11, self.zm)])

    def opposite(self):
        for n in range(len(self.full)):
            self.pass_on(n, 4, self.slots[3], 0, [(9, self.zp)])
            self.pass_on(n, 5, self.slots[3], 1, [(13, self.zm)])

    def finish(self):
        for n, g in enumerate(self.full):
            for j in range(4):
                self.arrived(self.part(g.at[self.far[j]], 0), 14 * n + 6 + j)
                self.arrived(self.part(g.at[self.far[j]], 1), 14 * n + 10 + j)
        for copy in self.sends:
            copy.wait_send()


def gather_kernel(wq, wd, small, x, ct, gq, gd, gs, gx, gc, send, recv, local_sem):
    f, s, (y, zl, px, zh, core) = place()
    sibling = device(y, zh * 2 + zl, px, 1 - core)
    others = [{"fsdp": (f + k) % 8, "seq": s} for k in range(1, 8)]
    zother = device(y, 2 * (1 - zh) + 1 - zl, px, core)
    own = [wq, wd.at[pl.ds(pl.multiple_of(core * 64, 64), 64)]]
    weights = Gather(own, [gq, gd], send, recv)
    barrier(others + [sibling, zother])
    base = 28
    weights.own_y()
    weights.started(x, gx.at[core], base, sibling)
    weights.started(ct, gc.at[core], base + 1, sibling)
    for k in range(1, 8):
        weights.started(small, gs.at[f], base + 1 + k, others[k - 1])
    weights.own_z()
    pairs = [(gx.at[core], x), (gc.at[core], ct), (gs.at[f], small), (gq.at[f], own[0]), (gd.at[f], own[1])]
    keeps = []
    for k, (b, a) in enumerate(pairs):
        copy = pltpu.make_async_copy(a, b, local_sem.at[k])
        copy.start()
        keeps.append(copy)
    weights.near()
    weights.opposite()
    weights.arrived(gx.at[1 - core], base)
    weights.arrived(gc.at[1 - core], base + 1)
    for k in range(1, 8):
        weights.arrived(gs.at[(f + 8 - k) % 8], base + 1 + k)
    weights.finish()
    for copy in keeps:
        copy.wait()


def gather(wq, wd, small, x, ct):
    def shape(*dims):
        return jax.ShapeDtypeStruct(dims, BF16)

    return pl.pallas_call(
        gather_kernel,
        out_shape=(
            shape(8, 128, 1536),
            shape(8, 64, 1024),
            shape(8, 16, 128),
            shape(2, 256, 1024),
            shape(2, 256, 1024),
        ),
        in_specs=[HBM] * 5,
        out_specs=(HBM,) * 5,
        scratch_shapes=[
            pltpu.SemaphoreType.DMA((37,)),
            pltpu.SemaphoreType.DMA((37,)),
            pltpu.SemaphoreType.DMA((5,)),
        ],
        compiler_params=pltpu.CompilerParams(collective_id=0, has_side_effects=True),
    )(wq, wd, small, x, ct)


def fold(op, a):
    result = a[:, :128]
    for j in range(128, a.shape[1], 128):
        result = op(result, a[:, j : j + 128])
    return result


def attention_kernel(
    packed, wh, wo, result, gh, go,
    hd, out, q_s, k_s, v_s, d_s, s_s, p_s, dk_s, dv_s, mx_s, l_s, o_s, dq_s,
    in_send, in_recv, out_send, out_recv, g_send, g_recv, local_sem,
):
    f, s, (y, zl, px, zh, core) = place()
    me = s // 2
    B = CHIP_TOKENS
    n = CHIPS
    scale = 1.0 / math.sqrt(HEAD)
    own = [wh, wo.at[pl.ds(pl.multiple_of(core * 256, 256), 256)]]
    weights = Gather(own, [gh, go], g_send, g_recv)

    def chip(j):
        return {"fsdp": f, "seq": j * 2 + core}

    barrier([chip((me + k) % n) for k in range(1, n)] + weights.neighbours())
    given = []
    for k in range(1, n):
        j = (me + k) % n
        copy = remote(packed.at[j], hd.at[me], in_send.at[k], in_recv.at[k], chip(j))
        copy.start()
        given.append(copy)
    weights.own_y()
    keeps = []
    for k, (a, b) in enumerate([(packed.at[me], hd.at[me]), (own[0], gh.at[f]), (own[1], go.at[f])]):
        copy = pltpu.make_async_copy(a, b, local_sem.at[k])
        copy.start()
        keeps.append(copy)
    keeps[0].wait()
    for k in range(1, n):
        ref = hd.at[(me + n - k) % n]
        remote(ref, ref, in_send.at[k], in_recv.at[k], chip(me)).wait_recv()
    weights.own_z()

    def block(i):
        return pl.ds(pl.multiple_of(i * B, B), B)

    def prepare(i, _):
        rows = block(i)
        piece = hd[i]
        q_s[rows, :] = piece[:, 0:64] * jnp.asarray(scale, BF16)
        k_s[rows, :] = piece[:, 64:128]
        v_s[rows, :] = piece[:, 128:192]
        d_s[rows, :] = piece[:, 192:256]
        return 0

    lax.fori_loop(0, n, prepare, 0)
    dk_s[...] = jnp.zeros_like(dk_s)
    dv_s[...] = jnp.zeros_like(dv_s)
    keep = lax.broadcasted_iota(jnp.int32, (B, B), 1) <= lax.broadcasted_iota(
        jnp.int32, (B, B), 0
    )

    def back_to(i):
        return remote(out.at[i], result.at[me], out_send.at[i], out_recv.at[me], chip(i))

    def query_block(t, _):
        i = n - 1 - t
        rows = block(i)
        qi = q_s[rows, :]
        mx_s[...] = jnp.full(mx_s.shape, -1e30, F32)

        def score(kb):
            return lax.dot_general(qi, k_s[block(kb), :], NT, preferred_element_type=F32)

        def first(kb, _):
            scores = score(kb)
            s_s[kb] = scores
            mx_s[...] = jnp.maximum(mx_s[...], fold(jnp.maximum, scores))
            return 0

        lax.fori_loop(0, i, first, 0)
        scores = jnp.where(keep, score(i), -1e30)
        s_s[i] = scores
        row_max = jnp.max(
            jnp.maximum(mx_s[...], fold(jnp.maximum, scores)), axis=1, keepdims=True
        )
        l_s[...] = jnp.zeros_like(l_s)
        o_s[...] = jnp.zeros_like(o_s)
        dq_s[...] = jnp.zeros_like(dq_s)

        def second(kb, _):
            p = jnp.exp(s_s[kb] - row_max)
            l_s[...] += fold(jnp.add, p)
            pb = p.astype(BF16)
            p_s[kb] = pb
            o_s[...] += jnp.dot(pb, v_s[block(kb), :], preferred_element_type=F32)
            return 0

        lax.fori_loop(0, i + 1, second, 0)
        inverse = 1.0 / jnp.sum(l_s[...], axis=1, keepdims=True)
        o = o_s[...] * inverse
        d = (d_s[rows, :].astype(F32) * inverse).astype(BF16)
        delta = jnp.sum(o * d.astype(F32), axis=1, keepdims=True)
        q_t = qi.T
        d_t = d.T

        def third(kb, _):
            cols = block(kb)
            pb = p_s[kb]
            dp = lax.dot_general(d, v_s[cols, :], NT, preferred_element_type=F32)
            ds = (pb.astype(F32) * (dp - delta)).astype(BF16)
            dq_s[...] += jnp.dot(ds, k_s[cols, :], preferred_element_type=F32)
            dk_s[:, cols] += jnp.dot(q_t, ds, preferred_element_type=F32)
            dv_s[:, cols] += jnp.dot(d_t, pb, preferred_element_type=F32)
            return 0

        lax.fori_loop(0, i + 1, third, 0)
        out[i, :, 0:64] = (dq_s[...] * scale).astype(BF16)
        out[i, :, 64:128] = dk_s[:, rows].T.astype(BF16)
        out[i, :, 128:192] = dv_s[:, rows].T.astype(BF16)
        out[i, :, 192:256] = o.astype(BF16)

        @pl.when(i != me)
        def _():
            back_to(i).start()

        @pl.when(i == me)
        def _():
            pltpu.make_async_copy(out.at[i], result.at[i], local_sem.at[3]).start()

        return 0

    lax.fori_loop(0, 1, query_block, 0)
    weights.near()
    lax.fori_loop(1, 2, query_block, 0)
    weights.opposite()
    lax.fori_loop(2, n, query_block, 0)

    for copy in given:
        copy.wait_send()
    keeps[1].wait()
    keeps[2].wait()
    weights.finish()
    for k in range(1, n):
        back_to((me + k) % n).wait_send()
    pltpu.make_async_copy(out.at[me], result.at[me], local_sem.at[3]).wait()
    for k in range(1, n):
        j = (me + k) % n
        ref = result.at[j]
        remote(ref, ref, out_send.at[j], out_recv.at[j], chip(me)).wait_recv()


def attention(packed, wh, wo):
    B = CHIP_TOKENS
    L = CHIPS * B
    return pl.pallas_call(
        attention_kernel,
        out_shape=(
            jax.ShapeDtypeStruct((CHIPS, B, 4 * HEAD), BF16),
            jax.ShapeDtypeStruct((8, 128, 2048), BF16),
            jax.ShapeDtypeStruct((8, 256, 1024), BF16),
        ),
        in_specs=[HBM] * 3,
        out_specs=(HBM,) * 3,
        scratch_shapes=[
            *[pltpu.VMEM((CHIPS, B, 4 * HEAD), BF16)] * 2,
            *[pltpu.VMEM((L, HEAD), BF16)] * 4,
            pltpu.VMEM((L // B, B, B), F32),
            pltpu.VMEM((L // B, B, B), BF16),
            *[pltpu.VMEM((HEAD, L), F32)] * 2,
            *[pltpu.VMEM((B, 128), F32)] * 2,
            *[pltpu.VMEM((B, HEAD), F32)] * 2,
            *[pltpu.SemaphoreType.DMA((CHIPS,))] * 4,
            *[pltpu.SemaphoreType.DMA((28,))] * 2,
            pltpu.SemaphoreType.DMA((4,)),
        ],
        compiler_params=pltpu.CompilerParams(
            collective_id=1, has_side_effects=True, vmem_limit_bytes=56 * MIB
        ),
    )(packed, wh, wo)


ORDERS = ("yzx", "zxy", "xyz")
LEADS = ((2, 4), (2, 4), (4, 2))


def from_input(n, ref, t, h):
    if n == 0:
        return ref.at[t, h]
    if n == 1:
        return ref.at[pl.ds(2 * h, 2), t % 2, t // 2]
    return ref.at[:, h, :, t]


def from_own(n, stage, own, t, h, where):
    y, zl, zh, px = where
    if stage == 1:
        if n == 0:
            return own.at[t % 2, t // 2, pl.ds(2 * h, 2)]
        if n == 1:
            return own.at[h, :, t]
        return own.at[h, t]
    half = own.shape[-1] // 2
    columns = pl.ds(h * half, half)
    if n == 0:
        return own.at[zl, zh, t, :, columns]
    if n == 1:
        return own.at[t // 2, t % 2, px, :, columns]
    return own.at[t % 2, y, t // 2, :, columns]


def add_into(dst, terms):
    lead = tuple(dst.shape[:-2])

    def body(k, _):
        at = []
        for extent in reversed(lead):
            at.insert(0, k % extent)
            k = k // extent
        at = (*at, slice(None), slice(None))
        total = dst[at].astype(F32)
        for t in terms:
            total = total + t[at].astype(F32)
        dst[at] = total.astype(BF16)
        return 0

    lax.fori_loop(0, math.prod(lead), body, 0)


def reduce_kernel(*refs):
    ins, small, outs, small_out = refs[0:3], refs[3], refs[4:7], refs[7]
    scratch = refs[8:]
    bufs = [scratch[9 * n : 9 * n + 9] for n in range(3)]
    (sm_a, sm_b, send, recv, local_sem, sm_send, sm_recv) = scratch[27:]
    f, s, (y, zl, px, zh, core) = place()
    z = zh * 2 + zl
    coordinate = {"y": y, "z": z, "x": px}
    where = (y, zl, zh, px)

    def along(axis, step):
        t = dict(coordinate)
        t[axis] = (t[axis] + step) % 4
        return device(t["y"], t["z"], t["x"], core)

    plus = {a: along(a, 1) for a in "yzx"}
    minus = {a: along(a, 3) for a in "yzx"}
    same_seq = [{"fsdp": (f + k) % 8, "seq": s} for k in range(1, 8)]
    same_fsdp = [{"fsdp": f, "seq": (s + k) % 16} for k in range(1, 16)]
    zother = device(y, 2 * (1 - zh) + 1 - zl, px, core)
    sibling = device(y, z, px, 1 - core)
    barrier(same_seq + same_fsdp + [zother])
    sends = []

    def started(src, dst, k, target):
        copy = remote(src, dst, send.at[k], recv.at[k], target)
        copy.start()
        sends.append(copy)

    def arrived(ref, k):
        remote(ref, ref, send.at[k], recv.at[k], sibling).wait_recv()

    def small_sent(src, dst, k, target):
        copy = remote(src, dst, sm_send.at[k], sm_recv.at[k], target)
        copy.start()
        sends.append(copy)

    def small_arrived(ref, k):
        remote(ref, ref, sm_send.at[k], sm_recv.at[k], sibling).wait_recv()

    for k in range(1, 8):
        small_sent(small.at[(f + k) % 8], sm_a.at[k], k, same_seq[k - 1])

    keeps = []
    for n in range(3):
        axis = ORDERS[n][0]
        p = coordinate[axis]
        src = ins[n]
        opp, fin, mid, own = bufs[n][0:4]
        b = 26 * n
        started(from_input(n, src, (p + 2) % 4, 0), opp.at[0], b, plus[axis])
        started(from_input(n, src, (p + 2) % 4, 1), opp.at[1], b + 1, minus[axis])
        pairs = [
            (from_input(n, src, (p + 1) % 4, 0), mid.at[0]),
            (from_input(n, src, (p + 3) % 4, 1), mid.at[1]),
            (from_input(n, src, p, 0), own.at[0]),
            (from_input(n, src, p, 1), own.at[1]),
        ]
        for k, (a, dst) in enumerate(pairs):
            copy = pltpu.make_async_copy(a, dst, local_sem.at[4 * n + k])
            copy.start()
            keeps.append(copy)
        started(from_input(n, src, (p + 1) % 4, 1), fin.at[0, 1], b + 2, plus[axis])
        started(from_input(n, src, (p + 3) % 4, 0), fin.at[1, 0], b + 3, minus[axis])

    def buffers(n, stage):
        if stage == 0:
            return bufs[n][0], bufs[n][1]
        return bufs[n][2 + 2 * stage], bufs[n][3 + 2 * stage]

    def begin(n, stage):
        axis = ORDERS[n][stage]
        p = coordinate[axis]
        own = bufs[n][3]
        opp, fin = buffers(n, stage)
        b = 26 * n + 6 * stage

        def view(t, h):
            return from_own(n, stage, own, t % 4, h, where)

        started(view(p + 2, 0), opp.at[0], b, plus[axis])
        started(view(p + 2, 1), opp.at[1], b + 1, minus[axis])
        started(view(p + 1, 1), fin.at[0, 1], b + 2, plus[axis])
        started(view(p + 3, 0), fin.at[1, 0], b + 3, minus[axis])

    def relay(n, stage):
        axis = ORDERS[n][stage]
        p = coordinate[axis]
        opp, fin = buffers(n, stage)
        b = 26 * n + 6 * stage
        if stage == 0:
            mids = bufs[n][2].at[0], bufs[n][2].at[1]
        else:
            own = bufs[n][3]
            mids = (
                from_own(n, stage, own, (p + 1) % 4, 0, where),
                from_own(n, stage, own, (p + 3) % 4, 1, where),
            )
        arrived(opp.at[0], b)
        add_into(mids[0], [opp.at[0]])
        started(mids[0], fin.at[0, 0], b + 4, plus[axis])
        arrived(opp.at[1], b + 1)
        add_into(mids[1], [opp.at[1]])
        started(mids[1], fin.at[1, 1], b + 5, minus[axis])

    def finish(n, stage):
        p = coordinate[ORDERS[n][stage]]
        own = bufs[n][3]
        _, fin = buffers(n, stage)
        b = 26 * n + 6 * stage
        arrived(fin.at[0, 1], b + 2)
        arrived(fin.at[1, 0], b + 3)
        arrived(fin.at[0, 0], b + 4)
        arrived(fin.at[1, 1], b + 5)
        for h in range(2):
            mine = own.at[h] if stage == 0 else from_own(n, stage, own, p, h, where)
            add_into(mine, [fin.at[0, h], fin.at[1, h]])

    for n in range(3):
        keeps[4 * n].wait()
        keeps[4 * n + 1].wait()
        relay(n, 0)

    for k in range(1, 8):
        small_arrived(sm_a.at[k], k)
    total = small[f]
    for k in range(1, 8):
        total = total + sm_a[k]
    sm_b[0] = total
    for k in range(1, 16):
        small_sent(sm_b.at[0], sm_b.at[k], 7 + k, same_fsdp[k - 1])

    for n in range(3):
        keeps[4 * n + 2].wait()
        keeps[4 * n + 3].wait()
        finish(n, 0)
        begin(n, 1)
    for n in range(3):
        relay(n, 1)
    for n in range(3):
        finish(n, 1)
        begin(n, 2)
    for n in range(3):
        relay(n, 2)

    chip = px * 2 + zh
    mine = zh * 4 + px
    gathers = []
    for n in range(3):
        finish(n, 2)
        own, out = bufs[n][3], outs[n]
        done = [own.at[zl, zh, px], own.at[y // 2, y % 2, px], own.at[zl, y, zh]][n]
        keep = pltpu.make_async_copy(done, out.at[core, mine], local_sem.at[12 + n])
        keep.start()
        gathers.append(keep)
        for k in range(1, 8):
            j = (chip + k) % 8
            started(done, out.at[core, mine], 26 * n + 17 + k, {"fsdp": f, "seq": j * 2 + core})
    for n in range(3):
        out = outs[n]
        for k in range(1, 8):
            j = (chip + 8 - k) % 8
            arrived(out.at[core, (j % 2) * 4 + j // 2], 26 * n + 17 + k)
        gathers[n].wait()
        started(out.at[core], out.at[core], 26 * n + 25, sibling)
    for k in range(1, 16):
        small_arrived(sm_b.at[k], 7 + k)
    total = sm_b[0]
    for k in range(1, 16):
        total = total + sm_b[k]
    small_out[...] = total
    for n in range(3):
        arrived(outs[n].at[1 - core], 26 * n + 25)
    for copy in sends:
        copy.wait_send()


def reduce_all(parts, small, collective_id):
    scratch = []
    for part, lead in zip(parts, LEADS):
        R, C = part.shape[-2:]
        for dims in (
            (2, *lead, R, C),
            (2, 2, *lead, R, C),
            (2, *lead, R, C),
            (2, *lead, R, C),
            (2, 2, R, C),
            (2, 2, 2, R, C),
            (2, R, C // 2),
            (2, 2, R, C // 2),
        ):
            scratch.append(pltpu.VMEM(dims, BF16))
        scratch.append(pltpu.SemaphoreType.DMA)
    outs = [jax.ShapeDtypeStruct((2, 8, *p.shape[-2:]), BF16) for p in parts]
    return pl.pallas_call(
        reduce_kernel,
        out_shape=(*outs, jax.ShapeDtypeStruct((16, 128), F32)),
        in_specs=[HBM, HBM, HBM, VMEM],
        out_specs=(HBM, HBM, HBM, VMEM),
        scratch_shapes=[
            *scratch,
            pltpu.VMEM((8, 16, 128), F32),
            pltpu.VMEM((16, 16, 128), F32),
            pltpu.SemaphoreType.DMA((78,)),
            pltpu.SemaphoreType.DMA((78,)),
            pltpu.SemaphoreType.DMA((15,)),
            pltpu.SemaphoreType.DMA((23,)),
            pltpu.SemaphoreType.DMA((23,)),
        ],
        compiler_params=pltpu.CompilerParams(
            collective_id=collective_id, has_side_effects=True, vmem_limit_bytes=48 * MIB
        ),
    )(*parts, small)


def turn(values, tables, sign):
    cosine, ahead, behind = tables
    moved = pltpu.roll(values, 120, 1) * ahead + pltpu.roll(values, 8, 1) * behind
    return values * cosine + sign * moved


def front_kernel(x, ct, wq, wd, vectors, bias, tables, packed, attn_out, mlp_out):
    values = x[...].astype(F32)
    centered = values - jnp.mean(values, axis=-1, keepdims=True)
    variance = jnp.mean(centered * centered, axis=-1, keepdims=True)
    normed = centered * lax.rsqrt(variance + epsilon)
    attn_out[...] = (normed * vectors[0:1, :] + vectors[1:2, :]).astype(BF16)
    mlp_out[...] = (normed * vectors[2:3, :] + vectors[3:4, :]).astype(BF16)
    low = lax.broadcasted_iota(jnp.int32, (CHIP_TOKENS, 128), 1) < HEAD
    rotary = (tables[0], tables[1], tables[2])
    for pair in range(4):
        a = attn_out[...]
        qk = slice(pair * 256, pair * 256 + 256)
        vs = slice(1024 + pair * 128, 1024 + pair * 128 + 128)
        projected = jnp.dot(a, wq[:, qk], preferred_element_type=F32) + bias[0:1, qk]
        for j in range(2):
            turned = turn(projected[:, j * 128 : j * 128 + 128], rotary, 1.0)
            packed[2 * pair + j, :, 0:128] = turned.astype(BF16)
        v = jnp.dot(a, wq[:, vs], preferred_element_type=F32) + bias[0:1, vs]
        rows = slice(pair * 128, pair * 128 + 128)
        d = lax.dot_general(ct[...], wd[rows, :], NT, preferred_element_type=F32)
        packed[2 * pair, :, 128:256] = jnp.where(low, v, pltpu.roll(d, 64, 1)).astype(BF16)
        packed[2 * pair + 1, :, 128:256] = jnp.where(low, pltpu.roll(v, 64, 1), d).astype(BF16)


def front(x, ct, wq, wd, vectors, bias, tables):
    T = CHIP_TOKENS
    return pl.pallas_call(
        front_kernel,
        out_shape=(
            jax.ShapeDtypeStruct((8, T, 256), BF16),
            jax.ShapeDtypeStruct((T, D), BF16),
            jax.ShapeDtypeStruct((T, D), BF16),
        ),
        in_specs=[VMEM] * 7,
        out_specs=(VMEM,) * 3,
        compiler_params=pltpu.CompilerParams(vmem_limit_bytes=48 * MIB),
    )(x, ct, wq, wd, vectors, bias, tables)


def back_kernel(packed, tables, grad, attended, bias):
    low = lax.broadcasted_iota(jnp.int32, (CHIP_TOKENS, 128), 1) < HEAD
    rotary = (tables[0], tables[1], tables[2])
    for pair in range(4):
        for j in range(2):
            at = slice((2 * pair + j) * 128, (2 * pair + j) * 128 + 128)
            turned = turn(packed[2 * pair + j, :, 0:128].astype(F32), rotary, -1.0).astype(BF16)
            grad[:, at] = turned
            bias[0:1, at] = jnp.sum(turned.astype(F32), axis=0, keepdims=True)
        a = packed[2 * pair, :, 128:256].astype(F32)
        b = packed[2 * pair + 1, :, 128:256].astype(F32)
        at = slice(1024 + pair * 128, 1024 + pair * 128 + 128)
        v = jnp.where(low, a, pltpu.roll(b, 64, 1))
        grad[:, at] = v.astype(BF16)
        bias[0:1, at] = jnp.sum(v, axis=0, keepdims=True)
        o = jnp.where(low, pltpu.roll(a, 64, 1), b)
        attended[:, pair * 128 : pair * 128 + 128] = o.astype(BF16)


def back(packed, tables):
    T = CHIP_TOKENS
    return pl.pallas_call(
        back_kernel,
        out_shape=(
            jax.ShapeDtypeStruct((T, 1536), BF16),
            jax.ShapeDtypeStruct((T, 512), BF16),
            jax.ShapeDtypeStruct((1, 1536), F32),
        ),
        in_specs=[VMEM] * 2,
        out_specs=(VMEM,) * 3,
        compiler_params=pltpu.CompilerParams(vmem_limit_bytes=48 * MIB),
    )(packed, tables)


def rotary_tables(first_position):
    half = ROT // 2
    frequency = 10000.0 ** (-2.0 * jnp.arange(half, dtype=F32) / ROT)
    positions = first_position + jnp.arange(CHIP_TOKENS, dtype=jnp.int32)
    angles = positions.astype(F32)[:, None] * frequency[None, :]
    cosine, sine = jnp.cos(angles), jnp.sin(angles)
    rest = HEAD - ROT
    one = jnp.ones((CHIP_TOKENS, rest), F32)
    zero = jnp.zeros((CHIP_TOKENS, rest), F32)
    none = jnp.zeros((CHIP_TOKENS, half), F32)
    rows = [
        jnp.concatenate([cosine, cosine, one] * 2, axis=1),
        jnp.concatenate([-sine, none, zero] * 2, axis=1),
        jnp.concatenate([none, sine, zero] * 2, axis=1),
    ]
    return jnp.stack(rows)


def gelu_and_slope(h):
    below = 0.5 * lax.erfc(-h * math.sqrt(0.5))
    density = jnp.exp(-0.5 * h * h) * (1.0 / math.sqrt(2.0 * math.pi))
    return h * below, below + h * density


def local(
    inputs,
    cotangent,
    ln_attn_gain,
    ln_attn_bias,
    ln_mlp_gain,
    ln_mlp_bias,
    qkv_weight,
    qkv_bias,
    dense_weight,
    dense_bias,
    hidden_weight,
    hidden_bias,
    output_weight,
    output_bias,
):
    seq = lax.axis_index("seq")
    core = seq % 2
    small = jnp.concatenate(
        [
            ln_attn_gain.reshape(1, 128),
            ln_attn_bias.reshape(1, 128),
            ln_mlp_gain.reshape(1, 128),
            ln_mlp_bias.reshape(1, 128),
            qkv_bias.reshape(3, 128),
            dense_bias.reshape(1, 128),
            hidden_bias.reshape(4, 128),
            output_bias.reshape(1, 128),
            jnp.zeros((3, 128), BF16),
        ]
    )
    own_qkv = lax.dynamic_index_in_dim(
        qkv_weight.reshape(128, 8, 2, 192), core, axis=2, keepdims=False
    )
    own_qkv = jnp.concatenate(
        [own_qkv[:, :, :128].reshape(128, 1024), own_qkv[:, :, 128:].reshape(128, 512)], axis=1
    )
    own_hidden = lax.dynamic_index_in_dim(
        hidden_weight.reshape(128, 8, 2, 256), core, axis=2, keepdims=False
    ).reshape(128, 2048)
    wq, wd, vectors, x, ct = gather(own_qkv, dense_weight, small, inputs, cotangent)
    wq = wq.reshape(D, 1536)
    wd = wd.reshape(512, D)
    x = x.reshape(CHIP_TOKENS, D)
    ct = ct.reshape(CHIP_TOKENS, D)
    vectors = vectors.astype(F32)
    norms = vectors[:, 0:4].transpose(1, 0, 2).reshape(4, D)
    head_bias = lax.dynamic_index_in_dim(
        vectors[:, 4:7].reshape(8, 2, 192), core, axis=1, keepdims=False
    )
    head_bias = jnp.concatenate(
        [head_bias[:, :128].reshape(1, 1024), head_bias[:, 128:].reshape(1, 512)], axis=1
    )
    out_bias = (vectors[:, 7] + vectors[:, 12]).reshape(1, D)
    unit_bias = lax.dynamic_index_in_dim(
        vectors[:, 8:12].reshape(8, 2, 256), core, axis=1, keepdims=False
    ).reshape(1, 2048)

    tables = rotary_tables((seq // 2) * CHIP_TOKENS)
    packed, attn_normed, mlp_normed = front(x, ct, wq, wd, norms, head_bias, tables)
    tokens, wh, wo = attention(packed, own_hidden, output_weight)
    wh = wh.reshape(D, 2048)
    wo = wo.reshape(2048, D)
    projected_grad, attended, head_bias_grad = back(tokens, tables)

    hidden = jnp.dot(mlp_normed, wh, preferred_element_type=F32) + unit_bias
    active, slope = gelu_and_slope(hidden)
    active = active.astype(BF16)
    active_grad = lax.dot_general(ct, wo, NT, preferred_element_type=F32)
    hidden_grad = (active_grad * slope).astype(BF16)
    output_weight_grad = lax.dot_general(active, ct, TN, preferred_element_type=F32)
    hidden_weight_grad = lax.dot_general(mlp_normed, hidden_grad, TN, preferred_element_type=F32)
    mlp_norm_grad = lax.dot_general(hidden_grad, wh, NT, preferred_element_type=F32)
    hidden_bias_grad = jnp.sum(hidden_grad.astype(F32), axis=0)

    branches = jnp.dot(attended, wd, preferred_element_type=F32) + jnp.dot(
        active, wo, preferred_element_type=F32
    )
    attn_norm_grad = lax.dot_general(projected_grad, wq, NT, preferred_element_type=F32)
    weighted = attn_norm_grad * norms[0:1] + mlp_norm_grad * norms[2:3]
    qkv_weight_grad = lax.dot_general(attn_normed, projected_grad, TN, preferred_element_type=F32)
    dense_weight_grad = lax.dot_general(attended, ct, TN, preferred_element_type=F32)

    values = x.astype(F32)
    centered = values - jnp.mean(values, axis=-1, keepdims=True)
    variance = jnp.mean(centered * centered, axis=-1, keepdims=True)
    scale = lax.rsqrt(variance + epsilon)
    normed = centered * scale
    attn_gain_grad = jnp.sum(attn_norm_grad * normed, axis=0)
    attn_bias_grad = jnp.sum(attn_norm_grad, axis=0)
    mlp_gain_grad = jnp.sum(mlp_norm_grad * normed, axis=0)
    mlp_bias_grad = jnp.sum(mlp_norm_grad, axis=0)

    def rows(a, c):
        return lax.dynamic_slice_in_dim(a, c * 256, 256, 0)

    swap = [(i, i + 1 - 2 * (i % 2)) for i in range(16)]
    given = jnp.concatenate(
        [rows(branches, 1 - core).astype(BF16), rows(weighted, 1 - core).astype(BF16)]
    )
    taken = lax.ppermute(given, "seq", swap).astype(F32)
    outputs = inputs.astype(F32) + rows(branches, core) + taken[:256] + out_bias
    w = rows(weighted, core) + taken[256:]
    n = rows(normed, core)
    input_grad = cotangent.astype(F32) + rows(scale, core) * (
        w - jnp.mean(w, axis=-1, keepdims=True) - n * jnp.mean(w * n, axis=-1, keepdims=True)
    )

    mine = (jnp.arange(2) == core).astype(F32)
    cotangent_sum = jnp.sum(cotangent.astype(F32), axis=0)
    per_head = jnp.concatenate(
        [head_bias_grad[0, :1024].reshape(8, 128), head_bias_grad[0, 1024:].reshape(8, 64)], axis=1
    )
    small_grads = jnp.concatenate(
        [
            attn_gain_grad.reshape(8, 1, 128),
            attn_bias_grad.reshape(8, 1, 128),
            mlp_gain_grad.reshape(8, 1, 128),
            mlp_bias_grad.reshape(8, 1, 128),
            (per_head[:, None, :] * mine[None, :, None]).reshape(8, 3, 128),
            cotangent_sum.reshape(8, 1, 128),
            (hidden_bias_grad.reshape(8, 1, 256) * mine[None, :, None]).reshape(8, 4, 128),
            jnp.zeros((8, 4, 128), F32),
        ],
        axis=1,
    )
    dense_part = dense_weight_grad.astype(BF16).reshape(8, 64, 2, 512).transpose(0, 2, 1, 3)
    heads_part = jnp.concatenate(
        [qkv_weight_grad.astype(BF16).reshape(8, 128, 1536), dense_part.reshape(8, 128, 512)],
        axis=2,
    )
    hidden_sum, output_sum, heads_sum, small_sum = reduce_all(
        (
            hidden_weight_grad.astype(BF16).reshape(4, 2, 2, 4, 16, 2048),
            output_weight_grad.astype(BF16).reshape(4, 2, 2, 4, 32, 1024),
            heads_part.reshape(4, 2, 2, 4, 16, 2048),
        ),
        small_grads,
        3,
    )
    hidden_total = (
        hidden_sum.reshape(2, 128, 8, 256).transpose(1, 2, 0, 3).reshape(128, FF).astype(F32)
    )
    output_total = output_sum.reshape(512, D).astype(F32)
    heads_sum = heads_sum.reshape(2, 128, 2048)
    qkv_total = jnp.concatenate(
        [
            heads_sum[:, :, :1024].reshape(2, 128, 8, 128),
            heads_sum[:, :, 1024:1536].reshape(2, 128, 8, 64),
        ],
        axis=3,
    )
    qkv_total = qkv_total.transpose(1, 2, 0, 3).reshape(128, 3 * D).astype(F32)
    dense_total = heads_sum[:, :, 1536:].reshape(2, 2, 64, 512).transpose(0, 2, 1, 3)
    dense_total = dense_total.reshape(128, D).astype(F32)
    return (
        outputs.astype(BF16),
        input_grad,
        small_sum[0],
        small_sum[1],
        small_sum[2],
        small_sum[3],
        qkv_total,
        small_sum[4:7].reshape(384),
        dense_total,
        small_sum[7],
        hidden_total,
        small_sum[8:12].reshape(512),
        output_total,
        small_sum[7],
    )


def solution(mesh):
    rows = P(("fsdp", "seq"), None)
    vector = P("fsdp")
    matrix = P("fsdp", None)
    shared = (vector,) * 4 + (matrix, vector) * 4
    return jax.shard_map(
        local,
        mesh=mesh,
        in_specs=(rows, rows, *shared),
        out_specs=(rows, rows, *shared),
        check_vma=False,
    )
```

```python
import functools
import math

import jax
import jax.numpy as jnp
from jax import lax
from jax.experimental import pallas as pl
from jax.experimental.pallas import tpu as pltpu
from jax.sharding import PartitionSpec as P

D = 1024
FF = 4096
HEADS = 16
HEAD = 64
ROT = 16
CHIP_TOKENS = 512
FSDP = 8
CHIPS = 8

epsilon = 1e-05
F32 = jnp.float32
BF16 = jnp.bfloat16
NT = (((1,), (1,)), ((), ()))
TN = (((0,), (0,)), ((), ()))
MIB = 2**20
HBM = pl.BlockSpec(memory_space=pl.ANY)
VMEM = pl.BlockSpec(memory_space=pltpu.VMEM)


def place():
    f = lax.axis_index("fsdp")
    s = lax.axis_index("seq")
    return f, s, (f // 2, f % 2, s // 4, (s // 2) % 2, s % 2)


def device(y, z, x, core):
    return {"fsdp": y * 2 + z % 2, "seq": x * 4 + (z // 2) * 2 + core}


def barrier(devices):
    sem = pltpu.get_barrier_semaphore()
    for d in devices:
        pl.semaphore_signal(sem, inc=1, device_id=d, device_id_type=pl.DeviceIdType.MESH)
    pl.semaphore_wait(sem, len(devices))


def remote(src, dst, send, recv, target):
    return pltpu.make_async_remote_copy(
        src_ref=src,
        dst_ref=dst,
        send_sem=send,
        recv_sem=recv,
        device_id=target,
        device_id_type=pl.DeviceIdType.MESH,
    )


class Gather:
    def __init__(self, own, full, send, recv):
        f, s, (y, zl, px, zh, core) = place()
        z = zh * 2 + zl
        self.own, self.full, self.send, self.recv = own, full, send, recv
        self.yp = device((y + 1) % 4, z, px, core)
        self.ym = device((y + 3) % 4, z, px, core)
        self.zp = device(y, (z + 1) % 4, px, core)
        self.zm = device(y, (z + 3) % 4, px, core)
        self.f = f
        self.slots = [f, (f + 6) % 8, (f + 2) % 8, (f + 4) % 8]
        flip = f + 1 - 2 * zl
        self.far = [flip, (flip + 6) % 8, (flip + 2) % 8, (flip + 4) % 8]
        self.sends = []

    def neighbours(self):
        return [self.yp, self.ym, self.zp, self.zm]

    def started(self, src, dst, k, target):
        copy = remote(src, dst, self.send.at[k], self.recv.at[k], target)
        copy.start()
        self.sends.append(copy)

    def arrived(self, ref, k):
        remote(ref, ref, self.send.at[k], self.recv.at[k], self.yp).wait_recv()

    @staticmethod
    def part(ref, h):
        rows = ref.shape[0] // 2
        return ref.at[pl.ds(h * rows, rows)]

    def own_y(self):
        for n, (o, g) in enumerate(zip(self.own, self.full)):
            for k, h, target in ((0, 0, self.yp), (3, 1, self.ym), (2, 0, self.ym), (1, 1, self.yp)):
                self.started(self.part(o, h), self.part(g.at[self.f], h), 14 * n + k, target)

    def own_z(self):
        for n, (o, g) in enumerate(zip(self.own, self.full)):
            for k, h, target in ((6, 0, self.zp), (10, 1, self.zm)):
                self.started(self.part(o, h), self.part(g.at[self.f], h), 14 * n + k, target)

    def pass_on(self, n, k, slot, h, targets):
        ref = self.part(self.full[n].at[slot], h)
        self.arrived(ref, 14 * n + k)
        for kk, target in targets:
            self.started(ref, ref, 14 * n + kk, target)

    def near(self):
        for n in range(len(self.full)):
            self.pass_on(n, 0, self.slots[1], 0, [(4, self.yp), (7, self.zp)])
            self.pass_on(n, 3, self.slots[2], 1, [(5, self.ym), (12, self.zm)])
            self.pass_on(n, 2, self.slots[2], 0, [(8, self.zp)])
            self.pass_on(n, 1, self.slots[1], 1, [(11, self.zm)])

    def opposite(self):
        for n in range(len(self.full)):
            self.pass_on(n, 4, self.slots[3], 0, [(9, self.zp)])
            self.pass_on(n, 5, self.slots[3], 1, [(13, self.zm)])

    def finish(self):
        for n, g in enumerate(self.full):
            for j in range(4):
                self.arrived(self.part(g.at[self.far[j]], 0), 14 * n + 6 + j)
                self.arrived(self.part(g.at[self.far[j]], 1), 14 * n + 10 + j)
        for copy in self.sends:
            copy.wait_send()


def gather_kernel(wq, wd, small, x, ct, gq, gd, gs, gx, gc, send, recv, local_sem):
    f, s, (y, zl, px, zh, core) = place()
    sibling = device(y, zh * 2 + zl, px, 1 - core)
    others = [{"fsdp": (f + k) % 8, "seq": s} for k in range(1, 8)]
    zother = device(y, 2 * (1 - zh) + 1 - zl, px, core)
    own = [wq, wd.at[pl.ds(pl.multiple_of(core * 64, 64), 64)]]
    weights = Gather(own, [gq, gd], send, recv)
    barrier(others + [sibling, zother])
    base = 28
    weights.own_y()
    weights.started(x, gx.at[core], base, sibling)
    weights.started(ct, gc.at[core], base + 1, sibling)
    for k in range(1, 8):
        weights.started(small, gs.at[f], base + 1 + k, others[k - 1])
    weights.own_z()
    pairs = [(gx.at[core], x), (gc.at[core], ct), (gs.at[f], small), (gq.at[f], own[0]), (gd.at[f], own[1])]
    keeps = []
    for k, (b, a) in enumerate(pairs):
        copy = pltpu.make_async_copy(a, b, local_sem.at[k])
        copy.start()
        keeps.append(copy)
    weights.near()
    weights.opposite()
    weights.arrived(gx.at[1 - core], base)
    weights.arrived(gc.at[1 - core], base + 1)
    for k in range(1, 8):
        weights.arrived(gs.at[(f + 8 - k) % 8], base + 1 + k)
    weights.finish()
    for copy in keeps:
        copy.wait()


def gather(wq, wd, small, x, ct):
    def shape(*dims):
        return jax.ShapeDtypeStruct(dims, BF16)

    return pl.pallas_call(
        gather_kernel,
        out_shape=(
            shape(8, 128, 1536),
            shape(8, 64, 1024),
            shape(8, 16, 128),
            shape(2, 256, 1024),
            shape(2, 256, 1024),
        ),
        in_specs=[HBM] * 5,
        out_specs=(HBM,) * 5,
        scratch_shapes=[
            pltpu.SemaphoreType.DMA((37,)),
            pltpu.SemaphoreType.DMA((37,)),
            pltpu.SemaphoreType.DMA((5,)),
        ],
        compiler_params=pltpu.CompilerParams(collective_id=0, has_side_effects=True),
    )(wq, wd, small, x, ct)


def fold(op, a):
    result = a[:, :128]
    for j in range(128, a.shape[1], 128):
        result = op(result, a[:, j : j + 128])
    return result


def attention_kernel(
    packed, wh, wo, result, gh, go,
    hd, out, q_s, k_s, v_s, d_s, s_s, p_s, dk_s, dv_s, mx_s, l_s, o_s, dq_s,
    in_send, in_recv, out_send, out_recv, g_send, g_recv, local_sem,
):
    f, s, (y, zl, px, zh, core) = place()
    me = s // 2
    B = CHIP_TOKENS
    n = CHIPS
    scale = 1.0 / math.sqrt(HEAD)
    own = [wh, wo.at[pl.ds(pl.multiple_of(core * 256, 256), 256)]]
    weights = Gather(own, [gh, go], g_send, g_recv)

    def chip(j):
        return {"fsdp": f, "seq": j * 2 + core}

    barrier([chip((me + k) % n) for k in range(1, n)] + weights.neighbours())
    given = []
    for k in range(1, n):
        j = (me + k) % n
        copy = remote(packed.at[j], hd.at[me], in_send.at[k], in_recv.at[k], chip(j))
        copy.start()
        given.append(copy)
    weights.own_y()
    keeps = []
    for k, (a, b) in enumerate([(packed.at[me], hd.at[me]), (own[0], gh.at[f]), (own[1], go.at[f])]):
        copy = pltpu.make_async_copy(a, b, local_sem.at[k])
        copy.start()
        keeps.append(copy)
    keeps[0].wait()
    for k in range(1, n):
        ref = hd.at[(me + n - k) % n]
        remote(ref, ref, in_send.at[k], in_recv.at[k], chip(me)).wait_recv()
    weights.own_z()

    def block(i):
        return pl.ds(pl.multiple_of(i * B, B), B)

    def prepare(i, _):
        rows = block(i)
        piece = hd[i]
        q_s[rows, :] = piece[:, 0:64] * jnp.asarray(scale, BF16)
        k_s[rows, :] = piece[:, 64:128]
        v_s[rows, :] = piece[:, 128:192]
        d_s[rows, :] = piece[:, 192:256]
        return 0

    lax.fori_loop(0, n, prepare, 0)
    dk_s[...] = jnp.zeros_like(dk_s)
    dv_s[...] = jnp.zeros_like(dv_s)
    keep = lax.broadcasted_iota(jnp.int32, (B, B), 1) <= lax.broadcasted_iota(
        jnp.int32, (B, B), 0
    )

    def back_to(i):
        return remote(out.at[i], result.at[me], out_send.at[i], out_recv.at[me], chip(i))

    def query_block(t, _):
        i = n - 1 - t
        rows = block(i)
        qi = q_s[rows, :]
        mx_s[...] = jnp.full(mx_s.shape, -1e30, F32)

        def score(kb):
            return lax.dot_general(qi, k_s[block(kb), :], NT, preferred_element_type=F32)

        def first(kb, _):
            scores = score(kb)
            s_s[kb] = scores
            mx_s[...] = jnp.maximum(mx_s[...], fold(jnp.maximum, scores))
            return 0

        lax.fori_loop(0, i, first, 0)
        scores = jnp.where(keep, score(i), -1e30)
        s_s[i] = scores
        row_max = jnp.max(
            jnp.maximum(mx_s[...], fold(jnp.maximum, scores)), axis=1, keepdims=True
        )
        l_s[...] = jnp.zeros_like(l_s)
        o_s[...] = jnp.zeros_like(o_s)
        dq_s[...] = jnp.zeros_like(dq_s)

        def second(kb, _):
            p = jnp.exp(s_s[kb] - row_max)
            l_s[...] += fold(jnp.add, p)
            pb = p.astype(BF16)
            p_s[kb] = pb
            o_s[...] += jnp.dot(pb, v_s[block(kb), :], preferred_element_type=F32)
            return 0

        lax.fori_loop(0, i + 1, second, 0)
        inverse = 1.0 / jnp.sum(l_s[...], axis=1, keepdims=True)
        o = o_s[...] * inverse
        d = (d_s[rows, :].astype(F32) * inverse).astype(BF16)
        delta = jnp.sum(o * d.astype(F32), axis=1, keepdims=True)
        q_t = qi.T
        d_t = d.T

        def third(kb, _):
            cols = block(kb)
            pb = p_s[kb]
            dp = lax.dot_general(d, v_s[cols, :], NT, preferred_element_type=F32)
            ds = (pb.astype(F32) * (dp - delta)).astype(BF16)
            dq_s[...] += jnp.dot(ds, k_s[cols, :], preferred_element_type=F32)
            dk_s[:, cols] += jnp.dot(q_t, ds, preferred_element_type=F32)
            dv_s[:, cols] += jnp.dot(d_t, pb, preferred_element_type=F32)
            return 0

        lax.fori_loop(0, i + 1, third, 0)
        out[i, :, 0:64] = (dq_s[...] * scale).astype(BF16)
        out[i, :, 64:128] = dk_s[:, rows].T.astype(BF16)
        out[i, :, 128:192] = dv_s[:, rows].T.astype(BF16)
        out[i, :, 192:256] = o.astype(BF16)

        @pl.when(i != me)
        def _():
            back_to(i).start()

        @pl.when(i == me)
        def _():
            pltpu.make_async_copy(out.at[i], result.at[i], local_sem.at[3]).start()

        return 0

    lax.fori_loop(0, 1, query_block, 0)
    weights.near()
    lax.fori_loop(1, 2, query_block, 0)
    weights.opposite()
    lax.fori_loop(2, n, query_block, 0)

    for copy in given:
        copy.wait_send()
    keeps[1].wait()
    keeps[2].wait()
    weights.finish()
    for k in range(1, n):
        back_to((me + k) % n).wait_send()
    pltpu.make_async_copy(out.at[me], result.at[me], local_sem.at[3]).wait()
    for k in range(1, n):
        j = (me + k) % n
        ref = result.at[j]
        remote(ref, ref, out_send.at[j], out_recv.at[j], chip(me)).wait_recv()


def attention(packed, wh, wo):
    B = CHIP_TOKENS
    L = CHIPS * B
    return pl.pallas_call(
        attention_kernel,
        out_shape=(
            jax.ShapeDtypeStruct((CHIPS, B, 4 * HEAD), BF16),
            jax.ShapeDtypeStruct((8, 128, 2048), BF16),
            jax.ShapeDtypeStruct((8, 256, 1024), BF16),
        ),
        in_specs=[HBM] * 3,
        out_specs=(HBM,) * 3,
        scratch_shapes=[
            *[pltpu.VMEM((CHIPS, B, 4 * HEAD), BF16)] * 2,
            *[pltpu.VMEM((L, HEAD), BF16)] * 4,
            pltpu.VMEM((L // B, B, B), F32),
            pltpu.VMEM((L // B, B, B), BF16),
            *[pltpu.VMEM((HEAD, L), F32)] * 2,
            *[pltpu.VMEM((B, 128), F32)] * 2,
            *[pltpu.VMEM((B, HEAD), F32)] * 2,
            *[pltpu.SemaphoreType.DMA((CHIPS,))] * 4,
            *[pltpu.SemaphoreType.DMA((28,))] * 2,
            pltpu.SemaphoreType.DMA((4,)),
        ],
        compiler_params=pltpu.CompilerParams(
            collective_id=1, has_side_effects=True, vmem_limit_bytes=56 * MIB
        ),
    )(packed, wh, wo)


ORDERS = ("yzx", "zxy", "xyz")
LEADS = ((2, 4), (2, 4), (4, 2))
ROWS = (16, 32, 16)
COLUMNS = (2048, 1024, 2048)


def chunk(n, stage, g, t, h, where):
    y, zl, zh, px = where
    if stage == 0:
        if n == 0:
            return g.at[t, h]
        if n == 1:
            return g.at[pl.ds(2 * h, 2), t % 2, t // 2]
        return g.at[:, h, :, t]
    if stage == 1:
        if n == 0:
            return g.at[y, t % 2, t // 2, pl.ds(2 * h, 2)]
        if n == 1:
            return g.at[pl.ds(2 * h, 2), zl, zh, t]
        return g.at[t, h, :, px]
    half = g.shape[-1] // 2
    columns = pl.ds(h * half, half)
    if n == 0:
        return g.at[y, zl, zh, t, :, columns]
    if n == 1:
        return g.at[t, zl, zh, px, :, columns]
    return g.at[y, t % 2, t // 2, px, :, columns]


def add_into(dst, terms):
    lead = tuple(dst.shape[:-2])

    def body(k, _):
        at = []
        for extent in reversed(lead):
            at.insert(0, k % extent)
            k = k // extent
        at = (*at, slice(None), slice(None))
        total = dst[at].astype(F32)
        for t in terms:
            total = total + t[at].astype(F32)
        dst[at] = total.astype(BF16)
        return 0

    lax.fori_loop(0, math.prod(lead), body, 0)


def normalised(values):
    values = values.astype(F32)
    centered = values - jnp.mean(values, axis=-1, keepdims=True)
    variance = jnp.mean(centered * centered, axis=-1, keepdims=True)
    scale = lax.rsqrt(variance + epsilon)
    return centered * scale, scale


def rest_kernel(
    tokens, x, ct, an, mn, wq, wd, wh, wo, norms, unit_bias, out_bias, tables,
    outputs, input_grad, hidden_out, output_out, qkv_out, dense_out, small_out,
    x_v, ct_v, an_v, mn_v, branches, weighted, sums, small, sm_a, sm_b, pair_send, pair_recv,
    g0, g1, g2, *rest,
):
    grads = (g0, g1, g2)
    bufs = [rest[7 * n : 7 * n + 7] for n in range(3)]
    send, recv, local_sem, sm_send, sm_recv = rest[21:]
    f, s, (y, zl, px, zh, core) = place()
    z = zh * 2 + zl
    coordinate = {"y": y, "z": z, "x": px}
    where = (y, zl, zh, px)
    T = CHIP_TOKENS

    def along(axis, step):
        t = dict(coordinate)
        t[axis] = (t[axis] + step) % 4
        return device(t["y"], t["z"], t["x"], core)

    plus = {a: along(a, 1) for a in "yzx"}
    minus = {a: along(a, 3) for a in "yzx"}
    same_seq = [{"fsdp": (f + k) % 8, "seq": s} for k in range(1, 8)]
    same_fsdp = [{"fsdp": f, "seq": (s + k) % 16} for k in range(1, 16)]
    zother = device(y, 2 * (1 - zh) + 1 - zl, px, core)
    sibling = device(y, z, px, 1 - core)
    sends = []

    def load(src, dst, k):
        copy = pltpu.make_async_copy(src, dst, local_sem.at[k])
        copy.start()
        return copy

    def started(src, dst, k, target):
        copy = remote(src, dst, send.at[k], recv.at[k], target)
        copy.start()
        sends.append(copy)

    def arrived(ref, k):
        remote(ref, ref, send.at[k], recv.at[k], sibling).wait_recv()

    def small_sent(src, dst, k, target):
        copy = remote(src, dst, sm_send.at[k], sm_recv.at[k], target)
        copy.start()
        sends.append(copy)

    def small_arrived(ref, k):
        remote(ref, ref, sm_send.at[k], sm_recv.at[k], sibling).wait_recv()

    def buffers(n, stage):
        return bufs[n][2 * stage], bufs[n][2 * stage + 1]

    def raw_copies(n, stage):
        axis = ORDERS[n][stage]
        p = coordinate[axis]
        opp, fin = buffers(n, stage)
        b = 26 * n + 6 * stage

        def copy(t, h, dst, k, target):
            src = chunk(n, stage, grads[n], t % 4, h, where)
            return remote(src, dst, send.at[k], recv.at[k], target)

        return [
            copy(p + 2, 0, opp.at[0], b, plus[axis]),
            copy(p + 2, 1, opp.at[1], b + 1, minus[axis]),
            copy(p + 1, 1, fin.at[0, 1], b + 2, plus[axis]),
            copy(p + 3, 0, fin.at[1, 0], b + 3, minus[axis]),
        ]

    def relay_copy(n, stage, h):
        axis = ORDERS[n][stage]
        _, fin = buffers(n, stage)
        k = 26 * n + 6 * stage + 4 + h
        t = coordinate[axis] + 1 + 2 * h
        src = chunk(n, stage, grads[n], t % 4, h, where)
        target = (plus, minus)[h][axis]
        return src, remote(src, fin.at[h, h], send.at[k], recv.at[k], target)

    def begin(n, stage):
        for copy in raw_copies(n, stage):
            copy.start()

    def relay(n, stage):
        opp, _ = buffers(n, stage)
        for h in range(2):
            mid, copy = relay_copy(n, stage, h)
            arrived(opp.at[h], 26 * n + 6 * stage + h)
            add_into(mid, [opp.at[h]])
            copy.start()

    def finish(n, stage):
        p = coordinate[ORDERS[n][stage]]
        _, fin = buffers(n, stage)
        b = 26 * n + 6 * stage
        arrived(fin.at[0, 1], b + 2)
        arrived(fin.at[1, 0], b + 3)
        arrived(fin.at[0, 0], b + 4)
        arrived(fin.at[1, 1], b + 5)
        for h in range(2):
            add_into(chunk(n, stage, grads[n], p, h, where), [fin.at[0, h], fin.at[1, h]])

    keeps = [load(a, b, k) for k, (a, b) in enumerate([(x, x_v), (ct, ct_v), (an, an_v), (mn, mn_v)])]
    barrier(same_seq + same_fsdp + [zother])
    small[...] = jnp.zeros_like(small)

    def attention_part(wq_v, wd_v, tk_v, pg_v, at_v, turned_v):
        loads = [load(a, b, 4 + k) for k, (a, b) in enumerate([(tokens, tk_v), (wq, wq_v), (wd, wd_v)])]
        for copy in keeps:
            copy.wait()
        loads[0].wait()
        low = lax.broadcasted_iota(jnp.int32, (T, 128), 1) < HEAD
        first = lax.broadcasted_iota(jnp.int32, (1, 128), 1) < HEAD
        rotary = (tables[0], tables[1], tables[2])
        for pair in range(4):
            for j in range(2):
                r = 2 * pair + j
                at = slice(r * 128, r * 128 + 128)
                turned = turn(tk_v[r, :, 0:128].astype(F32), rotary, -1.0).astype(BF16)
                pg_v[:, at] = turned
                small[r, pl.ds(4 + core, 1), :] = jnp.sum(turned.astype(F32), axis=0, keepdims=True)
            a = tk_v[2 * pair, :, 128:256].astype(F32)
            b = tk_v[2 * pair + 1, :, 128:256].astype(F32)
            v = jnp.where(low, a, pltpu.roll(b, 64, 1))
            pg_v[:, 1024 + pair * 128 : 1152 + pair * 128] = v.astype(BF16)
            total = jnp.sum(v, axis=0, keepdims=True)
            moved = jnp.sum(jnp.where(low, pltpu.roll(v, 64, 1), pltpu.roll(v, 64, 1)), axis=0, keepdims=True)
            zero = jnp.zeros_like(total)
            at_low = (jnp.where(first, total, zero), jnp.where(first, moved, zero))
            at_high = (jnp.where(first, zero, moved), jnp.where(first, zero, total))
            for j in range(2):
                small[2 * pair + j, 6:7, :] = jnp.where(core == 0, at_low[j], at_high[j])
            o = jnp.where(low, pltpu.roll(a, 64, 1), b)
            at_v[:, pair * 128 : pair * 128 + 128] = o.astype(BF16)

        turned_v[...] = an_v[...].T

        def qkv_columns(k, _):
            at = pl.ds(pl.multiple_of(k * 512, 512), 512)
            part = jnp.dot(turned_v[...], pg_v[:, at], preferred_element_type=F32)
            g2[:, :, :, :, :, at] = part.astype(BF16).reshape(4, 2, 2, 4, 16, 512)
            return 0

        lax.fori_loop(0, 3, qkv_columns, 0)
        turned_v[0:512, :] = at_v[...].T
        for k in range(2):
            part = jnp.dot(
                turned_v[0:512, :], ct_v[:, k * 512 : k * 512 + 512], preferred_element_type=F32
            )
            g2[:, :, k, :, :, 1536:2048] = part.astype(BF16).reshape(4, 2, 4, 16, 512)
        begin(2, 0)
        loads[1].wait()
        loads[2].wait()
        grad = lax.dot_general(pg_v[...], wq_v[...], NT, preferred_element_type=F32)
        normed, _ = normalised(x_v[...])
        sums[0:1, :] = jnp.sum(grad * normed, axis=0, keepdims=True)
        sums[1:2, :] = jnp.sum(grad, axis=0, keepdims=True)
        weighted[...] = grad * norms[0:1, :]
        branches[...] = jnp.dot(at_v[...], wd_v[...], preferred_element_type=F32)

    pl.run_scoped(
        attention_part,
        pltpu.VMEM((D, 1536), BF16),
        pltpu.VMEM((512, D), BF16),
        pltpu.VMEM((8, T, 256), BF16),
        pltpu.VMEM((T, 1536), BF16),
        pltpu.VMEM((T, 512), BF16),
        pltpu.VMEM((D, T), BF16),
    )

    def unit_part(wh_v, wo_v, act_v, hg_v, turned_v):
        loads = [load(a, b, 7 + k) for k, (a, b) in enumerate([(wh, wh_v), (wo, wo_v)])]
        loads[0].wait()
        loads[1].wait()

        def units(r, _):
            at = pl.ds(pl.multiple_of(r * 256, 256), 256)
            h = jnp.dot(mn_v[...], wh_v[:, at], preferred_element_type=F32) + unit_bias[0:1, at]
            below = 0.5 + 0.5 * lax.erf(h * math.sqrt(0.5))
            density = jnp.exp(-0.5 * h * h) * (1.0 / math.sqrt(2.0 * math.pi))
            act_v[:, at] = (h * below).astype(BF16)
            up = lax.dot_general(ct_v[...], wo_v[at, :], NT, preferred_element_type=F32)
            grad = (up * (below + h * density)).astype(BF16)
            hg_v[:, at] = grad
            total = jnp.sum(grad.astype(F32), axis=0, keepdims=True)
            small[r, pl.ds(8 + 2 * core, 1), :] = total[:, 0:128]
            small[r, pl.ds(9 + 2 * core, 1), :] = total[:, 128:256]
            return 0

        lax.fori_loop(0, 8, units, 0)
        turned_v[...] = act_v[...].T

        def output_rows(k, _):
            at = pl.ds(pl.multiple_of(k * 512, 512), 512)
            part = jnp.dot(turned_v[at, :], ct_v[...], preferred_element_type=F32)
            g1[k] = part.astype(BF16).reshape(2, 2, 4, 32, 1024)
            return 0

        lax.fori_loop(0, 4, output_rows, 0)
        begin(1, 0)
        turned_v[0:D, :] = mn_v[...].T

        def hidden_columns(k, _):
            at = pl.ds(pl.multiple_of(k * 512, 512), 512)
            part = jnp.dot(turned_v[0:D, :], hg_v[:, at], preferred_element_type=F32)
            g0[:, :, :, :, :, at] = part.astype(BF16).reshape(4, 2, 2, 4, 16, 512)
            return 0

        lax.fori_loop(0, 4, hidden_columns, 0)
        begin(0, 0)
        relay(2, 0)
        grad = lax.dot_general(hg_v[...], wh_v[...], NT, preferred_element_type=F32)
        normed, _ = normalised(x_v[...])
        sums[2:3, :] = jnp.sum(grad * normed, axis=0, keepdims=True)
        sums[3:4, :] = jnp.sum(grad, axis=0, keepdims=True)
        weighted[...] += grad * norms[2:3, :]
        branches[...] += jnp.dot(act_v[...], wo_v[...], preferred_element_type=F32)

    pl.run_scoped(
        unit_part,
        pltpu.VMEM((D, 2048), BF16),
        pltpu.VMEM((2048, D), BF16),
        pltpu.VMEM((T, 2048), BF16),
        pltpu.VMEM((T, 2048), BF16),
        pltpu.VMEM((2048, T), BF16),
    )

    other = pl.ds(pl.multiple_of((1 - core) * 256, 256), 256)
    mine = pl.ds(pl.multiple_of(core * 256, 256), 256)
    pair_send[0] = branches[other, :].astype(BF16)
    pair_send[1] = weighted[other, :].astype(BF16)
    started(pair_send, pair_recv, 78, sibling)
    sums[4:5, :] = jnp.sum(ct_v[mine, :].astype(F32), axis=0, keepdims=True)
    for r in range(8):
        at = slice(r * 128, r * 128 + 128)
        small[r, 0:4, :] = sums[0:4, at]
        small[r, 7:8, :] = sums[4:5, at]
    for k in range(1, 8):
        small_sent(small.at[(f + k) % 8], sm_a.at[k], k, same_seq[k - 1])
    relay(1, 0)
    relay(0, 0)
    arrived(pair_recv, 78)
    normed, scale = normalised(x_v[mine, :])
    total = x_v[mine, :].astype(F32) + branches[mine, :] + pair_recv[0].astype(F32) + out_bias[...]
    outputs[...] = total.astype(BF16)
    w = weighted[mine, :] + pair_recv[1].astype(F32)
    input_grad[...] = ct_v[mine, :].astype(F32) + scale * (
        w
        - jnp.mean(w, axis=-1, keepdims=True)
        - normed * jnp.mean(w * normed, axis=-1, keepdims=True)
    )
    finish(2, 0)
    begin(2, 1)
    for k in range(1, 8):
        small_arrived(sm_a.at[k], k)
    total = small[f]
    for k in range(1, 8):
        total = total + sm_a[k]
    sm_b[0] = total
    for k in range(1, 16):
        small_sent(sm_b.at[0], sm_b.at[k], 7 + k, same_fsdp[k - 1])
    finish(1, 0)
    begin(1, 1)
    finish(0, 0)
    begin(0, 1)

    across = device(y, (z + 2) % 4, px, core)
    xp, xm = plus["x"], minus["x"]

    def at_chip(n, zz, xx):
        return bufs[n][6].at[core, zz * 4 + xx % 4]

    def spread(n):
        b = 26 * n + 18
        done = grads[n].at[y, zl, zh, px]
        place_ = at_chip(n, zh, px)
        keep = pltpu.make_async_copy(done, place_, local_sem.at[9 + n])
        keep.start()
        started(done, place_, b, across)
        started(done, place_, b + 1, xp)
        started(done, place_, b + 2, xm)
        return keep

    def spread_on(n):
        b = 26 * n + 18
        theirs = at_chip(n, 1 - zh, px)
        arrived(theirs, b)
        started(theirs, theirs, b + 3, xp)
        started(theirs, theirs, b + 4, xm)
        left, right = at_chip(n, zh, px + 3), at_chip(n, 1 - zh, px + 1)
        arrived(left, b + 1)
        started(left, left, b + 5, xp)
        arrived(right, b + 4)
        started(right, right, b + 6, xm)

    def spread_end(n, keep):
        b = 26 * n + 18
        arrived(at_chip(n, zh, px + 1), b + 2)
        arrived(at_chip(n, 1 - zh, px + 3), b + 3)
        arrived(at_chip(n, zh, px + 2), b + 5)
        arrived(at_chip(n, 1 - zh, px + 2), b + 6)
        keep.wait()
        whole = bufs[n][6].at[core]
        started(whole, whole, b + 7, sibling)

    order = (2, 1, 0)
    for n in order:
        relay(n, 1)
    for n in order:
        finish(n, 1)
        begin(n, 2)
    for n in order:
        relay(n, 2)
    copies = {}
    for n in order:
        finish(n, 2)
        copies[n] = spread(n)
    for n in order:
        spread_on(n)
    for n in order:
        spread_end(n, copies[n])
    for k in range(1, 16):
        small_arrived(sm_b.at[k], 7 + k)
    total = sm_b[0]
    for k in range(1, 16):
        total = total + sm_b[k]
    small_out[...] = total

    def finals(hidden_v, output_v, qkv_v, dense_v):
        ends = []
        a = bufs[2][6]
        arrived(a.at[1 - core], 26 * 2 + 25)
        low = lax.broadcasted_iota(jnp.int32, (128, 128), 1) < HEAD
        for pair in range(4):
            v0 = a[0, :, :, 1024 + pair * 128 : 1152 + pair * 128].reshape(128, 128).astype(F32)
            v1 = a[1, :, :, 1024 + pair * 128 : 1152 + pair * 128].reshape(128, 128).astype(F32)
            for j in range(2):
                r = 2 * pair + j
                q0 = a[0, :, :, r * 128 : r * 128 + 128].reshape(128, 128).astype(F32)
                q1 = a[1, :, :, r * 128 : r * 128 + 128].reshape(128, 128).astype(F32)
                q1 = pltpu.roll(q1, 64, 1)
                left = v0 if j == 0 else pltpu.roll(v0, 64, 1)
                right = pltpu.roll(v1, 64, 1) if j == 0 else v1
                qkv_v[:, r * 384 : r * 384 + 128] = q0
                qkv_v[:, r * 384 + 128 : r * 384 + 256] = jnp.where(low, left, q1)
                qkv_v[:, r * 384 + 256 : r * 384 + 384] = jnp.where(low, q1, right)
        for c in range(2):
            for k in range(2):
                piece = a[c, k * 4 : k * 4 + 4, :, 1536:2048].reshape(64, 512)
                dense_v[c * 64 : c * 64 + 64, k * 512 : k * 512 + 512] = piece.astype(F32)
        ends.append(load(qkv_v, qkv_out, 12))
        ends.append(load(dense_v, dense_out, 13))
        a1 = bufs[1][6]
        arrived(a1.at[1 - core], 26 + 25)
        output_v[...] = a1[...].reshape(512, D).astype(F32)
        ends.append(load(output_v, output_out, 14))
        a0 = bufs[0][6]
        arrived(a0.at[1 - core], 25)
        for c in range(2):
            for r in range(8):
                piece = a0[c, :, :, r * 256 : r * 256 + 256].reshape(128, 256)
                hidden_v[:, r * 512 + c * 256 : r * 512 + c * 256 + 256] = piece.astype(F32)
        ends.append(load(hidden_v, hidden_out, 15))
        for copy in ends:
            copy.wait()

    pl.run_scoped(
        finals,
        pltpu.VMEM((128, FF), F32),
        pltpu.VMEM((512, D), F32),
        pltpu.VMEM((128, 3 * D), F32),
        pltpu.VMEM((128, D), F32),
    )
    for copy in sends:
        copy.wait_send()
    for n in range(3):
        for stage in range(3):
            for copy in raw_copies(n, stage):
                copy.wait_send()
            for h in range(2):
                relay_copy(n, stage, h)[1].wait_send()


def rest_of_block(*args):
    scratch = []
    for lead, R, C in zip(LEADS, ROWS, COLUMNS):
        for dims in (
            (2, *lead, R, C),
            (2, 2, *lead, R, C),
            (2, 2, R, C),
            (2, 2, 2, R, C),
            (2, R, C // 2),
            (2, 2, R, C // 2),
            (2, 8, R, C),
        ):
            scratch.append(pltpu.VMEM(dims, BF16))
    T = CHIP_TOKENS
    return pl.pallas_call(
        rest_kernel,
        out_shape=(
            jax.ShapeDtypeStruct((256, D), BF16),
            jax.ShapeDtypeStruct((256, D), F32),
            jax.ShapeDtypeStruct((128, FF), F32),
            jax.ShapeDtypeStruct((512, D), F32),
            jax.ShapeDtypeStruct((128, 3 * D), F32),
            jax.ShapeDtypeStruct((128, D), F32),
            jax.ShapeDtypeStruct((16, 128), F32),
        ),
        in_specs=[HBM] * 9 + [VMEM] * 4,
        out_specs=(VMEM, VMEM, HBM, HBM, HBM, HBM, VMEM),
        scratch_shapes=[
            *[pltpu.VMEM((T, D), BF16)] * 4,
            *[pltpu.VMEM((T, D), F32)] * 2,
            pltpu.VMEM((8, D), F32),
            pltpu.VMEM((8, 16, 128), F32),
            pltpu.VMEM((8, 16, 128), F32),
            pltpu.VMEM((16, 16, 128), F32),
            *[pltpu.VMEM((2, 256, D), BF16)] * 2,
            *[pltpu.VMEM((4, 2, 2, 4, R, C), BF16) for R, C in zip(ROWS, COLUMNS)],
            *scratch,
            pltpu.SemaphoreType.DMA((79,)),
            pltpu.SemaphoreType.DMA((79,)),
            pltpu.SemaphoreType.DMA((16,)),
            pltpu.SemaphoreType.DMA((23,)),
            pltpu.SemaphoreType.DMA((23,)),
        ],
        compiler_params=pltpu.CompilerParams(
            collective_id=2, has_side_effects=True, vmem_limit_bytes=62 * MIB
        ),
    )(*args)


def turn(values, tables, sign):
    cosine, ahead, behind = tables
    moved = pltpu.roll(values, 120, 1) * ahead + pltpu.roll(values, 8, 1) * behind
    return values * cosine + sign * moved


def front_kernel(x, ct, wq, wd, vectors, bias, tables, packed, attn_out, mlp_out):
    values = x[...].astype(F32)
    centered = values - jnp.mean(values, axis=-1, keepdims=True)
    variance = jnp.mean(centered * centered, axis=-1, keepdims=True)
    normed = centered * lax.rsqrt(variance + epsilon)
    attn_out[...] = (normed * vectors[0:1, :] + vectors[1:2, :]).astype(BF16)
    mlp_out[...] = (normed * vectors[2:3, :] + vectors[3:4, :]).astype(BF16)
    low = lax.broadcasted_iota(jnp.int32, (CHIP_TOKENS, 128), 1) < HEAD
    rotary = (tables[0], tables[1], tables[2])
    for pair in range(4):
        a = attn_out[...]
        qk = slice(pair * 256, pair * 256 + 256)
        vs = slice(1024 + pair * 128, 1024 + pair * 128 + 128)
        projected = jnp.dot(a, wq[:, qk], preferred_element_type=F32) + bias[0:1, qk]
        for j in range(2):
            turned = turn(projected[:, j * 128 : j * 128 + 128], rotary, 1.0)
            packed[2 * pair + j, :, 0:128] = turned.astype(BF16)
        v = jnp.dot(a, wq[:, vs], preferred_element_type=F32) + bias[0:1, vs]
        rows = slice(pair * 128, pair * 128 + 128)
        d = lax.dot_general(ct[...], wd[rows, :], NT, preferred_element_type=F32)
        packed[2 * pair, :, 128:256] = jnp.where(low, v, pltpu.roll(d, 64, 1)).astype(BF16)
        packed[2 * pair + 1, :, 128:256] = jnp.where(low, pltpu.roll(v, 64, 1), d).astype(BF16)


def front(x, ct, wq, wd, vectors, bias, tables):
    T = CHIP_TOKENS
    return pl.pallas_call(
        front_kernel,
        out_shape=(
            jax.ShapeDtypeStruct((8, T, 256), BF16),
            jax.ShapeDtypeStruct((T, D), BF16),
            jax.ShapeDtypeStruct((T, D), BF16),
        ),
        in_specs=[VMEM] * 7,
        out_specs=(VMEM,) * 3,
        compiler_params=pltpu.CompilerParams(vmem_limit_bytes=48 * MIB),
    )(x, ct, wq, wd, vectors, bias, tables)


def rotary_tables(first_position):
    half = ROT // 2
    frequency = 10000.0 ** (-2.0 * jnp.arange(half, dtype=F32) / ROT)
    positions = first_position + jnp.arange(CHIP_TOKENS, dtype=jnp.int32)
    angles = positions.astype(F32)[:, None] * frequency[None, :]
    cosine, sine = jnp.cos(angles), jnp.sin(angles)
    rest = HEAD - ROT
    one = jnp.ones((CHIP_TOKENS, rest), F32)
    zero = jnp.zeros((CHIP_TOKENS, rest), F32)
    none = jnp.zeros((CHIP_TOKENS, half), F32)
    rows = [
        jnp.concatenate([cosine, cosine, one] * 2, axis=1),
        jnp.concatenate([-sine, none, zero] * 2, axis=1),
        jnp.concatenate([none, sine, zero] * 2, axis=1),
    ]
    return jnp.stack(rows)


def local(
    inputs,
    cotangent,
    ln_attn_gain,
    ln_attn_bias,
    ln_mlp_gain,
    ln_mlp_bias,
    qkv_weight,
    qkv_bias,
    dense_weight,
    dense_bias,
    hidden_weight,
    hidden_bias,
    output_weight,
    output_bias,
):
    seq = lax.axis_index("seq")
    core = seq % 2
    small = jnp.concatenate(
        [
            ln_attn_gain.reshape(1, 128),
            ln_attn_bias.reshape(1, 128),
            ln_mlp_gain.reshape(1, 128),
            ln_mlp_bias.reshape(1, 128),
            qkv_bias.reshape(3, 128),
            dense_bias.reshape(1, 128),
            hidden_bias.reshape(4, 128),
            output_bias.reshape(1, 128),
            jnp.zeros((3, 128), BF16),
        ]
    )
    own_qkv = lax.dynamic_index_in_dim(
        qkv_weight.reshape(128, 8, 2, 192), core, axis=2, keepdims=False
    )
    own_qkv = jnp.concatenate(
        [own_qkv[:, :, :128].reshape(128, 1024), own_qkv[:, :, 128:].reshape(128, 512)], axis=1
    )
    own_hidden = lax.dynamic_index_in_dim(
        hidden_weight.reshape(128, 8, 2, 256), core, axis=2, keepdims=False
    ).reshape(128, 2048)
    wq, wd, vectors, x, ct = gather(own_qkv, dense_weight, small, inputs, cotangent)
    wq = wq.reshape(D, 1536)
    wd = wd.reshape(512, D)
    x = x.reshape(CHIP_TOKENS, D)
    ct = ct.reshape(CHIP_TOKENS, D)
    vectors = vectors.astype(F32)
    norms = vectors[:, 0:4].transpose(1, 0, 2).reshape(4, D)
    head_bias = lax.dynamic_index_in_dim(
        vectors[:, 4:7].reshape(8, 2, 192), core, axis=1, keepdims=False
    )
    head_bias = jnp.concatenate(
        [head_bias[:, :128].reshape(1, 1024), head_bias[:, 128:].reshape(1, 512)], axis=1
    )
    out_bias = (vectors[:, 7] + vectors[:, 12]).reshape(1, D)
    unit_bias = lax.dynamic_index_in_dim(
        vectors[:, 8:12].reshape(8, 2, 256), core, axis=1, keepdims=False
    ).reshape(1, 2048)

    tables = rotary_tables((seq // 2) * CHIP_TOKENS)
    packed, attn_normed, mlp_normed = front(x, ct, wq, wd, norms, head_bias, tables)
    tokens, wh, wo = attention(packed, own_hidden, output_weight)
    wh = wh.reshape(D, 2048)
    wo = wo.reshape(2048, D)
    outputs, input_grad, hidden_total, output_total, qkv_total, dense_total, sums = rest_of_block(
        tokens, x, ct, attn_normed, mlp_normed, wq, wd, wh, wo, norms, unit_bias, out_bias, tables
    )
    head_bias_total = jnp.concatenate([sums[4], sums[6, :64], sums[5], sums[6, 64:]])
    return (
        outputs,
        input_grad,
        sums[0],
        sums[1],
        sums[2],
        sums[3],
        qkv_total,
        head_bias_total,
        dense_total,
        sums[7],
        hidden_total,
        sums[8:12].reshape(512),
        output_total,
        sums[7],
    )


def solution(mesh):
    rows = P(("fsdp", "seq"), None)
    vector = P("fsdp")
    matrix = P("fsdp", None)
    shared = (vector,) * 4 + (matrix, vector) * 4
    return jax.shard_map(
        local,
        mesh=mesh,
        in_specs=(rows, rows, *shared),
        out_specs=(rows, rows, *shared),
        check_vma=False,
    )
```

```python
import functools
import math

import jax
import jax.numpy as jnp
import numpy as np
from jax import lax
from jax.experimental import pallas as pl
from jax.experimental.pallas import tpu as pltpu
from jax.sharding import PartitionSpec as P

D = 1024
FF = 4096
HEADS = 16
HEAD = 64
ROT = 16
CHIP_TOKENS = 512
FSDP = 8
CHIPS = 8

epsilon = 1e-05
F32 = jnp.float32
BF16 = jnp.bfloat16
NT = (((1,), (1,)), ((), ()))
TN = (((0,), (0,)), ((), ()))
MIB = 2**20
HBM = pl.BlockSpec(memory_space=pl.ANY)
VMEM = pl.BlockSpec(memory_space=pltpu.VMEM)


def place():
    f = lax.axis_index("fsdp")
    s = lax.axis_index("seq")
    return f, s, (f // 2, f % 2, s // 4, (s // 2) % 2, s % 2)


def device(y, z, x, core):
    return {"fsdp": y * 2 + z % 2, "seq": x * 4 + (z // 2) * 2 + core}


def barrier(devices):
    sem = pltpu.get_barrier_semaphore()
    for d in devices:
        pl.semaphore_signal(sem, inc=1, device_id=d, device_id_type=pl.DeviceIdType.MESH)
    pl.semaphore_wait(sem, len(devices))


def remote(src, dst, send, recv, target):
    return pltpu.make_async_remote_copy(
        src_ref=src,
        dst_ref=dst,
        send_sem=send,
        recv_sem=recv,
        device_id=target,
        device_id_type=pl.DeviceIdType.MESH,
    )


class Gather:
    def __init__(self, own, full, send, recv):
        f, s, (y, zl, px, zh, core) = place()
        z = zh * 2 + zl
        self.own, self.full, self.send, self.recv = own, full, send, recv
        self.yp = device((y + 1) % 4, z, px, core)
        self.ym = device((y + 3) % 4, z, px, core)
        self.zp = device(y, (z + 1) % 4, px, core)
        self.zm = device(y, (z + 3) % 4, px, core)
        self.f = f
        self.slots = [f, (f + 6) % 8, (f + 2) % 8, (f + 4) % 8]
        flip = f + 1 - 2 * zl
        self.far = [flip, (flip + 6) % 8, (flip + 2) % 8, (flip + 4) % 8]
        self.sends = []

    def neighbours(self):
        return [self.yp, self.ym, self.zp, self.zm]

    def started(self, src, dst, k, target):
        copy = remote(src, dst, self.send.at[k], self.recv.at[k], target)
        copy.start()
        self.sends.append(copy)

    def arrived(self, ref, k):
        remote(ref, ref, self.send.at[k], self.recv.at[k], self.yp).wait_recv()

    @staticmethod
    def part(ref, h):
        rows = ref.shape[0] // 2
        return ref.at[pl.ds(h * rows, rows)]

    def own_y(self):
        for n, (o, g) in enumerate(zip(self.own, self.full)):
            for k, h, target in ((0, 0, self.yp), (3, 1, self.ym), (2, 0, self.ym), (1, 1, self.yp)):
                self.started(self.part(o, h), self.part(g.at[self.f], h), 14 * n + k, target)

    def own_z(self):
        for n, (o, g) in enumerate(zip(self.own, self.full)):
            for k, h, target in ((6, 0, self.zp), (10, 1, self.zm)):
                self.started(self.part(o, h), self.part(g.at[self.f], h), 14 * n + k, target)

    def pass_on(self, n, k, slot, h, targets):
        ref = self.part(self.full[n].at[slot], h)
        self.arrived(ref, 14 * n + k)
        for kk, target in targets:
            self.started(ref, ref, 14 * n + kk, target)

    def near_y(self):
        for n in range(len(self.full)):
            self.pass_on(n, 0, self.slots[1], 0, [(4, self.yp)])
            self.pass_on(n, 3, self.slots[2], 1, [(5, self.ym)])

    def near_z(self):
        for n, g in enumerate(self.full):
            for k, slot, h, target in ((7, 1, 0, self.zp), (12, 2, 1, self.zm)):
                ref = self.part(g.at[self.slots[slot]], h)
                self.started(ref, ref, 14 * n + k, target)
            self.pass_on(n, 2, self.slots[2], 0, [(8, self.zp)])
            self.pass_on(n, 1, self.slots[1], 1, [(11, self.zm)])

    def opposite(self):
        for n in range(len(self.full)):
            self.pass_on(n, 4, self.slots[3], 0, [(9, self.zp)])
            self.pass_on(n, 5, self.slots[3], 1, [(13, self.zm)])

    def finish(self):
        for n, g in enumerate(self.full):
            for j in range(4):
                self.arrived(self.part(g.at[self.far[j]], 0), 14 * n + 6 + j)
                self.arrived(self.part(g.at[self.far[j]], 1), 14 * n + 10 + j)
        for copy in self.sends:
            copy.wait_send()


def fold(op, a):
    result = a[:, :128]
    for j in range(128, a.shape[1], 128):
        result = op(result, a[:, j : j + 128])
    return result


def attention_kernel(
    qkv_w, dense_w, hidden_w, output_w, small, x, ct, cosine, sine,
    result, gh, go, wq_out, wd_out, x_out, ct_out, an_out, mn_out, vectors,
    raw_q, own_q, own_h, own_o, wq, wd, x_v, ct_v, an, mn, vec, norms, bias, tables, packed,
    hd, out, q_s, k_s, v_s, d_s, s_s, p_s, dk_s, dv_s, mx_s, l_s, o_s, dq_s,
    in_send, in_recv, out_send, out_recv, a_send, a_recv, g_send, g_recv, local_sem,
):
    f, s, (y, zl, px, zh, core) = place()
    me = s // 2
    B = CHIP_TOKENS
    n = CHIPS
    scale = 1.0 / math.sqrt(HEAD)
    sibling = device(y, zh * 2 + zl, px, 1 - core)
    others = [{"fsdp": (f + k) % 8, "seq": s} for k in range(1, 8)]
    zother = device(y, 2 * (1 - zh) + 1 - zl, px, core)

    def chip(j):
        return {"fsdp": f, "seq": j * 2 + core}

    greeted = others + [sibling, zother] + [chip((me + k) % n) for k in range(1, n)]
    entered = pltpu.get_barrier_semaphore()
    for d in greeted:
        pl.semaphore_signal(entered, inc=1, device_id=d, device_id_type=pl.DeviceIdType.MESH)

    def load(src, dst, k):
        copy = pltpu.make_async_copy(src, dst, local_sem.at[k])
        copy.start()
        return copy

    own_d = dense_w.at[pl.ds(pl.multiple_of(core * 64, 64), 64)]
    here = pl.ds(pl.multiple_of(me * B, B), B)
    load_q = load(qkv_w, raw_q, 0)
    loads = [
        load(own_d, wd.at[f], 1),
        load(x, x_v.at[core], 2),
        load(ct, ct_v.at[core], 3),
        load(small, vec.at[f], 4),
        load(cosine.at[here], tables.at[0], 5),
        load(sine.at[here], tables.at[1], 6),
    ]
    load_o = load(output_w.at[pl.ds(pl.multiple_of(core * 256, 256), 256)], own_o, 7)
    load_h = [
        load(
            hidden_w.at[:, pl.ds(pl.multiple_of(r * 512 + core * 256, 256), 256)],
            own_h.at[:, pl.ds(r * 256, 256)],
            8 + r,
        )
        for r in range(8)
    ]
    load_q.wait()
    low = lax.broadcasted_iota(jnp.int32, (128, 128), 1) < HEAD
    even = core == 0
    held = None
    for r in range(8):
        t0, t1, t2 = [raw_q[:, r * 384 + j * 128 : r * 384 + j * 128 + 128].astype(F32) for j in range(3)]
        t2 = pltpu.roll(t2, 64, 1)
        qk = jnp.where(even, t0, jnp.where(low, pltpu.roll(t1, 64, 1), t2))
        v = jnp.where(even, t1, t2)
        own_q[:, r * 128 : r * 128 + 128] = qk.astype(BF16)
        if r % 2 == 0:
            held = v
        else:
            at = 1024 + r // 2 * 128
            own_q[:, at : at + 128] = jnp.where(low, held, pltpu.roll(v, 64, 1)).astype(BF16)
    pl.semaphore_wait(entered, len(greeted))

    heads = Gather([own_q, own_d], [wq, wd], a_send, a_recv)
    units = Gather([own_h, own_o], [gh, go], g_send, g_recv)
    heads.own_y()
    heads.started(x, x_v.at[core], 28, sibling)
    heads.started(ct, ct_v.at[core], 29, sibling)
    for k in range(1, 8):
        heads.started(small, vec.at[f], 29 + k, others[k - 1])
    heads.own_z()
    wq[f] = own_q[...]

    for copy in loads:
        copy.wait()
    heads.arrived(x_v.at[1 - core], 28)
    for k in range(1, 8):
        heads.arrived(vec.at[(f + 8 - k) % 8], 29 + k)
    heads.near_y()
    for r in range(8):
        at = slice(r * 128, r * 128 + 128)
        norms[0:4, at] = vec[r, 0:4, :]
        bias[0:1, at] = vec[r, pl.ds(4 + core, 1), :]
    first = low[0:1, :]
    for pair in range(4):
        a, b = vec[2 * pair, 6:7, :], vec[2 * pair + 1, 6:7, :]
        v_even = jnp.where(first, a, pltpu.roll(b, 64, 1))
        v_odd = jnp.where(first, pltpu.roll(a, 64, 1), b)
        at = slice(1024 + pair * 128, 1152 + pair * 128)
        bias[0:1, at] = jnp.where(even, v_even, v_odd)
    for c in range(2):
        rows = slice(c * 256, c * 256 + 256)
        normed, _ = normalised(x_v[c])
        an[rows, :] = (normed * norms[0:1, :] + norms[1:2, :]).astype(BF16)
        mn[rows, :] = (normed * norms[2:3, :] + norms[3:4, :]).astype(BF16)
        if c == 0:
            heads.near_z()
    heads.opposite()
    heads.arrived(ct_v.at[1 - core], 29)
    load_o.wait()
    for copy in load_h:
        copy.wait()
    units.own_y()
    heads.finish()

    def given(j):
        return remote(packed.at[j], hd.at[me], in_send.at[j], in_recv.at[me], chip(j))

    wide = lax.broadcasted_iota(jnp.int32, (B, 128), 1) < HEAD
    rotary = (tables[0], tables[1])
    tokens = ct_v[...].reshape(B, D)
    for pair in range(4):
        a = an[...]
        qk = slice(pair * 256, pair * 256 + 256)
        vs = slice(1024 + pair * 128, 1024 + pair * 128 + 128)
        weight = wq[:, :, qk].reshape(D, 256)
        projected = jnp.dot(a, weight, preferred_element_type=F32) + bias[0:1, qk]
        for j in range(2):
            turned = turn(projected[:, j * 128 : j * 128 + 128], rotary, 1.0)
            packed[2 * pair + j, :, 0:128] = turned.astype(BF16)
        weight = wq[:, :, vs].reshape(D, 128)
        v = jnp.dot(a, weight, preferred_element_type=F32) + bias[0:1, vs]
        weight = wd[2 * pair : 2 * pair + 2].reshape(128, D)
        d = lax.dot_general(tokens, weight, NT, preferred_element_type=F32)
        packed[2 * pair, :, 128:256] = jnp.where(wide, v, pltpu.roll(d, 64, 1)).astype(BF16)
        packed[2 * pair + 1, :, 128:256] = jnp.where(wide, pltpu.roll(v, 64, 1), d).astype(BF16)
        for j in (2 * pair, 2 * pair + 1):

            @pl.when(me != j)
            def _():
                given(j).start()

    hd[me] = packed[me]
    units.near_y()
    saves = [
        load(a, b, 16 + k)
        for k, (a, b) in enumerate(
            [
                (own_h, gh.at[f]),
                (own_o, go.at[f]),
                (wq, wq_out),
                (wd, wd_out),
                (x_v, x_out),
                (ct_v, ct_out),
                (an, an_out),
                (mn, mn_out),
                (vec, vectors),
            ]
        )
    ]
    for k in range(1, n):
        j = (me + n - k) % n
        remote(hd.at[j], hd.at[j], in_send.at[j], in_recv.at[j], chip(j)).wait_recv()
    units.own_z()
    units.near_z()

    def block(i):
        return pl.ds(pl.multiple_of(i * B, B), B)

    def prepare(i, _):
        rows = block(i)
        piece = hd[i]
        q_s[rows, :] = piece[:, 0:64] * jnp.asarray(scale, BF16)
        k_s[rows, :] = piece[:, 64:128]
        v_s[rows, :] = piece[:, 128:192]
        d_s[rows, :] = piece[:, 192:256]
        return 0

    lax.fori_loop(0, n, prepare, 0)
    dk_s[...] = jnp.zeros_like(dk_s)
    dv_s[...] = jnp.zeros_like(dv_s)
    keep = lax.broadcasted_iota(jnp.int32, (B, B), 1) <= lax.broadcasted_iota(
        jnp.int32, (B, B), 0
    )

    def back_to(i):
        return remote(out.at[i], result.at[me], out_send.at[i], out_recv.at[me], chip(i))

    def query_block(t, _):
        i = n - 1 - t
        rows = block(i)
        qi = q_s[rows, :]
        mx_s[...] = jnp.full(mx_s.shape, -1e30, F32)

        def score(kb):
            return lax.dot_general(qi, k_s[block(kb), :], NT, preferred_element_type=F32)

        def first(kb, _):
            scores = score(kb)
            s_s[kb] = scores
            mx_s[...] = jnp.maximum(mx_s[...], fold(jnp.maximum, scores))
            return 0

        lax.fori_loop(0, i, first, 0)
        scores = jnp.where(keep, score(i), -1e30)
        s_s[i] = scores
        row_max = jnp.max(
            jnp.maximum(mx_s[...], fold(jnp.maximum, scores)), axis=1, keepdims=True
        )
        l_s[...] = jnp.zeros_like(l_s)
        o_s[...] = jnp.zeros_like(o_s)
        dq_s[...] = jnp.zeros_like(dq_s)

        def second(kb, _):
            p = jnp.exp(s_s[kb] - row_max)
            l_s[...] += fold(jnp.add, p)
            pb = p.astype(BF16)
            p_s[kb] = pb
            o_s[...] += jnp.dot(pb, v_s[block(kb), :], preferred_element_type=F32)
            return 0

        lax.fori_loop(0, i + 1, second, 0)
        inverse = 1.0 / jnp.sum(l_s[...], axis=1, keepdims=True)
        o = o_s[...] * inverse
        d = (d_s[rows, :].astype(F32) * inverse).astype(BF16)
        delta = jnp.sum(o * d.astype(F32), axis=1, keepdims=True)
        q_t = qi.T
        d_t = d.T

        def third(kb, _):
            cols = block(kb)
            pb = p_s[kb]
            dp = lax.dot_general(d, v_s[cols, :], NT, preferred_element_type=F32)
            ds = (pb.astype(F32) * (dp - delta)).astype(BF16)
            dq_s[...] += jnp.dot(ds, k_s[cols, :], preferred_element_type=F32)
            dk_s[:, cols] += jnp.dot(q_t, ds, preferred_element_type=F32)
            dv_s[:, cols] += jnp.dot(d_t, pb, preferred_element_type=F32)
            return 0

        lax.fori_loop(0, i + 1, third, 0)
        out[i, :, 0:64] = (dq_s[...] * scale).astype(BF16)
        out[i, :, 64:128] = dk_s[:, rows].T.astype(BF16)
        out[i, :, 128:192] = dv_s[:, rows].T.astype(BF16)
        out[i, :, 192:256] = o.astype(BF16)

        @pl.when(i != me)
        def _():
            back_to(i).start()

        @pl.when(i == me)
        def _():
            pltpu.make_async_copy(out.at[i], result.at[i], local_sem.at[25]).start()

        return 0

    lax.fori_loop(0, 1, query_block, 0)
    units.opposite()
    lax.fori_loop(1, n, query_block, 0)

    for k in range(1, n):
        given((me + k) % n).wait_send()
    for copy in saves:
        copy.wait()
    units.finish()
    for k in range(1, n):
        back_to((me + k) % n).wait_send()
    pltpu.make_async_copy(out.at[me], result.at[me], local_sem.at[25]).wait()
    for k in range(1, n):
        j = (me + k) % n
        ref = result.at[j]
        remote(ref, ref, out_send.at[j], out_recv.at[j], chip(me)).wait_recv()


def attention(*args):
    B = CHIP_TOKENS
    L = CHIPS * B

    def shape(*dims):
        return jax.ShapeDtypeStruct(dims, BF16)

    return pl.pallas_call(
        attention_kernel,
        out_shape=(
            shape(CHIPS, B, 4 * HEAD),
            shape(8, 128, 2048),
            shape(8, 256, 1024),
            shape(8, 128, 1536),
            shape(8, 64, 1024),
            shape(2, 256, D),
            shape(2, 256, D),
            shape(B, D),
            shape(B, D),
            jax.ShapeDtypeStruct((8, 16, 128), F32),
        ),
        in_specs=[HBM] * 9,
        out_specs=(HBM,) * 10,
        scratch_shapes=[
            pltpu.VMEM((128, 3072), BF16),
            pltpu.VMEM((128, 1536), BF16),
            pltpu.VMEM((128, 2048), BF16),
            pltpu.VMEM((256, 1024), BF16),
            pltpu.VMEM((8, 128, 1536), BF16),
            pltpu.VMEM((8, 64, 1024), BF16),
            *[pltpu.VMEM((2, 256, D), BF16)] * 2,
            *[pltpu.VMEM((B, D), BF16)] * 2,
            pltpu.VMEM((8, 16, 128), F32),
            pltpu.VMEM((8, D), F32),
            pltpu.VMEM((8, 1536), F32),
            pltpu.VMEM((2, B, 128), F32),
            *[pltpu.VMEM((CHIPS, B, 4 * HEAD), BF16)] * 3,
            *[pltpu.VMEM((L, HEAD), BF16)] * 4,
            pltpu.VMEM((L // B, B, B), F32),
            pltpu.VMEM((L // B, B, B), BF16),
            *[pltpu.VMEM((HEAD, L), F32)] * 2,
            *[pltpu.VMEM((B, 128), F32)] * 2,
            *[pltpu.VMEM((B, HEAD), F32)] * 2,
            *[pltpu.SemaphoreType.DMA((CHIPS,))] * 4,
            *[pltpu.SemaphoreType.DMA((37,))] * 2,
            *[pltpu.SemaphoreType.DMA((28,))] * 2,
            pltpu.SemaphoreType.DMA((26,)),
        ],
        compiler_params=pltpu.CompilerParams(
            collective_id=1, has_side_effects=True, vmem_limit_bytes=60 * MIB
        ),
    )(*args)


ORDERS = ("yzx", "zxy", "xyz")
LEADS = ((2, 4), (2, 4), (4, 2))
ROWS = (16, 32, 16)
COLUMNS = (2048, 1024, 2048)


def chunk(n, stage, g, t, h, where):
    y, zl, zh, px = where
    if stage == 0:
        if n == 0:
            return g.at[t, h]
        if n == 1:
            return g.at[pl.ds(2 * h, 2), t % 2, t // 2]
        return g.at[:, h, :, t]
    if stage == 1:
        if n == 0:
            return g.at[y, t % 2, t // 2, pl.ds(2 * h, 2)]
        if n == 1:
            return g.at[pl.ds(2 * h, 2), zl, zh, t]
        return g.at[t, h, :, px]
    half = g.shape[-1] // 2
    columns = pl.ds(h * half, half)
    if n == 0:
        return g.at[y, zl, zh, t, :, columns]
    if n == 1:
        return g.at[t, zl, zh, px, :, columns]
    return g.at[y, t % 2, t // 2, px, :, columns]


def add_into(dst, terms):
    lead = tuple(dst.shape[:-2])

    def body(k, _):
        at = []
        for extent in reversed(lead):
            at.insert(0, k % extent)
            k = k // extent
        at = (*at, slice(None), slice(None))
        total = dst[at].astype(F32)
        for t in terms:
            total = total + t[at].astype(F32)
        dst[at] = total.astype(BF16)
        return 0

    lax.fori_loop(0, math.prod(lead), body, 0)


def normalised(values):
    values = values.astype(F32)
    centered = values - jnp.mean(values, axis=-1, keepdims=True)
    variance = jnp.mean(centered * centered, axis=-1, keepdims=True)
    scale = lax.rsqrt(variance + epsilon)
    return centered * scale, scale


def rest_kernel(
    tokens, x, ct, an, mn, wq, wd, wh, wo, vec, cosine, sine,
    outputs, input_grad, gathered0, gathered1, gathered2, small_out,
    tables, norms, unit_bias, x_v, ct_v, an_v, mn_v, branches, weighted, sums, small, sm_a, sm_b, pair_send, pair_recv,
    g0, g1, g2, *rest,
):
    grads = (g0, g1, g2)
    gathered = (gathered0, gathered1, gathered2)
    bufs = [(*rest[6 * n : 6 * n + 6], gathered[n]) for n in range(3)]
    send, recv, local_sem, sm_send, sm_recv = rest[18:]
    f, s, (y, zl, px, zh, core) = place()
    z = zh * 2 + zl
    coordinate = {"y": y, "z": z, "x": px}
    where = (y, zl, zh, px)
    T = CHIP_TOKENS

    def along(axis, step):
        t = dict(coordinate)
        t[axis] = (t[axis] + step) % 4
        return device(t["y"], t["z"], t["x"], core)

    plus = {a: along(a, 1) for a in "yzx"}
    minus = {a: along(a, 3) for a in "yzx"}
    same_seq = [{"fsdp": (f + k) % 8, "seq": s} for k in range(1, 8)]
    same_fsdp = [{"fsdp": f, "seq": (s + k) % 16} for k in range(1, 16)]
    zother = device(y, 2 * (1 - zh) + 1 - zl, px, core)
    sibling = device(y, z, px, 1 - core)
    sends = []

    def load(src, dst, k):
        copy = pltpu.make_async_copy(src, dst, local_sem.at[k])
        copy.start()
        return copy

    def started(src, dst, k, target):
        copy = remote(src, dst, send.at[k], recv.at[k], target)
        copy.start()
        sends.append(copy)

    def arrived(ref, k):
        remote(ref, ref, send.at[k], recv.at[k], sibling).wait_recv()

    def small_sent(src, dst, k, target):
        copy = remote(src, dst, sm_send.at[k], sm_recv.at[k], target)
        copy.start()
        sends.append(copy)

    def small_arrived(ref, k):
        remote(ref, ref, sm_send.at[k], sm_recv.at[k], sibling).wait_recv()

    def buffers(n, stage):
        return bufs[n][2 * stage], bufs[n][2 * stage + 1]

    def raw_copies(n, stage):
        axis = ORDERS[n][stage]
        p = coordinate[axis]
        opp, fin = buffers(n, stage)
        b = 26 * n + 6 * stage

        def copy(t, h, dst, k, target):
            src = chunk(n, stage, grads[n], t % 4, h, where)
            return remote(src, dst, send.at[k], recv.at[k], target)

        return [
            copy(p + 2, 0, opp.at[0], b, plus[axis]),
            copy(p + 2, 1, opp.at[1], b + 1, minus[axis]),
            copy(p + 1, 1, fin.at[0, 1], b + 2, plus[axis]),
            copy(p + 3, 0, fin.at[1, 0], b + 3, minus[axis]),
        ]

    def relay_copy(n, stage, h):
        axis = ORDERS[n][stage]
        _, fin = buffers(n, stage)
        k = 26 * n + 6 * stage + 4 + h
        t = coordinate[axis] + 1 + 2 * h
        src = chunk(n, stage, grads[n], t % 4, h, where)
        target = (plus, minus)[h][axis]
        return src, remote(src, fin.at[h, h], send.at[k], recv.at[k], target)

    def begin(n, stage):
        for copy in raw_copies(n, stage):
            copy.start()

    def relay(n, stage):
        opp, _ = buffers(n, stage)
        for h in range(2):
            mid, copy = relay_copy(n, stage, h)
            arrived(opp.at[h], 26 * n + 6 * stage + h)
            add_into(mid, [opp.at[h]])
            copy.start()

    def finish(n, stage):
        p = coordinate[ORDERS[n][stage]]
        _, fin = buffers(n, stage)
        b = 26 * n + 6 * stage
        arrived(fin.at[0, 1], b + 2)
        arrived(fin.at[1, 0], b + 3)
        arrived(fin.at[0, 0], b + 4)
        arrived(fin.at[1, 1], b + 5)
        for h in range(2):
            add_into(chunk(n, stage, grads[n], p, h, where), [fin.at[0, h], fin.at[1, h]])

    keeps = [load(a, b, k) for k, (a, b) in enumerate([(x, x_v), (ct, ct_v), (an, an_v), (mn, mn_v)])]
    barrier(same_seq + same_fsdp + [zother])
    small[...] = jnp.zeros_like(small)
    here = pl.ds(pl.multiple_of((px * 2 + zh) * T, T), T)
    keeps += [load(cosine.at[here], tables.at[0], 12), load(sine.at[here], tables.at[1], 13)]
    for r in range(8):
        at = slice(r * 128, r * 128 + 128)
        norms[0:4, at] = vec[r, 0:4, :]
        norms[4:5, at] = vec[r, 7:8, :] + vec[r, 12:13, :]
        for j in range(2):
            unit_bias[0:1, r * 256 + j * 128 : r * 256 + j * 128 + 128] = vec[
                r, pl.ds(8 + 2 * core + j, 1), :
            ]

    def attention_part(wq_v, wd_v, tk_v, pg_v, at_v, turned_v):
        loads = [load(a, b, 4 + k) for k, (a, b) in enumerate([(tokens, tk_v), (wq, wq_v), (wd, wd_v)])]
        for copy in keeps:
            copy.wait()
        loads[0].wait()
        low = lax.broadcasted_iota(jnp.int32, (T, 128), 1) < HEAD
        first = lax.broadcasted_iota(jnp.int32, (1, 128), 1) < HEAD
        rotary = (tables[0], tables[1])
        for pair in range(4):
            for j in range(2):
                r = 2 * pair + j
                at = slice(r * 128, r * 128 + 128)
                turned = turn(tk_v[r, :, 0:128].astype(F32), rotary, -1.0).astype(BF16)
                pg_v[:, at] = turned
                small[r, pl.ds(4 + core, 1), :] = jnp.sum(turned.astype(F32), axis=0, keepdims=True)
            a = tk_v[2 * pair, :, 128:256].astype(F32)
            b = tk_v[2 * pair + 1, :, 128:256].astype(F32)
            v = jnp.where(low, a, pltpu.roll(b, 64, 1))
            pg_v[:, 1024 + pair * 128 : 1152 + pair * 128] = v.astype(BF16)
            total = jnp.sum(v, axis=0, keepdims=True)
            moved = jnp.sum(jnp.where(low, pltpu.roll(v, 64, 1), pltpu.roll(v, 64, 1)), axis=0, keepdims=True)
            zero = jnp.zeros_like(total)
            at_low = (jnp.where(first, total, zero), jnp.where(first, moved, zero))
            at_high = (jnp.where(first, zero, moved), jnp.where(first, zero, total))
            for j in range(2):
                small[2 * pair + j, 6:7, :] = jnp.where(core == 0, at_low[j], at_high[j])
            o = jnp.where(low, pltpu.roll(a, 64, 1), b)
            at_v[:, pair * 128 : pair * 128 + 128] = o.astype(BF16)

        turned_v[...] = an_v[...].T

        def qkv_columns(k, _):
            at = pl.ds(pl.multiple_of(k * 512, 512), 512)
            part = jnp.dot(turned_v[...], pg_v[:, at], preferred_element_type=F32)
            g2[:, :, :, :, :, at] = part.astype(BF16).reshape(4, 2, 2, 4, 16, 512)
            return 0

        lax.fori_loop(0, 3, qkv_columns, 0)
        turned_v[0:512, :] = at_v[...].T
        for k in range(2):
            part = jnp.dot(
                turned_v[0:512, :], ct_v[:, k * 512 : k * 512 + 512], preferred_element_type=F32
            )
            g2[:, :, k, :, :, 1536:2048] = part.astype(BF16).reshape(4, 2, 4, 16, 512)
        begin(2, 0)
        loads[1].wait()
        loads[2].wait()
        grad = lax.dot_general(pg_v[...], wq_v[...], NT, preferred_element_type=F32)
        normed, _ = normalised(x_v[...])
        sums[0:1, :] = jnp.sum(grad * normed, axis=0, keepdims=True)
        sums[1:2, :] = jnp.sum(grad, axis=0, keepdims=True)
        weighted[...] = grad * norms[0:1, :]
        branches[...] = jnp.dot(at_v[...], wd_v[...], preferred_element_type=F32)

    pl.run_scoped(
        attention_part,
        pltpu.VMEM((D, 1536), BF16),
        pltpu.VMEM((512, D), BF16),
        pltpu.VMEM((8, T, 256), BF16),
        pltpu.VMEM((T, 1536), BF16),
        pltpu.VMEM((T, 512), BF16),
        pltpu.VMEM((D, T), BF16),
    )

    def unit_part(wh_v, wo_v, act_v, hg_v, turned_v):
        loads = [load(a, b, 7 + k) for k, (a, b) in enumerate([(wh, wh_v), (wo, wo_v)])]
        loads[0].wait()
        loads[1].wait()

        def units(r, _):
            at = pl.ds(pl.multiple_of(r * 256, 256), 256)
            h = jnp.dot(mn_v[...], wh_v[:, at], preferred_element_type=F32) + unit_bias[0:1, at]
            below = 0.5 + 0.5 * lax.erf(h * math.sqrt(0.5))
            density = jnp.exp(-0.5 * h * h) * (1.0 / math.sqrt(2.0 * math.pi))
            act_v[:, at] = (h * below).astype(BF16)
            up = lax.dot_general(ct_v[...], wo_v[at, :], NT, preferred_element_type=F32)
            grad = (up * (below + h * density)).astype(BF16)
            hg_v[:, at] = grad
            total = jnp.sum(grad.astype(F32), axis=0, keepdims=True)
            small[r, pl.ds(8 + 2 * core, 1), :] = total[:, 0:128]
            small[r, pl.ds(9 + 2 * core, 1), :] = total[:, 128:256]
            return 0

        lax.fori_loop(0, 8, units, 0)
        turned_v[...] = act_v[...].T

        def output_rows(k, _):
            at = pl.ds(pl.multiple_of(k * 512, 512), 512)
            part = jnp.dot(turned_v[at, :], ct_v[...], preferred_element_type=F32)
            g1[k] = part.astype(BF16).reshape(2, 2, 4, 32, 1024)
            return 0

        lax.fori_loop(0, 4, output_rows, 0)
        begin(1, 0)
        turned_v[0:D, :] = mn_v[...].T

        def hidden_columns(k, _):
            at = pl.ds(pl.multiple_of(k * 512, 512), 512)
            part = jnp.dot(turned_v[0:D, :], hg_v[:, at], preferred_element_type=F32)
            g0[:, :, :, :, :, at] = part.astype(BF16).reshape(4, 2, 2, 4, 16, 512)
            return 0

        lax.fori_loop(0, 4, hidden_columns, 0)
        begin(0, 0)
        relay(2, 0)
        grad = lax.dot_general(hg_v[...], wh_v[...], NT, preferred_element_type=F32)
        normed, _ = normalised(x_v[...])
        sums[2:3, :] = jnp.sum(grad * normed, axis=0, keepdims=True)
        sums[3:4, :] = jnp.sum(grad, axis=0, keepdims=True)
        weighted[...] += grad * norms[2:3, :]
        branches[...] += jnp.dot(act_v[...], wo_v[...], preferred_element_type=F32)

    pl.run_scoped(
        unit_part,
        pltpu.VMEM((D, 2048), BF16),
        pltpu.VMEM((2048, D), BF16),
        pltpu.VMEM((T, 2048), BF16),
        pltpu.VMEM((T, 2048), BF16),
        pltpu.VMEM((2048, T), BF16),
    )

    other = pl.ds(pl.multiple_of((1 - core) * 256, 256), 256)
    mine = pl.ds(pl.multiple_of(core * 256, 256), 256)
    pair_send[0] = branches[other, :].astype(BF16)
    pair_send[1] = weighted[other, :].astype(BF16)
    started(pair_send, pair_recv, 78, sibling)
    sums[4:5, :] = jnp.sum(ct_v[mine, :].astype(F32), axis=0, keepdims=True)
    for r in range(8):
        at = slice(r * 128, r * 128 + 128)
        small[r, 0:4, :] = sums[0:4, at]
        small[r, 7:8, :] = sums[4:5, at]
    for k in range(1, 8):
        small_sent(small.at[(f + k) % 8], sm_a.at[k], k, same_seq[k - 1])
    relay(1, 0)
    relay(0, 0)
    arrived(pair_recv, 78)
    normed, scale = normalised(x_v[mine, :])
    total = x_v[mine, :].astype(F32) + branches[mine, :] + pair_recv[0].astype(F32) + norms[4:5, :]
    outputs[...] = total.astype(BF16)
    w = weighted[mine, :] + pair_recv[1].astype(F32)
    input_grad[...] = ct_v[mine, :].astype(F32) + scale * (
        w
        - jnp.mean(w, axis=-1, keepdims=True)
        - normed * jnp.mean(w * normed, axis=-1, keepdims=True)
    )
    finish(2, 0)
    begin(2, 1)
    for k in range(1, 8):
        small_arrived(sm_a.at[k], k)
    total = small[f]
    for k in range(1, 8):
        total = total + sm_a[k]
    sm_b[0] = total
    for k in range(1, 16):
        small_sent(sm_b.at[0], sm_b.at[k], 7 + k, same_fsdp[k - 1])
    finish(1, 0)
    begin(1, 1)
    finish(0, 0)
    begin(0, 1)

    across = device(y, (z + 2) % 4, px, core)
    xp, xm = plus["x"], minus["x"]

    def at_chip(n, zz, xx):
        return bufs[n][6].at[core, zz * 4 + xx % 4]

    def spread(n):
        b = 26 * n + 18
        done = grads[n].at[y, zl, zh, px]
        place_ = at_chip(n, zh, px)
        keep = pltpu.make_async_copy(done, place_, local_sem.at[9 + n])
        keep.start()
        started(done, place_, b, across)
        started(done, place_, b + 1, xp)
        started(done, place_, b + 2, xm)
        return keep

    def spread_on(n):
        b = 26 * n + 18
        theirs = at_chip(n, 1 - zh, px)
        arrived(theirs, b)
        started(theirs, theirs, b + 3, xp)
        started(theirs, theirs, b + 4, xm)
        left, right = at_chip(n, zh, px + 3), at_chip(n, 1 - zh, px + 1)
        arrived(left, b + 1)
        started(left, left, b + 5, xp)
        arrived(right, b + 4)
        started(right, right, b + 6, xm)

    def spread_end(n, keep):
        b = 26 * n + 18
        arrived(at_chip(n, zh, px + 1), b + 2)
        arrived(at_chip(n, 1 - zh, px + 3), b + 3)
        arrived(at_chip(n, zh, px + 2), b + 5)
        arrived(at_chip(n, 1 - zh, px + 2), b + 6)
        keep.wait()
        whole = bufs[n][6].at[core]
        started(whole, whole, b + 7, sibling)

    order = (2, 1, 0)
    for n in order:
        relay(n, 1)
    for n in order:
        finish(n, 1)
        begin(n, 2)
    for n in order:
        relay(n, 2)
    copies = {}
    for n in order:
        finish(n, 2)
        copies[n] = spread(n)
    for n in order:
        spread_on(n)
    for n in order:
        spread_end(n, copies[n])
    for k in range(1, 16):
        small_arrived(sm_b.at[k], 7 + k)
    total = sm_b[0]
    for k in range(1, 16):
        total = total + sm_b[k]
    small_out[...] = total

    for n in order:
        arrived(gathered[n].at[1 - core], 26 * n + 25)
    for copy in sends:
        copy.wait_send()
    for n in range(3):
        for stage in range(3):
            for copy in raw_copies(n, stage):
                copy.wait_send()
            for h in range(2):
                relay_copy(n, stage, h)[1].wait_send()


def rest_of_block(*args):
    scratch = []
    for lead, R, C in zip(LEADS, ROWS, COLUMNS):
        for dims in (
            (2, *lead, R, C),
            (2, 2, *lead, R, C),
            (2, 2, R, C),
            (2, 2, 2, R, C),
            (2, R, C // 2),
            (2, 2, R, C // 2),
        ):
            scratch.append(pltpu.VMEM(dims, BF16))
    T = CHIP_TOKENS
    return pl.pallas_call(
        rest_kernel,
        out_shape=(
            jax.ShapeDtypeStruct((256, D), BF16),
            jax.ShapeDtypeStruct((256, D), F32),
            *[jax.ShapeDtypeStruct((2, 8, R, C), BF16) for R, C in zip(ROWS, COLUMNS)],
            jax.ShapeDtypeStruct((16, 128), F32),
        ),
        in_specs=[HBM] * 9 + [VMEM, HBM, HBM],
        out_specs=(VMEM, VMEM, HBM, HBM, HBM, VMEM),
        scratch_shapes=[
            pltpu.VMEM((2, T, 128), F32),
            pltpu.VMEM((8, D), F32),
            pltpu.VMEM((8, 2048), F32),
            *[pltpu.VMEM((T, D), BF16)] * 4,
            *[pltpu.VMEM((T, D), F32)] * 2,
            pltpu.VMEM((8, D), F32),
            pltpu.VMEM((8, 16, 128), F32),
            pltpu.VMEM((8, 16, 128), F32),
            pltpu.VMEM((16, 16, 128), F32),
            *[pltpu.VMEM((2, 256, D), BF16)] * 2,
            *[pltpu.VMEM((4, 2, 2, 4, R, C), BF16) for R, C in zip(ROWS, COLUMNS)],
            *scratch,
            pltpu.SemaphoreType.DMA((79,)),
            pltpu.SemaphoreType.DMA((79,)),
            pltpu.SemaphoreType.DMA((16,)),
            pltpu.SemaphoreType.DMA((23,)),
            pltpu.SemaphoreType.DMA((23,)),
        ],
        compiler_params=pltpu.CompilerParams(
            collective_id=2, has_side_effects=True, vmem_limit_bytes=62 * MIB
        ),
    )(*args)


def position_tables():
    half = ROT // 2
    frequency = np.power(10000.0, -2.0 * np.arange(half) / ROT).astype(np.float32)
    angles = np.arange(CHIPS * CHIP_TOKENS, dtype=np.float32)[:, None] * frequency[None, :]
    angles = angles.astype(np.float64)
    cosine = np.ones((CHIPS * CHIP_TOKENS, 2 * HEAD), np.float32)
    sine = np.zeros((CHIPS * CHIP_TOKENS, 2 * HEAD), np.float32)
    for at in (0, HEAD):
        cosine[:, at : at + half] = cosine[:, at + half : at + ROT] = np.cos(angles)
        sine[:, at : at + half] = -np.sin(angles)
        sine[:, at + half : at + ROT] = np.sin(angles)
    return cosine, sine


def turn(values, tables, sign):
    lane = lax.broadcasted_iota(jnp.int32, values.shape, 1) % HEAD
    moved = jnp.where(lane < ROT // 2, pltpu.roll(values, 120, 1), pltpu.roll(values, 8, 1))
    return values * tables[0] + sign * (moved * tables[1])


def finals_kernel(a0, a1, a2, sums, hidden, output, qkv, dense, *vectors):
    low = lax.broadcasted_iota(jnp.int32, (128, 128), 1) < HEAD
    for pair in range(4):
        at = slice(1024 + pair * 128, 1152 + pair * 128)
        v0 = a2[0, :, :, at].reshape(128, 128).astype(F32)
        v1 = a2[1, :, :, at].reshape(128, 128).astype(F32)
        for j in range(2):
            r = 2 * pair + j
            q0 = a2[0, :, :, r * 128 : r * 128 + 128].reshape(128, 128).astype(F32)
            q1 = a2[1, :, :, r * 128 : r * 128 + 128].reshape(128, 128).astype(F32)
            q1 = pltpu.roll(q1, 64, 1)
            left = v0 if j == 0 else pltpu.roll(v0, 64, 1)
            right = pltpu.roll(v1, 64, 1) if j == 0 else v1
            qkv[:, r * 384 : r * 384 + 128] = q0
            qkv[:, r * 384 + 128 : r * 384 + 256] = jnp.where(low, left, q1)
            qkv[:, r * 384 + 256 : r * 384 + 384] = jnp.where(low, q1, right)
    for c in range(2):
        for k in range(2):
            piece = a2[c, k * 4 : k * 4 + 4, :, 1536:2048].reshape(64, 512)
            dense[c * 64 : c * 64 + 64, k * 512 : k * 512 + 512] = piece.astype(F32)
        for r in range(8):
            piece = a0[c, :, :, r * 256 : r * 256 + 256].reshape(128, 256)
            hidden[:, r * 512 + c * 256 : r * 512 + c * 256 + 256] = piece.astype(F32)
    output[...] = a1[...].reshape(512, D).astype(F32)
    for k in range(4):
        vectors[k][...] = sums[k : k + 1, :]
    first = lax.broadcasted_iota(jnp.int32, (1, 128), 1) < HEAD
    q1 = pltpu.roll(sums[5:6, :], 64, 1)
    vectors[4][:, 0:128] = sums[4:5, :]
    vectors[4][:, 128:256] = jnp.where(first, sums[6:7, :], q1)
    vectors[4][:, 256:384] = jnp.where(first, q1, sums[6:7, :])
    vectors[5][...] = sums[7:8, :]
    for k in range(4):
        vectors[6][:, k * 128 : k * 128 + 128] = sums[8 + k : 9 + k, :]


def finals(a0, a1, a2, sums):
    widths = (128, 128, 128, 128, 384, 128, 512)
    return pl.pallas_call(
        finals_kernel,
        out_shape=(
            jax.ShapeDtypeStruct((128, FF), F32),
            jax.ShapeDtypeStruct((512, D), F32),
            jax.ShapeDtypeStruct((128, 3 * D), F32),
            jax.ShapeDtypeStruct((128, D), F32),
            *[jax.ShapeDtypeStruct((1, w), F32) for w in widths],
        ),
        in_specs=[VMEM] * 4,
        out_specs=(VMEM,) * 11,
        compiler_params=pltpu.CompilerParams(vmem_limit_bytes=48 * MIB),
    )(a0, a1, a2, sums)


def local(
    inputs,
    cotangent,
    ln_attn_gain,
    ln_attn_bias,
    ln_mlp_gain,
    ln_mlp_bias,
    qkv_weight,
    qkv_bias,
    dense_weight,
    dense_bias,
    hidden_weight,
    hidden_bias,
    output_weight,
    output_bias,
):
    bias = qkv_bias.reshape(2, 192)
    small = jnp.concatenate(
        [
            ln_attn_gain,
            ln_attn_bias,
            ln_mlp_gain,
            ln_mlp_bias,
            bias[:, :128].reshape(256),
            bias[:, 128:].reshape(128),
            dense_bias,
            hidden_bias,
            output_bias,
            jnp.zeros((3 * 128,), BF16),
        ]
    ).reshape(16, 128)
    cosine, sine = (jnp.asarray(t) for t in position_tables())
    tokens, wh, wo, wq, wd, x, ct, attn_normed, mlp_normed, vectors = attention(
        qkv_weight,
        dense_weight,
        hidden_weight,
        output_weight,
        small.astype(F32),
        inputs,
        cotangent,
        cosine,
        sine,
    )
    outputs, input_grad, *gathered, sums = rest_of_block(
        tokens,
        x.reshape(CHIP_TOKENS, D),
        ct.reshape(CHIP_TOKENS, D),
        attn_normed,
        mlp_normed,
        wq.reshape(D, 1536),
        wd.reshape(512, D),
        wh.reshape(D, 2048),
        wo.reshape(2048, D),
        vectors,
        cosine,
        sine,
    )
    hidden, output, qkv, dense, *vectors = finals(*gathered, sums)
    ag, ab, mg, mb, qb, db, hb = (v.reshape(v.shape[1]) for v in vectors)
    return (outputs, input_grad, ag, ab, mg, mb, qkv, qb, dense, db, hidden, hb, output, db)


def solution(mesh):
    rows = P(("fsdp", "seq"), None)
    vector = P("fsdp")
    matrix = P("fsdp", None)
    shared = (vector,) * 4 + (matrix, vector) * 4
    return jax.shard_map(
        local,
        mesh=mesh,
        in_specs=(rows, rows, *shared),
        out_specs=(rows, rows, *shared),
        check_vma=False,
    )
```

```python
import functools
import math

import jax
import jax.numpy as jnp
import numpy as np
from jax import lax
from jax.experimental import pallas as pl
from jax.experimental.pallas import tpu as pltpu
from jax.sharding import PartitionSpec as P

D = 1024
FF = 4096
HEADS = 16
HEAD = 64
ROT = 16
CHIP_TOKENS = 512
FSDP = 8
CHIPS = 8

epsilon = 1e-05
F32 = jnp.float32
BF16 = jnp.bfloat16
NT = (((1,), (1,)), ((), ()))
TN = (((0,), (0,)), ((), ()))
MIB = 2**20
HBM = pl.BlockSpec(memory_space=pl.ANY)
VMEM = pl.BlockSpec(memory_space=pltpu.VMEM)


def place():
    f = lax.axis_index("fsdp")
    s = lax.axis_index("seq")
    return f, s, (f // 2, f % 2, s // 4, (s // 2) % 2, s % 2)


def device(y, z, x, core):
    return {"fsdp": y * 2 + z % 2, "seq": x * 4 + (z // 2) * 2 + core}


def barrier(devices):
    sem = pltpu.get_barrier_semaphore()
    for d in devices:
        pl.semaphore_signal(sem, inc=1, device_id=d, device_id_type=pl.DeviceIdType.MESH)
    pl.semaphore_wait(sem, len(devices))


def remote(src, dst, send, recv, target):
    return pltpu.make_async_remote_copy(
        src_ref=src,
        dst_ref=dst,
        send_sem=send,
        recv_sem=recv,
        device_id=target,
        device_id_type=pl.DeviceIdType.MESH,
    )


class Gather:
    def __init__(self, own, full, send, recv):
        f, s, (y, zl, px, zh, core) = place()
        z = zh * 2 + zl
        self.own, self.full, self.send, self.recv = own, full, send, recv
        self.yp = device((y + 1) % 4, z, px, core)
        self.ym = device((y + 3) % 4, z, px, core)
        self.zp = device(y, (z + 1) % 4, px, core)
        self.zm = device(y, (z + 3) % 4, px, core)
        self.f = f
        self.slots = [f, (f + 6) % 8, (f + 2) % 8, (f + 4) % 8]
        flip = f + 1 - 2 * zl
        self.far = [flip, (flip + 6) % 8, (flip + 2) % 8, (flip + 4) % 8]
        self.sends = []

    def neighbours(self):
        return [self.yp, self.ym, self.zp, self.zm]

    def started(self, src, dst, k, target):
        copy = remote(src, dst, self.send.at[k], self.recv.at[k], target)
        copy.start()
        self.sends.append(copy)

    def arrived(self, ref, k):
        remote(ref, ref, self.send.at[k], self.recv.at[k], self.yp).wait_recv()

    @staticmethod
    def part(ref, h):
        rows = ref.shape[0] // 2
        return ref.at[pl.ds(h * rows, rows)]

    def own_y(self):
        for n, (o, g) in enumerate(zip(self.own, self.full)):
            for k, h, target in ((0, 0, self.yp), (3, 1, self.ym), (2, 0, self.ym), (1, 1, self.yp)):
                self.started(self.part(o, h), self.part(g.at[self.f], h), 14 * n + k, target)

    def own_z(self):
        for n, (o, g) in enumerate(zip(self.own, self.full)):
            for k, h, target in ((6, 0, self.zp), (10, 1, self.zm)):
                self.started(self.part(o, h), self.part(g.at[self.f], h), 14 * n + k, target)

    def pass_on(self, n, k, slot, h, targets):
        ref = self.part(self.full[n].at[slot], h)
        self.arrived(ref, 14 * n + k)
        for kk, target in targets:
            self.started(ref, ref, 14 * n + kk, target)

    def near_y(self):
        for n in range(len(self.full)):
            self.pass_on(n, 0, self.slots[1], 0, [(4, self.yp)])
            self.pass_on(n, 3, self.slots[2], 1, [(5, self.ym)])

    def near_z(self):
        for n, g in enumerate(self.full):
            for k, slot, h, target in ((7, 1, 0, self.zp), (12, 2, 1, self.zm)):
                ref = self.part(g.at[self.slots[slot]], h)
                self.started(ref, ref, 14 * n + k, target)
            self.pass_on(n, 2, self.slots[2], 0, [(8, self.zp)])
            self.pass_on(n, 1, self.slots[1], 1, [(11, self.zm)])

    def opposite_y(self):
        for n, g in enumerate(self.full):
            self.arrived(self.part(g.at[self.slots[3]], 0), 14 * n + 4)
            self.arrived(self.part(g.at[self.slots[3]], 1), 14 * n + 5)

    def ends_z(self):
        for k, slot in ((0, self.f), (3, self.slots[3])):
            for n, g in enumerate(self.full):
                a, b = self.part(g.at[slot], 0), self.part(g.at[slot], 1)
                if k == 0:
                    a, b = self.part(self.own[n], 0), self.part(self.own[n], 1)
                at = g.at[slot]
                self.started(a, self.part(at, 0), 14 * n + 6 + k, self.zp)
                self.started(b, self.part(at, 1), 14 * n + 10 + k, self.zm)

    def sides_y(self):
        for n in range(len(self.full)):
            self.pass_on(n, 6, self.far[0], 0, [(7, self.yp), (8, self.ym)])
            self.pass_on(n, 10, self.far[0], 1, [(11, self.yp), (12, self.ym)])

    def finish_mixed(self):
        for n, g in enumerate(self.full):
            for k, slot, h in (
                (1, self.slots[1], 1),
                (2, self.slots[2], 0),
                (7, self.far[1], 0),
                (8, self.far[2], 0),
                (11, self.far[1], 1),
                (12, self.far[2], 1),
                (9, self.far[3], 0),
                (13, self.far[3], 1),
            ):
                self.arrived(self.part(g.at[slot], h), 14 * n + k)
        for copy in self.sends:
            copy.wait_send()

    def opposite(self):
        for n in range(len(self.full)):
            self.pass_on(n, 4, self.slots[3], 0, [(9, self.zp)])
            self.pass_on(n, 5, self.slots[3], 1, [(13, self.zm)])

    def finish(self):
        for n, g in enumerate(self.full):
            for j in range(4):
                self.arrived(self.part(g.at[self.far[j]], 0), 14 * n + 6 + j)
                self.arrived(self.part(g.at[self.far[j]], 1), 14 * n + 10 + j)
        for copy in self.sends:
            copy.wait_send()


def fold(op, a):
    result = a[:, :128]
    for j in range(128, a.shape[1], 128):
        result = op(result, a[:, j : j + 128])
    return result


def attention_kernel(
    qkv_w, dense_w, hidden_w, output_w, small, x, ct, cosine, sine,
    result_q, result_k, gh, go, wq_out, wd_out, x_out, ct_out, an_out, mn_out, vectors,
    raw_q, own_q, own_h, own_o, wq, wd, x_v, ct_v, an, mn, vec, norms, bias, tables, packed,
    hd, out_q, out_k, q_s, k_s, v_s, d_s, s_s, p_s, dk_s, dv_s, mx_s, l_s, o_s, dq_s,
    in_send, in_recv, out_send, out_recv, a_send, a_recv, g_send, g_recv, local_sem,
):
    f, s, (y, zl, px, zh, core) = place()
    me = s // 2
    B = CHIP_TOKENS
    n = CHIPS
    scale = 1.0 / math.sqrt(HEAD)
    sibling = device(y, zh * 2 + zl, px, 1 - core)
    others = [{"fsdp": (f + k) % 8, "seq": s} for k in range(1, 8)]
    zother = device(y, 2 * (1 - zh) + 1 - zl, px, core)

    def chip(j):
        return {"fsdp": f, "seq": j * 2 + core}

    greeted = others + [sibling, zother] + [chip((me + k) % n) for k in range(1, n)]
    entered = pltpu.get_barrier_semaphore()
    for d in greeted:
        pl.semaphore_signal(entered, inc=1, device_id=d, device_id_type=pl.DeviceIdType.MESH)

    def load(src, dst, k):
        copy = pltpu.make_async_copy(src, dst, local_sem.at[k])
        copy.start()
        return copy

    own_d = dense_w.at[pl.ds(pl.multiple_of(core * 64, 64), 64)]
    here = pl.ds(pl.multiple_of(me * B, B), B)
    load_q = load(qkv_w, raw_q, 0)
    loads = [
        load(own_d, wd.at[f], 1),
        load(x, x_v.at[core], 2),
        load(ct, ct_v.at[core], 3),
        load(small, vec.at[f], 4),
        load(cosine.at[here], tables.at[0], 5),
        load(sine.at[here], tables.at[1], 6),
    ]
    load_o = load(output_w.at[pl.ds(pl.multiple_of(core * 256, 256), 256)], own_o, 7)
    load_h = [
        load(
            hidden_w.at[:, pl.ds(pl.multiple_of(r * 512 + core * 256, 256), 256)],
            own_h.at[:, pl.ds(r * 256, 256)],
            8 + r,
        )
        for r in range(8)
    ]
    load_q.wait()
    low = lax.broadcasted_iota(jnp.int32, (128, 128), 1) < HEAD
    even = core == 0
    held = None
    for r in range(8):
        t0, t1, t2 = [raw_q[:, r * 384 + j * 128 : r * 384 + j * 128 + 128].astype(F32) for j in range(3)]
        t2 = pltpu.roll(t2, 64, 1)
        qk = jnp.where(even, t0, jnp.where(low, pltpu.roll(t1, 64, 1), t2))
        v = jnp.where(even, t1, t2)
        own_q[:, r * 128 : r * 128 + 128] = qk.astype(BF16)
        if r % 2 == 0:
            held = v
        else:
            at = 1024 + r // 2 * 128
            own_q[:, at : at + 128] = jnp.where(low, held, pltpu.roll(v, 64, 1)).astype(BF16)
    pl.semaphore_wait(entered, len(greeted))

    heads = Gather([own_q, own_d], [wq, wd], a_send, a_recv)
    units = Gather([own_h, own_o], [gh, go], g_send, g_recv)
    heads.own_y()
    heads.started(x, x_v.at[core], 28, sibling)
    heads.started(ct, ct_v.at[core], 29, sibling)
    for k in range(1, 8):
        heads.started(small, vec.at[f], 29 + k, others[k - 1])
    heads.own_z()
    wq[f] = own_q[...]

    for copy in loads:
        copy.wait()
    heads.arrived(x_v.at[1 - core], 28)
    for k in range(1, 8):
        heads.arrived(vec.at[(f + 8 - k) % 8], 29 + k)
    heads.near_y()
    for r in range(8):
        at = slice(r * 128, r * 128 + 128)
        norms[0:4, at] = vec[r, 0:4, :]
        bias[0:1, at] = vec[r, pl.ds(4 + core, 1), :]
    first = low[0:1, :]
    for pair in range(4):
        a, b = vec[2 * pair, 6:7, :], vec[2 * pair + 1, 6:7, :]
        v_even = jnp.where(first, a, pltpu.roll(b, 64, 1))
        v_odd = jnp.where(first, pltpu.roll(a, 64, 1), b)
        at = slice(1024 + pair * 128, 1152 + pair * 128)
        bias[0:1, at] = jnp.where(even, v_even, v_odd)
    for c in range(2):
        rows = slice(c * 256, c * 256 + 256)
        normed, _ = normalised(x_v[c])
        an[rows, :] = (normed * norms[0:1, :] + norms[1:2, :]).astype(BF16)
        mn[rows, :] = (normed * norms[2:3, :] + norms[3:4, :]).astype(BF16)
        if c == 0:
            heads.near_z()
    heads.opposite()
    heads.arrived(ct_v.at[1 - core], 29)
    load_o.wait()
    for copy in load_h:
        copy.wait()
    units.own_y()
    heads.finish()

    def given(j):
        return remote(packed.at[j], hd.at[me], in_send.at[j], in_recv.at[me], chip(j))

    wide = lax.broadcasted_iota(jnp.int32, (B, 128), 1) < HEAD
    rotary = (tables[0], tables[1])
    tokens = ct_v[...].reshape(B, D)

    def project(t, _):
        pair = (px + 1 + t) % 4
        a = an[...]
        qk = pl.ds(pl.multiple_of(pair * 256, 256), 256)
        vs = pl.ds(pl.multiple_of(1024 + pair * 128, 128), 128)
        weight = wq[:, :, qk].reshape(D, 256)
        projected = jnp.dot(a, weight, preferred_element_type=F32) + bias[0:1, qk]
        for j in range(2):
            turned = turn(projected[:, j * 128 : j * 128 + 128], rotary, 1.0)
            packed[2 * pair + j, :, 0:128] = turned.astype(BF16)
        weight = wq[:, :, vs].reshape(D, 128)
        v = jnp.dot(a, weight, preferred_element_type=F32) + bias[0:1, vs]
        weight = wd[pl.ds(2 * pair, 2)].reshape(128, D)
        d = lax.dot_general(tokens, weight, NT, preferred_element_type=F32)
        packed[2 * pair, :, 128:256] = jnp.where(wide, v, pltpu.roll(d, 64, 1)).astype(BF16)
        packed[2 * pair + 1, :, 128:256] = jnp.where(wide, pltpu.roll(v, 64, 1), d).astype(BF16)
        for j in range(2):

            @pl.when(2 * pair + j != me)
            def _():
                given(2 * pair + j).start()

        return 0

    lax.fori_loop(0, 4, project, 0)
    hd[me] = packed[me]
    units.near_y()
    saves = [
        load(a, b, 16 + k)
        for k, (a, b) in enumerate(
            [
                (own_h, gh.at[f]),
                (own_o, go.at[f]),
                (wq, wq_out),
                (wd, wd_out),
                (x_v, x_out),
                (ct_v, ct_out),
                (an, an_out),
                (mn, mn_out),
                (vec, vectors),
            ]
        )
    ]
    for k in range(1, n):
        j = (me + n - k) % n
        remote(hd.at[j], hd.at[j], in_send.at[j], in_recv.at[j], chip(j)).wait_recv()
    units.opposite_y()
    units.ends_z()

    def block(i):
        return pl.ds(pl.multiple_of(i * B, B), B)

    def prepare(i, _):
        rows = block(i)
        piece = hd[i]
        q_s[rows, :] = piece[:, 0:64] * jnp.asarray(scale, BF16)
        k_s[rows, :] = piece[:, 64:128]
        v_s[rows, :] = piece[:, 128:192]
        d_s[rows, :] = piece[:, 192:256]
        return 0

    lax.fori_loop(0, n, prepare, 0)
    dk_s[...] = jnp.zeros_like(dk_s)
    dv_s[...] = jnp.zeros_like(dv_s)
    keep = lax.broadcasted_iota(jnp.int32, (B, B), 1) <= lax.broadcasted_iota(
        jnp.int32, (B, B), 0
    )

    def back_to(i, h):
        src, dst = (out_q, result_q) if h == 0 else (out_k, result_k)
        return remote(
            src.at[i], dst.at[me], out_send.at[8 * h + i], out_recv.at[8 * h + me], chip(i)
        )

    def keep_own(h):
        src, dst = (out_q, result_q) if h == 0 else (out_k, result_k)
        return pltpu.make_async_copy(src.at[me], dst.at[me], local_sem.at[25 + h])

    def in_pairs(count, body):
        def pair(k, _):
            body(2 * k)
            body(2 * k + 1)
            return 0

        def single(k, _):
            body(k)
            return 0

        lax.fori_loop(0, count // 2, pair, 0)
        lax.fori_loop(count // 2 * 2, count, single, 0)

    def query_block(t, _):
        i = (me + 1 + t) % n
        rows = block(i)
        qi = q_s[rows, :]
        mx_s[...] = jnp.full(mx_s.shape, -1e30, F32)

        def score(kb):
            return lax.dot_general(qi, k_s[block(kb), :], NT, preferred_element_type=F32)

        def first(kb):
            scores = score(kb)
            s_s[kb] = scores
            mx_s[...] = jnp.maximum(mx_s[...], fold(jnp.maximum, scores))

        in_pairs(i, first)
        scores = jnp.where(keep, score(i), -1e30)
        s_s[i] = scores
        row_max = jnp.max(
            jnp.maximum(mx_s[...], fold(jnp.maximum, scores)), axis=1, keepdims=True
        )
        l_s[...] = jnp.zeros_like(l_s)
        o_s[...] = jnp.zeros_like(o_s)
        dq_s[...] = jnp.zeros_like(dq_s)

        def second(kb):
            p = jnp.exp(s_s[kb] - row_max)
            l_s[...] += fold(jnp.add, p)
            pb = p.astype(BF16)
            p_s[kb] = pb
            o_s[...] += jnp.dot(pb, v_s[block(kb), :], preferred_element_type=F32)

        in_pairs(i + 1, second)
        inverse = 1.0 / jnp.sum(l_s[...], axis=1, keepdims=True)
        o = o_s[...] * inverse
        d = (d_s[rows, :].astype(F32) * inverse).astype(BF16)
        delta = jnp.sum(o * d.astype(F32), axis=1, keepdims=True)
        q_t = qi.T
        d_t = d.T

        def third(kb):
            cols = block(kb)
            pb = p_s[kb]
            dp = lax.dot_general(d, v_s[cols, :], NT, preferred_element_type=F32)
            ds = (pb.astype(F32) * (dp - delta)).astype(BF16)
            dq_s[...] += jnp.dot(ds, k_s[cols, :], preferred_element_type=F32)
            dk_s[:, cols] += jnp.dot(q_t, ds, preferred_element_type=F32)
            dv_s[:, cols] += jnp.dot(d_t, pb, preferred_element_type=F32)

        in_pairs(i + 1, third)
        out_q[i, :, 0:64] = (dq_s[...] * scale).astype(BF16)
        out_q[i, :, 64:128] = o.astype(BF16)

        @pl.when(i != me)
        def _():
            back_to(i, 0).start()

        return 0

    def key_block(t, _):
        i = (me + 1 + t) % n
        rows = block(i)
        out_k[i, :, 0:64] = dv_s[:, rows].T.astype(BF16)
        out_k[i, :, 64:128] = dk_s[:, rows].T.astype(BF16)

        @pl.when(i != me)
        def _():
            back_to(i, 1).start()

        return 0

    lax.fori_loop(0, 1, query_block, 0)
    units.sides_y()
    lax.fori_loop(1, n, query_block, 0)

    lax.fori_loop(0, n, key_block, 0)
    keep_own(0).start()
    keep_own(1).start()

    for k in range(1, n):
        given((me + k) % n).wait_send()
    for copy in saves:
        copy.wait()
    units.finish_mixed()
    for h, result in enumerate((result_q, result_k)):
        for k in range(1, n):
            back_to((me + k) % n, h).wait_send()
        keep_own(h).wait()
        for k in range(1, n):
            j = (me + k) % n
            ref = result.at[j]
            remote(ref, ref, out_send.at[8 * h + j], out_recv.at[8 * h + j], chip(me)).wait_recv()


def attention(*args):
    B = CHIP_TOKENS
    L = CHIPS * B

    def shape(*dims):
        return jax.ShapeDtypeStruct(dims, BF16)

    return pl.pallas_call(
        attention_kernel,
        out_shape=(
            shape(CHIPS, B, 2 * HEAD),
            shape(CHIPS, B, 2 * HEAD),
            shape(8, 128, 2048),
            shape(8, 256, 1024),
            shape(8, 128, 1536),
            shape(8, 64, 1024),
            shape(2, 256, D),
            shape(2, 256, D),
            shape(B, D),
            shape(B, D),
            jax.ShapeDtypeStruct((8, 16, 128), F32),
        ),
        in_specs=[HBM] * 9,
        out_specs=(HBM,) * 11,
        scratch_shapes=[
            pltpu.VMEM((128, 3072), BF16),
            pltpu.VMEM((128, 1536), BF16),
            pltpu.VMEM((128, 2048), BF16),
            pltpu.VMEM((256, 1024), BF16),
            pltpu.VMEM((8, 128, 1536), BF16),
            pltpu.VMEM((8, 64, 1024), BF16),
            *[pltpu.VMEM((2, 256, D), BF16)] * 2,
            *[pltpu.VMEM((B, D), BF16)] * 2,
            pltpu.VMEM((8, 16, 128), F32),
            pltpu.VMEM((8, D), F32),
            pltpu.VMEM((8, 1536), F32),
            pltpu.VMEM((2, B, 128), F32),
            *[pltpu.VMEM((CHIPS, B, 4 * HEAD), BF16)] * 2,
            *[pltpu.VMEM((CHIPS, B, 2 * HEAD), BF16)] * 2,
            *[pltpu.VMEM((L, HEAD), BF16)] * 4,
            pltpu.VMEM((L // B, B, B), F32),
            pltpu.VMEM((L // B, B, B), BF16),
            *[pltpu.VMEM((HEAD, L), F32)] * 2,
            *[pltpu.VMEM((B, 128), F32)] * 2,
            *[pltpu.VMEM((B, HEAD), F32)] * 2,
            *[pltpu.SemaphoreType.DMA((CHIPS,))] * 2,
            *[pltpu.SemaphoreType.DMA((2 * CHIPS,))] * 2,
            *[pltpu.SemaphoreType.DMA((37,))] * 2,
            *[pltpu.SemaphoreType.DMA((28,))] * 2,
            pltpu.SemaphoreType.DMA((27,)),
        ],
        compiler_params=pltpu.CompilerParams(
            collective_id=1, has_side_effects=True, vmem_limit_bytes=60 * MIB
        ),
    )(*args)


ORDERS = ("yzx", "zxy", "xyz")
LEADS = ((2, 4), (2, 4), (4, 2))
ROWS = (16, 32, 16)
COLUMNS = (2048, 1024, 2048)


def chunk(n, stage, g, t, h, where):
    y, zl, zh, px = where
    if stage == 0:
        if n == 0:
            return g.at[t, h]
        if n == 1:
            return g.at[pl.ds(2 * h, 2), t % 2, t // 2]
        return g.at[:, h, :, t]
    if stage == 1:
        if n == 0:
            return g.at[y, t % 2, t // 2, pl.ds(2 * h, 2)]
        if n == 1:
            return g.at[pl.ds(2 * h, 2), zl, zh, t]
        return g.at[t, h, :, px]
    half = g.shape[-1] // 2
    columns = pl.ds(h * half, half)
    if n == 0:
        return g.at[y, zl, zh, t, :, columns]
    if n == 1:
        return g.at[t, zl, zh, px, :, columns]
    return g.at[y, t % 2, t // 2, px, :, columns]


def add_into(dst, terms):
    lead = tuple(dst.shape[:-2])

    def body(k, _):
        at = []
        for extent in reversed(lead):
            at.insert(0, k % extent)
            k = k // extent
        at = (*at, slice(None), slice(None))
        total = dst[at].astype(F32)
        for t in terms:
            total = total + t[at].astype(F32)
        dst[at] = total.astype(BF16)
        return 0

    lax.fori_loop(0, math.prod(lead), body, 0)


def normalised(values):
    values = values.astype(F32)
    centered = values - jnp.mean(values, axis=-1, keepdims=True)
    variance = jnp.mean(centered * centered, axis=-1, keepdims=True)
    scale = lax.rsqrt(variance + epsilon)
    return centered * scale, scale


def rest_kernel(
    tokens_q, tokens_k, x, ct, an, mn, wq, wd, wh, wo, vec, cosine, sine,
    outputs, input_grad, gathered0, gathered1, gathered2, small_out,
    tables, norms, unit_bias, x_v, ct_v, an_v, mn_v, branches, weighted, sums, small, sm_a, sm_b, pair_send, pair_recv,
    g0, g1, g2, *rest,
):
    grads = (g0, g1, g2)
    gathered = (gathered0, gathered1, gathered2)
    bufs = [(*rest[6 * n : 6 * n + 6], gathered[n]) for n in range(3)]
    send, recv, local_sem, sm_send, sm_recv = rest[18:]
    f, s, (y, zl, px, zh, core) = place()
    z = zh * 2 + zl
    coordinate = {"y": y, "z": z, "x": px}
    where = (y, zl, zh, px)
    T = CHIP_TOKENS

    def along(axis, step):
        t = dict(coordinate)
        t[axis] = (t[axis] + step) % 4
        return device(t["y"], t["z"], t["x"], core)

    plus = {a: along(a, 1) for a in "yzx"}
    minus = {a: along(a, 3) for a in "yzx"}
    same_seq = [{"fsdp": (f + k) % 8, "seq": s} for k in range(1, 8)]
    same_fsdp = [{"fsdp": f, "seq": (s + k) % 16} for k in range(1, 16)]
    zother = device(y, 2 * (1 - zh) + 1 - zl, px, core)
    sibling = device(y, z, px, 1 - core)
    sends = []

    def load(src, dst, k):
        copy = pltpu.make_async_copy(src, dst, local_sem.at[k])
        copy.start()
        return copy

    def started(src, dst, k, target):
        copy = remote(src, dst, send.at[k], recv.at[k], target)
        copy.start()
        sends.append(copy)

    def arrived(ref, k):
        remote(ref, ref, send.at[k], recv.at[k], sibling).wait_recv()

    def small_sent(src, dst, k, target):
        copy = remote(src, dst, sm_send.at[k], sm_recv.at[k], target)
        copy.start()
        sends.append(copy)

    def small_arrived(ref, k):
        remote(ref, ref, sm_send.at[k], sm_recv.at[k], sibling).wait_recv()

    def buffers(n, stage):
        return bufs[n][2 * stage], bufs[n][2 * stage + 1]

    def raw_copies(n, stage):
        axis = ORDERS[n][stage]
        p = coordinate[axis]
        opp, fin = buffers(n, stage)
        b = 26 * n + 6 * stage

        def copy(t, h, dst, k, target):
            src = chunk(n, stage, grads[n], t % 4, h, where)
            return remote(src, dst, send.at[k], recv.at[k], target)

        return [
            copy(p + 2, 0, opp.at[0], b, plus[axis]),
            copy(p + 2, 1, opp.at[1], b + 1, minus[axis]),
            copy(p + 1, 1, fin.at[0, 1], b + 2, plus[axis]),
            copy(p + 3, 0, fin.at[1, 0], b + 3, minus[axis]),
        ]

    def relay_copy(n, stage, h):
        axis = ORDERS[n][stage]
        _, fin = buffers(n, stage)
        k = 26 * n + 6 * stage + 4 + h
        t = coordinate[axis] + 1 + 2 * h
        src = chunk(n, stage, grads[n], t % 4, h, where)
        target = (plus, minus)[h][axis]
        return src, remote(src, fin.at[h, h], send.at[k], recv.at[k], target)

    def begin(n, stage):
        for copy in raw_copies(n, stage):
            copy.start()

    def relay(n, stage):
        opp, _ = buffers(n, stage)
        for h in range(2):
            mid, copy = relay_copy(n, stage, h)
            arrived(opp.at[h], 26 * n + 6 * stage + h)
            add_into(mid, [opp.at[h]])
            copy.start()

    def finish(n, stage):
        p = coordinate[ORDERS[n][stage]]
        _, fin = buffers(n, stage)
        b = 26 * n + 6 * stage
        arrived(fin.at[0, 1], b + 2)
        arrived(fin.at[1, 0], b + 3)
        arrived(fin.at[0, 0], b + 4)
        arrived(fin.at[1, 1], b + 5)
        for h in range(2):
            add_into(chunk(n, stage, grads[n], p, h, where), [fin.at[0, h], fin.at[1, h]])

    keeps = [load(a, b, k) for k, (a, b) in enumerate([(x, x_v), (ct, ct_v), (an, an_v), (mn, mn_v)])]
    barrier(same_seq + same_fsdp + [zother])
    small[...] = jnp.zeros_like(small)
    here = pl.ds(pl.multiple_of((px * 2 + zh) * T, T), T)
    keeps += [load(cosine.at[here], tables.at[0], 12), load(sine.at[here], tables.at[1], 13)]
    for r in range(8):
        at = slice(r * 128, r * 128 + 128)
        norms[0:4, at] = vec[r, 0:4, :]
        norms[4:5, at] = vec[r, 7:8, :] + vec[r, 12:13, :]
        for j in range(2):
            unit_bias[0:1, r * 256 + j * 128 : r * 256 + j * 128 + 128] = vec[
                r, pl.ds(8 + 2 * core + j, 1), :
            ]

    def attention_part(wq_v, wd_v, tq_v, tk_v, pg_v, at_v, turned_v):
        loads = [load(a, b, 4 + k) for k, (a, b) in enumerate([(tokens_q, tq_v), (wq, wq_v), (wd, wd_v)])]
        load_k = load(tokens_k, tk_v, 14)
        for copy in keeps:
            copy.wait()
        loads[0].wait()
        load_k.wait()
        low = lax.broadcasted_iota(jnp.int32, (T, 128), 1) < HEAD
        first = lax.broadcasted_iota(jnp.int32, (1, 128), 1) < HEAD
        rotary = (tables[0], tables[1])
        for pair in range(4):
            for j in range(2):
                r = 2 * pair + j
                at = slice(r * 128, r * 128 + 128)
                qk = jnp.where(low, tq_v[r].astype(F32), tk_v[r].astype(F32))
                turned = turn(qk, rotary, -1.0).astype(BF16)
                pg_v[:, at] = turned
                small[r, pl.ds(4 + core, 1), :] = jnp.sum(turned.astype(F32), axis=0, keepdims=True)
            a, b = [
                jnp.where(low, tk_v[r].astype(F32), tq_v[r].astype(F32))
                for r in (2 * pair, 2 * pair + 1)
            ]
            v = jnp.where(low, a, pltpu.roll(b, 64, 1))
            pg_v[:, 1024 + pair * 128 : 1152 + pair * 128] = v.astype(BF16)
            total = jnp.sum(v, axis=0, keepdims=True)
            moved = jnp.sum(pltpu.roll(v, 64, 1), axis=0, keepdims=True)
            zero = jnp.zeros_like(total)
            at_low = (jnp.where(first, total, zero), jnp.where(first, moved, zero))
            at_high = (jnp.where(first, zero, moved), jnp.where(first, zero, total))
            for j in range(2):
                small[2 * pair + j, 6:7, :] = jnp.where(core == 0, at_low[j], at_high[j])
            o = jnp.where(low, pltpu.roll(a, 64, 1), b)
            at_v[:, pair * 128 : pair * 128 + 128] = o.astype(BF16)

        turned_v[...] = an_v[...].T

        def qkv_columns(k, _):
            at = pl.ds(pl.multiple_of(k * 512, 512), 512)
            part = jnp.dot(turned_v[...], pg_v[:, at], preferred_element_type=F32)
            g2[:, :, :, :, :, at] = part.astype(BF16).reshape(4, 2, 2, 4, 16, 512)
            return 0

        lax.fori_loop(0, 3, qkv_columns, 0)
        turned_v[0:512, :] = at_v[...].T
        for k in range(2):
            part = jnp.dot(
                turned_v[0:512, :], ct_v[:, k * 512 : k * 512 + 512], preferred_element_type=F32
            )
            g2[:, :, k, :, :, 1536:2048] = part.astype(BF16).reshape(4, 2, 4, 16, 512)
        begin(2, 0)
        loads[1].wait()
        loads[2].wait()
        grad = lax.dot_general(pg_v[...], wq_v[...], NT, preferred_element_type=F32)
        normed, _ = normalised(x_v[...])
        sums[0:1, :] = jnp.sum(grad * normed, axis=0, keepdims=True)
        sums[1:2, :] = jnp.sum(grad, axis=0, keepdims=True)
        weighted[...] = grad * norms[0:1, :]
        branches[...] = jnp.dot(at_v[...], wd_v[...], preferred_element_type=F32)

    pl.run_scoped(
        attention_part,
        pltpu.VMEM((D, 1536), BF16),
        pltpu.VMEM((512, D), BF16),
        pltpu.VMEM((8, T, 128), BF16),
        pltpu.VMEM((8, T, 128), BF16),
        pltpu.VMEM((T, 1536), BF16),
        pltpu.VMEM((T, 512), BF16),
        pltpu.VMEM((D, T), BF16),
    )

    def unit_part(wh_v, wo_v, act_v, hg_v, turned_v):
        loads = [load(a, b, 7 + k) for k, (a, b) in enumerate([(wh, wh_v), (wo, wo_v)])]
        loads[0].wait()
        loads[1].wait()

        def units(r, _):
            at = pl.ds(pl.multiple_of(r * 256, 256), 256)
            h = jnp.dot(mn_v[...], wh_v[:, at], preferred_element_type=F32) + unit_bias[0:1, at]
            below = 0.5 + 0.5 * lax.erf(h * math.sqrt(0.5))
            density = jnp.exp(-0.5 * h * h) * (1.0 / math.sqrt(2.0 * math.pi))
            act_v[:, at] = (h * below).astype(BF16)
            up = lax.dot_general(ct_v[...], wo_v[at, :], NT, preferred_element_type=F32)
            grad = (up * (below + h * density)).astype(BF16)
            hg_v[:, at] = grad
            total = jnp.sum(grad.astype(F32), axis=0, keepdims=True)
            small[r, pl.ds(8 + 2 * core, 1), :] = total[:, 0:128]
            small[r, pl.ds(9 + 2 * core, 1), :] = total[:, 128:256]
            return 0

        lax.fori_loop(0, 8, units, 0)
        turned_v[...] = act_v[...].T

        def output_rows(k, _):
            at = pl.ds(pl.multiple_of(k * 512, 512), 512)
            part = jnp.dot(turned_v[at, :], ct_v[...], preferred_element_type=F32)
            g1[k] = part.astype(BF16).reshape(2, 2, 4, 32, 1024)
            return 0

        lax.fori_loop(0, 4, output_rows, 0)
        begin(1, 0)
        turned_v[0:D, :] = mn_v[...].T

        def hidden_columns(k, _):
            at = pl.ds(pl.multiple_of(k * 512, 512), 512)
            part = jnp.dot(turned_v[0:D, :], hg_v[:, at], preferred_element_type=F32)
            g0[:, :, :, :, :, at] = part.astype(BF16).reshape(4, 2, 2, 4, 16, 512)
            return 0

        lax.fori_loop(0, 4, hidden_columns, 0)
        begin(0, 0)
        relay(2, 0)
        grad = lax.dot_general(hg_v[...], wh_v[...], NT, preferred_element_type=F32)
        normed, _ = normalised(x_v[...])
        sums[2:3, :] = jnp.sum(grad * normed, axis=0, keepdims=True)
        sums[3:4, :] = jnp.sum(grad, axis=0, keepdims=True)
        weighted[...] += grad * norms[2:3, :]
        branches[...] += jnp.dot(act_v[...], wo_v[...], preferred_element_type=F32)

    pl.run_scoped(
        unit_part,
        pltpu.VMEM((D, 2048), BF16),
        pltpu.VMEM((2048, D), BF16),
        pltpu.VMEM((T, 2048), BF16),
        pltpu.VMEM((T, 2048), BF16),
        pltpu.VMEM((2048, T), BF16),
    )

    other = pl.ds(pl.multiple_of((1 - core) * 256, 256), 256)
    mine = pl.ds(pl.multiple_of(core * 256, 256), 256)
    pair_send[0] = branches[other, :].astype(BF16)
    pair_send[1] = weighted[other, :].astype(BF16)
    started(pair_send, pair_recv, 78, sibling)
    sums[4:5, :] = jnp.sum(ct_v[mine, :].astype(F32), axis=0, keepdims=True)
    for r in range(8):
        at = slice(r * 128, r * 128 + 128)
        small[r, 0:4, :] = sums[0:4, at]
        small[r, 7:8, :] = sums[4:5, at]
    for k in range(1, 8):
        small_sent(small.at[(f + k) % 8], sm_a.at[k], k, same_seq[k - 1])
    relay(1, 0)
    relay(0, 0)
    arrived(pair_recv, 78)
    normed, scale = normalised(x_v[mine, :])
    total = x_v[mine, :].astype(F32) + branches[mine, :] + pair_recv[0].astype(F32) + norms[4:5, :]
    outputs[...] = total.astype(BF16)
    w = weighted[mine, :] + pair_recv[1].astype(F32)
    input_grad[...] = ct_v[mine, :].astype(F32) + scale * (
        w
        - jnp.mean(w, axis=-1, keepdims=True)
        - normed * jnp.mean(w * normed, axis=-1, keepdims=True)
    )
    finish(2, 0)
    begin(2, 1)
    for k in range(1, 8):
        small_arrived(sm_a.at[k], k)
    total = small[f]
    for k in range(1, 8):
        total = total + sm_a[k]
    sm_b[0] = total
    for k in range(1, 16):
        small_sent(sm_b.at[0], sm_b.at[k], 7 + k, same_fsdp[k - 1])
    finish(1, 0)
    begin(1, 1)
    finish(0, 0)
    begin(0, 1)

    across = device(y, (z + 2) % 4, px, core)
    xp, xm = plus["x"], minus["x"]

    def at_chip(n, zz, xx):
        return bufs[n][6].at[core, zz * 4 + xx % 4]

    def spread(n):
        b = 26 * n + 18
        done = grads[n].at[y, zl, zh, px]
        place_ = at_chip(n, zh, px)
        keep = pltpu.make_async_copy(done, place_, local_sem.at[9 + n])
        keep.start()
        started(done, place_, b, across)
        started(done, place_, b + 1, xp)
        started(done, place_, b + 2, xm)
        return keep

    def spread_on(n):
        b = 26 * n + 18
        theirs = at_chip(n, 1 - zh, px)
        arrived(theirs, b)
        started(theirs, theirs, b + 3, xp)
        started(theirs, theirs, b + 4, xm)
        left, right = at_chip(n, zh, px + 3), at_chip(n, 1 - zh, px + 1)
        arrived(left, b + 1)
        started(left, left, b + 5, xp)
        arrived(right, b + 4)
        started(right, right, b + 6, xm)

    def spread_end(n, keep):
        b = 26 * n + 18
        arrived(at_chip(n, zh, px + 1), b + 2)
        arrived(at_chip(n, 1 - zh, px + 3), b + 3)
        arrived(at_chip(n, zh, px + 2), b + 5)
        arrived(at_chip(n, 1 - zh, px + 2), b + 6)
        keep.wait()
        whole = bufs[n][6].at[core]
        started(whole, whole, b + 7, sibling)

    order = (2, 1, 0)
    for n in order:
        relay(n, 1)
    for n in order:
        finish(n, 1)
        begin(n, 2)
    for n in order:
        relay(n, 2)
    copies = {}
    for n in order:
        finish(n, 2)
        copies[n] = spread(n)
    for n in order:
        spread_on(n)
    for n in order:
        spread_end(n, copies[n])
    for k in range(1, 16):
        small_arrived(sm_b.at[k], 7 + k)
    total = sm_b[0]
    for k in range(1, 16):
        total = total + sm_b[k]
    small_out[...] = total

    for n in order:
        arrived(gathered[n].at[1 - core], 26 * n + 25)
    for copy in sends:
        copy.wait_send()
    for n in range(3):
        for stage in range(3):
            for copy in raw_copies(n, stage):
                copy.wait_send()
            for h in range(2):
                relay_copy(n, stage, h)[1].wait_send()


def rest_of_block(*args):
    scratch = []
    for lead, R, C in zip(LEADS, ROWS, COLUMNS):
        for dims in (
            (2, *lead, R, C),
            (2, 2, *lead, R, C),
            (2, 2, R, C),
            (2, 2, 2, R, C),
            (2, R, C // 2),
            (2, 2, R, C // 2),
        ):
            scratch.append(pltpu.VMEM(dims, BF16))
    T = CHIP_TOKENS
    return pl.pallas_call(
        rest_kernel,
        out_shape=(
            jax.ShapeDtypeStruct((256, D), BF16),
            jax.ShapeDtypeStruct((256, D), F32),
            *[jax.ShapeDtypeStruct((2, 8, R, C), BF16) for R, C in zip(ROWS, COLUMNS)],
            jax.ShapeDtypeStruct((16, 128), F32),
        ),
        in_specs=[HBM] * 10 + [VMEM, HBM, HBM],
        out_specs=(VMEM, VMEM, HBM, HBM, HBM, VMEM),
        scratch_shapes=[
            pltpu.VMEM((2, T, 128), F32),
            pltpu.VMEM((8, D), F32),
            pltpu.VMEM((8, 2048), F32),
            *[pltpu.VMEM((T, D), BF16)] * 4,
            *[pltpu.VMEM((T, D), F32)] * 2,
            pltpu.VMEM((8, D), F32),
            pltpu.VMEM((8, 16, 128), F32),
            pltpu.VMEM((8, 16, 128), F32),
            pltpu.VMEM((16, 16, 128), F32),
            *[pltpu.VMEM((2, 256, D), BF16)] * 2,
            *[pltpu.VMEM((4, 2, 2, 4, R, C), BF16) for R, C in zip(ROWS, COLUMNS)],
            *scratch,
            pltpu.SemaphoreType.DMA((79,)),
            pltpu.SemaphoreType.DMA((79,)),
            pltpu.SemaphoreType.DMA((16,)),
            pltpu.SemaphoreType.DMA((23,)),
            pltpu.SemaphoreType.DMA((23,)),
        ],
        compiler_params=pltpu.CompilerParams(
            collective_id=2, has_side_effects=True, vmem_limit_bytes=62 * MIB
        ),
    )(*args)


def position_tables():
    half = ROT // 2
    frequency = np.power(10000.0, -2.0 * np.arange(half) / ROT).astype(np.float32)
    angles = np.arange(CHIPS * CHIP_TOKENS, dtype=np.float32)[:, None] * frequency[None, :]
    angles = angles.astype(np.float64)
    cosine = np.ones((CHIPS * CHIP_TOKENS, 2 * HEAD), np.float32)
    sine = np.zeros((CHIPS * CHIP_TOKENS, 2 * HEAD), np.float32)
    for at in (0, HEAD):
        cosine[:, at : at + half] = cosine[:, at + half : at + ROT] = np.cos(angles)
        sine[:, at : at + half] = -np.sin(angles)
        sine[:, at + half : at + ROT] = np.sin(angles)
    return cosine, sine


def turn(values, tables, sign):
    lane = lax.broadcasted_iota(jnp.int32, values.shape, 1) % HEAD
    moved = jnp.where(lane < ROT // 2, pltpu.roll(values, 120, 1), pltpu.roll(values, 8, 1))
    return values * tables[0] + sign * (moved * tables[1])


def finals_kernel(
    h0, h1, h2, out_in, grad_in, sums, hidden, output, qkv, dense, out_ref, grad_ref, *rest
):
    vectors, (a0, a1, a2, sem) = rest[:7], rest[7:]
    loads = [
        pltpu.make_async_copy(a, b, sem.at[k])
        for k, (a, b) in enumerate(
            [(h2, a2), (h0, a0), (h1, a1), (out_in, out_ref), (grad_in, grad_ref)]
        )
    ]
    for copy in loads:
        copy.start()
    loads[0].wait()
    low = lax.broadcasted_iota(jnp.int32, (128, 128), 1) < HEAD
    for pair in range(4):
        at = slice(1024 + pair * 128, 1152 + pair * 128)
        v0 = a2[0, :, :, at].reshape(128, 128).astype(F32)
        v1 = a2[1, :, :, at].reshape(128, 128).astype(F32)
        for j in range(2):
            r = 2 * pair + j
            q0 = a2[0, :, :, r * 128 : r * 128 + 128].reshape(128, 128).astype(F32)
            q1 = a2[1, :, :, r * 128 : r * 128 + 128].reshape(128, 128).astype(F32)
            q1 = pltpu.roll(q1, 64, 1)
            left = v0 if j == 0 else pltpu.roll(v0, 64, 1)
            right = pltpu.roll(v1, 64, 1) if j == 0 else v1
            qkv[:, r * 384 : r * 384 + 128] = q0
            qkv[:, r * 384 + 128 : r * 384 + 256] = jnp.where(low, left, q1)
            qkv[:, r * 384 + 256 : r * 384 + 384] = jnp.where(low, q1, right)
    for c in range(2):
        for k in range(2):
            piece = a2[c, k * 4 : k * 4 + 4, :, 1536:2048].reshape(64, 512)
            dense[c * 64 : c * 64 + 64, k * 512 : k * 512 + 512] = piece.astype(F32)
    loads[1].wait()
    for c in range(2):
        for r in range(8):
            piece = a0[c, :, :, r * 256 : r * 256 + 256].reshape(128, 256)
            hidden[:, r * 512 + c * 256 : r * 512 + c * 256 + 256] = piece.astype(F32)
    loads[2].wait()
    output[...] = a1[...].reshape(512, D).astype(F32)
    loads[3].wait()
    loads[4].wait()
    for k in range(4):
        vectors[k][...] = sums[k : k + 1, :]
    first = lax.broadcasted_iota(jnp.int32, (1, 128), 1) < HEAD
    q1 = pltpu.roll(sums[5:6, :], 64, 1)
    vectors[4][:, 0:128] = sums[4:5, :]
    vectors[4][:, 128:256] = jnp.where(first, sums[6:7, :], q1)
    vectors[4][:, 256:384] = jnp.where(first, q1, sums[6:7, :])
    vectors[5][...] = sums[7:8, :]
    for k in range(4):
        vectors[6][:, k * 128 : k * 128 + 128] = sums[8 + k : 9 + k, :]


def finals(a0, a1, a2, outputs, input_grad, sums):
    widths = (128, 128, 128, 128, 384, 128, 512)
    return pl.pallas_call(
        finals_kernel,
        out_shape=(
            jax.ShapeDtypeStruct((128, FF), F32),
            jax.ShapeDtypeStruct((512, D), F32),
            jax.ShapeDtypeStruct((128, 3 * D), F32),
            jax.ShapeDtypeStruct((128, D), F32),
            jax.ShapeDtypeStruct((256, D), BF16),
            jax.ShapeDtypeStruct((256, D), F32),
            *[jax.ShapeDtypeStruct((1, w), F32) for w in widths],
        ),
        in_specs=[HBM] * 5 + [VMEM],
        out_specs=(VMEM,) * 13,
        scratch_shapes=[
            *[pltpu.VMEM((2, 8, R, C), BF16) for R, C in zip(ROWS, COLUMNS)],
            pltpu.SemaphoreType.DMA((5,)),
        ],
        compiler_params=pltpu.CompilerParams(vmem_limit_bytes=60 * MIB),
    )(a0, a1, a2, outputs, input_grad, sums)


def local(
    inputs,
    cotangent,
    ln_attn_gain,
    ln_attn_bias,
    ln_mlp_gain,
    ln_mlp_bias,
    qkv_weight,
    qkv_bias,
    dense_weight,
    dense_bias,
    hidden_weight,
    hidden_bias,
    output_weight,
    output_bias,
):
    bias = qkv_bias.reshape(2, 192)
    small = jnp.zeros((16, 128), F32)
    for k, rows in (
        (0, ln_attn_gain),
        (1, ln_attn_bias),
        (2, ln_mlp_gain),
        (3, ln_mlp_bias),
        (4, bias[:, :128]),
        (6, bias[:, 128:]),
        (7, dense_bias),
        (8, hidden_bias),
        (12, output_bias),
    ):
        rows = rows.reshape(-1, 128).astype(F32)
        small = small + jnp.pad(rows, ((k, 16 - k - rows.shape[0]), (0, 0)))
    cosine, sine = (jnp.asarray(t) for t in position_tables())
    tokens_q, tokens_k, wh, wo, wq, wd, x, ct, attn_normed, mlp_normed, vectors = attention(
        qkv_weight,
        dense_weight,
        hidden_weight,
        output_weight,
        small,
        inputs,
        cotangent,
        cosine,
        sine,
    )
    outputs, input_grad, *gathered, sums = rest_of_block(
        tokens_q,
        tokens_k,
        x.reshape(CHIP_TOKENS, D),
        ct.reshape(CHIP_TOKENS, D),
        attn_normed,
        mlp_normed,
        wq.reshape(D, 1536),
        wd.reshape(512, D),
        wh.reshape(D, 2048),
        wo.reshape(2048, D),
        vectors,
        cosine,
        sine,
    )
    hidden, output, qkv, dense, outputs, input_grad, *vectors = finals(
        *gathered, outputs, input_grad, sums
    )
    ag, ab, mg, mb, qb, db, hb = (v.reshape(v.shape[1]) for v in vectors)
    return (outputs, input_grad, ag, ab, mg, mb, qkv, qb, dense, db, hidden, hb, output, db)


def solution(mesh):
    rows = P(("fsdp", "seq"), None)
    vector = P("fsdp")
    matrix = P("fsdp", None)
    shared = (vector,) * 4 + (matrix, vector) * 4
    return jax.shard_map(
        local,
        mesh=mesh,
        in_specs=(rows, rows, *shared),
        out_specs=(rows, rows, *shared),
        check_vma=False,
    )
```

```python
import functools
import math

import jax
import jax.numpy as jnp
import numpy as np
from jax import lax
from jax.experimental import pallas as pl
from jax.experimental.pallas import tpu as pltpu
from jax.sharding import PartitionSpec as P

D = 1024
FF = 4096
HEADS = 16
HEAD = 64
ROT = 16
CHIP_TOKENS = 512
FSDP = 8
CHIPS = 8

epsilon = 1e-05
F32 = jnp.float32
BF16 = jnp.bfloat16
NT = (((1,), (1,)), ((), ()))
TN = (((0,), (0,)), ((), ()))
MIB = 2**20
HBM = pl.BlockSpec(memory_space=pl.ANY)
VMEM = pl.BlockSpec(memory_space=pltpu.VMEM)


def place():
    f = lax.axis_index("fsdp")
    s = lax.axis_index("seq")
    return f, s, (f // 2, f % 2, s // 4, (s // 2) % 2, s % 2)


def device(y, z, x, core):
    return {"fsdp": y * 2 + z % 2, "seq": x * 4 + (z // 2) * 2 + core}


def barrier(devices):
    sem = pltpu.get_barrier_semaphore()
    for d in devices:
        pl.semaphore_signal(sem, inc=1, device_id=d, device_id_type=pl.DeviceIdType.MESH)
    pl.semaphore_wait(sem, len(devices))


def remote(src, dst, send, recv, target):
    return pltpu.make_async_remote_copy(
        src_ref=src,
        dst_ref=dst,
        send_sem=send,
        recv_sem=recv,
        device_id=target,
        device_id_type=pl.DeviceIdType.MESH,
    )


class Gather:
    def __init__(self, own, full, send, recv):
        f, s, (y, zl, px, zh, core) = place()
        z = zh * 2 + zl
        self.own, self.full, self.send, self.recv = own, full, send, recv
        self.yp = device((y + 1) % 4, z, px, core)
        self.ym = device((y + 3) % 4, z, px, core)
        self.zp = device(y, (z + 1) % 4, px, core)
        self.zm = device(y, (z + 3) % 4, px, core)
        self.f = f
        self.slots = [f, (f + 6) % 8, (f + 2) % 8, (f + 4) % 8]
        flip = f + 1 - 2 * zl
        self.far = [flip, (flip + 6) % 8, (flip + 2) % 8, (flip + 4) % 8]
        self.sends = []

    def neighbours(self):
        return [self.yp, self.ym, self.zp, self.zm]

    def started(self, src, dst, k, target):
        copy = remote(src, dst, self.send.at[k], self.recv.at[k], target)
        copy.start()
        self.sends.append(copy)

    def arrived(self, ref, k):
        remote(ref, ref, self.send.at[k], self.recv.at[k], self.yp).wait_recv()

    @staticmethod
    def part(ref, h):
        rows = ref.shape[0] // 2
        return ref.at[pl.ds(h * rows, rows)]

    def own_y(self):
        for n, (o, g) in enumerate(zip(self.own, self.full)):
            for k, h, target in ((0, 0, self.yp), (3, 1, self.ym), (2, 0, self.ym), (1, 1, self.yp)):
                self.started(self.part(o, h), self.part(g.at[self.f], h), 14 * n + k, target)

    def own_z(self):
        for n, (o, g) in enumerate(zip(self.own, self.full)):
            for k, h, target in ((6, 0, self.zp), (10, 1, self.zm)):
                self.started(self.part(o, h), self.part(g.at[self.f], h), 14 * n + k, target)

    def pass_on(self, n, k, slot, h, targets):
        ref = self.part(self.full[n].at[slot], h)
        self.arrived(ref, 14 * n + k)
        for kk, target in targets:
            self.started(ref, ref, 14 * n + kk, target)

    def near_y(self):
        for n in range(len(self.full)):
            self.pass_on(n, 0, self.slots[1], 0, [(4, self.yp)])
            self.pass_on(n, 3, self.slots[2], 1, [(5, self.ym)])

    def near_z(self):
        for n, g in enumerate(self.full):
            for k, slot, h, target in ((7, 1, 0, self.zp), (12, 2, 1, self.zm)):
                ref = self.part(g.at[self.slots[slot]], h)
                self.started(ref, ref, 14 * n + k, target)
            self.pass_on(n, 2, self.slots[2], 0, [(8, self.zp)])
            self.pass_on(n, 1, self.slots[1], 1, [(11, self.zm)])

    def opposite_y(self):
        for n, g in enumerate(self.full):
            self.arrived(self.part(g.at[self.slots[3]], 0), 14 * n + 4)
            self.arrived(self.part(g.at[self.slots[3]], 1), 14 * n + 5)

    def ends_z(self):
        for k, slot in ((0, self.f), (3, self.slots[3])):
            for n, g in enumerate(self.full):
                a, b = self.part(g.at[slot], 0), self.part(g.at[slot], 1)
                if k == 0:
                    a, b = self.part(self.own[n], 0), self.part(self.own[n], 1)
                at = g.at[slot]
                self.started(a, self.part(at, 0), 14 * n + 6 + k, self.zp)
                self.started(b, self.part(at, 1), 14 * n + 10 + k, self.zm)

    def sides_y(self):
        for n in range(len(self.full)):
            self.pass_on(n, 6, self.far[0], 0, [(7, self.yp), (8, self.ym)])
            self.pass_on(n, 10, self.far[0], 1, [(11, self.yp), (12, self.ym)])

    def finish_mixed(self):
        for n, g in enumerate(self.full):
            for k, slot, h in (
                (1, self.slots[1], 1),
                (2, self.slots[2], 0),
                (7, self.far[1], 0),
                (8, self.far[2], 0),
                (11, self.far[1], 1),
                (12, self.far[2], 1),
                (9, self.far[3], 0),
                (13, self.far[3], 1),
            ):
                self.arrived(self.part(g.at[slot], h), 14 * n + k)
        for copy in self.sends:
            copy.wait_send()

    def opposite(self):
        for n in range(len(self.full)):
            self.pass_on(n, 4, self.slots[3], 0, [(9, self.zp)])
            self.pass_on(n, 5, self.slots[3], 1, [(13, self.zm)])

    def finish(self):
        for n, g in enumerate(self.full):
            for j in range(4):
                self.arrived(self.part(g.at[self.far[j]], 0), 14 * n + 6 + j)
                self.arrived(self.part(g.at[self.far[j]], 1), 14 * n + 10 + j)
        for copy in self.sends:
            copy.wait_send()


def fold(op, a):
    result = a[:, :128]
    for j in range(128, a.shape[1], 128):
        result = op(result, a[:, j : j + 128])
    return result


def attention_kernel(
    qkv_w, dense_w, hidden_w, output_w, small, x, ct, cosine, sine,
    result_q, result_k, gh, go, wq_out, wd_out, x_out, ct_out, an_out, mn_out, vectors,
    raw_q, own_q, own_h, own_o, wq, wd, x_v, ct_v, an, mn, vec, norms, bias, tables, packed,
    hd, out_q, out_k, q_s, k_s, v_s, d_s, s_s, p_s, dk_s, dv_s, mx_s, l_s, o_s, dq_s,
    in_send, in_recv, out_send, out_recv, a_send, a_recv, g_send, g_recv, local_sem,
):
    f, s, (y, zl, px, zh, core) = place()
    me = s // 2
    B = CHIP_TOKENS
    n = CHIPS
    scale = 1.0 / math.sqrt(HEAD)
    sibling = device(y, zh * 2 + zl, px, 1 - core)
    others = [{"fsdp": (f + k) % 8, "seq": s} for k in range(1, 8)]
    zother = device(y, 2 * (1 - zh) + 1 - zl, px, core)

    def chip(j):
        return {"fsdp": f, "seq": j * 2 + core}

    greeted = others + [sibling, zother] + [chip((me + k) % n) for k in range(1, n)]
    entered = pltpu.get_barrier_semaphore()
    for d in greeted:
        pl.semaphore_signal(entered, inc=1, device_id=d, device_id_type=pl.DeviceIdType.MESH)

    def load(src, dst, k):
        copy = pltpu.make_async_copy(src, dst, local_sem.at[k])
        copy.start()
        return copy

    own_d = dense_w.at[pl.ds(pl.multiple_of(core * 64, 64), 64)]
    here = pl.ds(pl.multiple_of(me * B, B), B)
    load_q = load(qkv_w, raw_q, 0)
    loads = [
        load(own_d, wd.at[f], 1),
        load(x, x_v.at[core], 2),
        load(ct, ct_v.at[core], 3),
        load(small, vec.at[f], 4),
        load(cosine.at[here], tables.at[0], 5),
        load(sine.at[here], tables.at[1], 6),
    ]
    load_o = load(output_w.at[pl.ds(pl.multiple_of(core * 256, 256), 256)], own_o, 7)
    load_h = [
        load(
            hidden_w.at[:, pl.ds(pl.multiple_of(r * 512 + core * 256, 256), 256)],
            own_h.at[:, pl.ds(r * 256, 256)],
            8 + r,
        )
        for r in range(8)
    ]
    load_q.wait()
    low = lax.broadcasted_iota(jnp.int32, (128, 128), 1) < HEAD
    even = core == 0
    held = None
    for r in range(8):
        t0, t1, t2 = [raw_q[:, r * 384 + j * 128 : r * 384 + j * 128 + 128].astype(F32) for j in range(3)]
        t2 = pltpu.roll(t2, 64, 1)
        qk = jnp.where(even, t0, jnp.where(low, pltpu.roll(t1, 64, 1), t2))
        v = jnp.where(even, t1, t2)
        own_q[:, r * 128 : r * 128 + 128] = qk.astype(BF16)
        if r % 2 == 0:
            held = v
        else:
            at = 1024 + r // 2 * 128
            own_q[:, at : at + 128] = jnp.where(low, held, pltpu.roll(v, 64, 1)).astype(BF16)
    pl.semaphore_wait(entered, len(greeted))

    heads = Gather([own_q, own_d], [wq, wd], a_send, a_recv)
    units = Gather([own_h, own_o], [gh, go], g_send, g_recv)
    heads.own_y()
    heads.started(x, x_v.at[core], 28, sibling)
    heads.started(ct, ct_v.at[core], 29, sibling)
    for k in range(1, 8):
        heads.started(small, vec.at[f], 29 + k, others[k - 1])
    heads.own_z()
    wq[f] = own_q[...]

    for copy in loads:
        copy.wait()
    heads.arrived(x_v.at[1 - core], 28)
    for k in range(1, 8):
        heads.arrived(vec.at[(f + 8 - k) % 8], 29 + k)
    heads.near_y()
    for r in range(8):
        at = slice(r * 128, r * 128 + 128)
        norms[0:4, at] = vec[r, 0:4, :]
        bias[0:1, at] = vec[r, pl.ds(4 + core, 1), :]
    first = low[0:1, :]
    for pair in range(4):
        a, b = vec[2 * pair, 6:7, :], vec[2 * pair + 1, 6:7, :]
        v_even = jnp.where(first, a, pltpu.roll(b, 64, 1))
        v_odd = jnp.where(first, pltpu.roll(a, 64, 1), b)
        at = slice(1024 + pair * 128, 1152 + pair * 128)
        bias[0:1, at] = jnp.where(even, v_even, v_odd)
    for c in range(2):
        rows = slice(c * 256, c * 256 + 256)
        normed, _ = normalised(x_v[c])
        an[rows, :] = (normed * norms[0:1, :] + norms[1:2, :]).astype(BF16)
        mn[rows, :] = (normed * norms[2:3, :] + norms[3:4, :]).astype(BF16)
        if c == 0:
            heads.near_z()
    heads.opposite()
    heads.arrived(ct_v.at[1 - core], 29)
    load_o.wait()
    for copy in load_h:
        copy.wait()
    units.own_y()
    heads.finish()

    def given(j):
        return remote(packed.at[j], hd.at[me], in_send.at[j], in_recv.at[me], chip(j))

    wide = lax.broadcasted_iota(jnp.int32, (B, 128), 1) < HEAD
    rotary = (tables[0], tables[1])
    tokens = ct_v[...].reshape(B, D)

    def project(t, _):
        pair = (px + 1 + t) % 4
        a = an[...]
        qk = pl.ds(pl.multiple_of(pair * 256, 256), 256)
        vs = pl.ds(pl.multiple_of(1024 + pair * 128, 128), 128)
        weight = wq[:, :, qk].reshape(D, 256)
        projected = jnp.dot(a, weight, preferred_element_type=F32) + bias[0:1, qk]
        for j in range(2):
            turned = turn(projected[:, j * 128 : j * 128 + 128], rotary, 1.0)
            packed[2 * pair + j, :, 0:128] = turned.astype(BF16)
        weight = wq[:, :, vs].reshape(D, 128)
        v = jnp.dot(a, weight, preferred_element_type=F32) + bias[0:1, vs]
        weight = wd[pl.ds(2 * pair, 2)].reshape(128, D)
        d = lax.dot_general(tokens, weight, NT, preferred_element_type=F32)
        packed[2 * pair, :, 128:256] = jnp.where(wide, v, pltpu.roll(d, 64, 1)).astype(BF16)
        packed[2 * pair + 1, :, 128:256] = jnp.where(wide, pltpu.roll(v, 64, 1), d).astype(BF16)
        for j in range(2):

            @pl.when(2 * pair + j != me)
            def _():
                given(2 * pair + j).start()

        return 0

    lax.fori_loop(0, 4, project, 0)
    hd[me] = packed[me]
    units.near_y()
    saves = [
        load(a, b, 16 + k)
        for k, (a, b) in enumerate(
            [
                (own_h, gh.at[f]),
                (own_o, go.at[f]),
                (wq, wq_out),
                (wd, wd_out),
                (x_v, x_out),
                (ct_v, ct_out),
                (an, an_out),
                (mn, mn_out),
                (vec, vectors),
            ]
        )
    ]
    for k in range(1, n):
        j = (me + n - k) % n
        remote(hd.at[j], hd.at[j], in_send.at[j], in_recv.at[j], chip(j)).wait_recv()
    units.opposite_y()
    units.ends_z()

    def block(i):
        return pl.ds(pl.multiple_of(i * B, B), B)

    def prepare(i, _):
        rows = block(i)
        piece = hd[i]
        q_s[rows, :] = piece[:, 0:64] * jnp.asarray(scale, BF16)
        k_s[rows, :] = piece[:, 64:128]
        v_s[rows, :] = piece[:, 128:192]
        d_s[rows, :] = piece[:, 192:256]
        return 0

    lax.fori_loop(0, n, prepare, 0)
    dk_s[...] = jnp.zeros_like(dk_s)
    dv_s[...] = jnp.zeros_like(dv_s)
    keep = lax.broadcasted_iota(jnp.int32, (B, B), 1) <= lax.broadcasted_iota(
        jnp.int32, (B, B), 0
    )

    def back_to(i, h):
        src, dst = (out_q, result_q) if h == 0 else (out_k, result_k)
        return remote(
            src.at[i], dst.at[me], out_send.at[8 * h + i], out_recv.at[8 * h + me], chip(i)
        )

    def keep_own(h):
        src, dst = (out_q, result_q) if h == 0 else (out_k, result_k)
        return pltpu.make_async_copy(src.at[me], dst.at[me], local_sem.at[25 + h])

    def in_pairs(count, body):
        def pair(k, _):
            body(2 * k)
            body(2 * k + 1)
            return 0

        def single(k, _):
            body(k)
            return 0

        lax.fori_loop(0, count // 2, pair, 0)
        lax.fori_loop(count // 2 * 2, count, single, 0)

    def query_block(t, _):
        i = (me + 1 + t) % n
        rows = block(i)
        qi = q_s[rows, :]
        mx_s[...] = jnp.full(mx_s.shape, -1e30, F32)

        def score(kb):
            return lax.dot_general(qi, k_s[block(kb), :], NT, preferred_element_type=F32)

        def first(kb):
            scores = score(kb)
            s_s[kb] = scores
            mx_s[...] = jnp.maximum(mx_s[...], fold(jnp.maximum, scores))

        in_pairs(i, first)
        scores = jnp.where(keep, score(i), -1e30)
        s_s[i] = scores
        row_max = jnp.max(
            jnp.maximum(mx_s[...], fold(jnp.maximum, scores)), axis=1, keepdims=True
        )
        l_s[...] = jnp.zeros_like(l_s)
        o_s[...] = jnp.zeros_like(o_s)
        dq_s[...] = jnp.zeros_like(dq_s)

        def second(kb):
            p = jnp.exp(s_s[kb] - row_max)
            l_s[...] += fold(jnp.add, p)
            pb = p.astype(BF16)
            p_s[kb] = pb
            o_s[...] += jnp.dot(pb, v_s[block(kb), :], preferred_element_type=F32)

        in_pairs(i + 1, second)
        inverse = 1.0 / jnp.sum(l_s[...], axis=1, keepdims=True)
        o = o_s[...] * inverse
        d = (d_s[rows, :].astype(F32) * inverse).astype(BF16)
        delta = jnp.sum(o * d.astype(F32), axis=1, keepdims=True)
        q_t = qi.T
        d_t = d.T

        def third(kb):
            cols = block(kb)
            pb = p_s[kb]
            dp = lax.dot_general(d, v_s[cols, :], NT, preferred_element_type=F32)
            ds = (pb.astype(F32) * (dp - delta)).astype(BF16)
            dq_s[...] += jnp.dot(ds, k_s[cols, :], preferred_element_type=F32)
            dk_s[:, cols] += jnp.dot(q_t, ds, preferred_element_type=F32)
            dv_s[:, cols] += jnp.dot(d_t, pb, preferred_element_type=F32)

        in_pairs(i + 1, third)
        out_q[i, :, 0:64] = (dq_s[...] * scale).astype(BF16)
        out_q[i, :, 64:128] = o.astype(BF16)

        @pl.when(i != me)
        def _():
            back_to(i, 0).start()

        return 0

    def key_block(t, _):
        i = (me + 1 + t) % n
        rows = block(i)
        out_k[i, :, 0:64] = dv_s[:, rows].T.astype(BF16)
        out_k[i, :, 64:128] = dk_s[:, rows].T.astype(BF16)

        @pl.when(i != me)
        def _():
            back_to(i, 1).start()

        return 0

    lax.fori_loop(0, 3, query_block, 0)
    units.sides_y()
    lax.fori_loop(3, n, query_block, 0)

    lax.fori_loop(0, n, key_block, 0)
    keep_own(0).start()
    keep_own(1).start()

    for k in range(1, n):
        given((me + k) % n).wait_send()
    for copy in saves:
        copy.wait()
    units.finish_mixed()
    for h, result in enumerate((result_q, result_k)):
        for k in range(1, n):
            back_to((me + k) % n, h).wait_send()
        keep_own(h).wait()
        for k in range(1, n):
            j = (me + k) % n
            ref = result.at[j]
            remote(ref, ref, out_send.at[8 * h + j], out_recv.at[8 * h + j], chip(me)).wait_recv()


def attention(*args):
    B = CHIP_TOKENS
    L = CHIPS * B

    def shape(*dims):
        return jax.ShapeDtypeStruct(dims, BF16)

    return pl.pallas_call(
        attention_kernel,
        out_shape=(
            shape(CHIPS, B, 2 * HEAD),
            shape(CHIPS, B, 2 * HEAD),
            shape(8, 128, 2048),
            shape(8, 256, 1024),
            shape(8, 128, 1536),
            shape(8, 64, 1024),
            shape(2, 256, D),
            shape(2, 256, D),
            shape(B, D),
            shape(B, D),
            jax.ShapeDtypeStruct((8, 16, 128), F32),
        ),
        in_specs=[HBM] * 9,
        out_specs=(HBM,) * 11,
        scratch_shapes=[
            pltpu.VMEM((128, 3072), BF16),
            pltpu.VMEM((128, 1536), BF16),
            pltpu.VMEM((128, 2048), BF16),
            pltpu.VMEM((256, 1024), BF16),
            pltpu.VMEM((8, 128, 1536), BF16),
            pltpu.VMEM((8, 64, 1024), BF16),
            *[pltpu.VMEM((2, 256, D), BF16)] * 2,
            *[pltpu.VMEM((B, D), BF16)] * 2,
            pltpu.VMEM((8, 16, 128), F32),
            pltpu.VMEM((8, D), F32),
            pltpu.VMEM((8, 1536), F32),
            pltpu.VMEM((2, B, 128), F32),
            *[pltpu.VMEM((CHIPS, B, 4 * HEAD), BF16)] * 2,
            *[pltpu.VMEM((CHIPS, B, 2 * HEAD), BF16)] * 2,
            *[pltpu.VMEM((L, HEAD), BF16)] * 4,
            pltpu.VMEM((L // B, B, B), F32),
            pltpu.VMEM((L // B, B, B), BF16),
            *[pltpu.VMEM((HEAD, L), F32)] * 2,
            *[pltpu.VMEM((B, 128), F32)] * 2,
            *[pltpu.VMEM((B, HEAD), F32)] * 2,
            *[pltpu.SemaphoreType.DMA((CHIPS,))] * 2,
            *[pltpu.SemaphoreType.DMA((2 * CHIPS,))] * 2,
            *[pltpu.SemaphoreType.DMA((37,))] * 2,
            *[pltpu.SemaphoreType.DMA((28,))] * 2,
            pltpu.SemaphoreType.DMA((27,)),
        ],
        compiler_params=pltpu.CompilerParams(
            collective_id=1, has_side_effects=True, vmem_limit_bytes=60 * MIB
        ),
    )(*args)


ORDERS = ("yzx", "zxy", "xyz")
LEADS = ((2, 4), (2, 4), (4, 2))
ROWS = (16, 32, 16)
COLUMNS = (2048, 1024, 2048)


def chunk(n, stage, g, t, h, where):
    y, zl, zh, px = where
    if stage == 0:
        if n == 0:
            return g.at[t, h]
        if n == 1:
            return g.at[pl.ds(2 * h, 2), t % 2, t // 2]
        return g.at[:, h, :, t]
    if stage == 1:
        return (g.at[y, t % 2, t // 2], g.at[:, zl, zh, t], g.at[t, :, :, px])[n]
    return (g.at[y, zl, zh, t], g.at[t, zl, zh, px], g.at[y, t % 2, t // 2, px])[n]


def add_into(dst, terms):
    lead = tuple(dst.shape[:-2])

    def body(k, _):
        at = []
        for extent in reversed(lead):
            at.insert(0, k % extent)
            k = k // extent
        at = (*at, slice(None), slice(None))
        total = dst[at].astype(F32)
        for t in terms:
            total = total + t[at].astype(F32)
        dst[at] = total.astype(BF16)
        return 0

    lax.fori_loop(0, math.prod(lead), body, 0)


def normalised(values):
    values = values.astype(F32)
    centered = values - jnp.mean(values, axis=-1, keepdims=True)
    variance = jnp.mean(centered * centered, axis=-1, keepdims=True)
    scale = lax.rsqrt(variance + epsilon)
    return centered * scale, scale


def rest_kernel(
    tokens_q, tokens_k, x, ct, an, mn, wq, wd, wh, wo, vec, cosine, sine,
    outputs, input_grad, gathered0, gathered1, gathered2, small_out,
    tables, norms, unit_bias, x_v, ct_v, an_v, branches, weighted, sums, small, sm_a, sm_b, pair_send, pair_recv,
    g0, g1, g2, *rest,
):
    grads = (g0, g1, g2)
    gathered = (gathered0, gathered1, gathered2)
    bufs = [(*rest[4 * n : 4 * n + 4], gathered[n]) for n in range(3)]
    wq_v, wd_v, tq_v, tk_v, pg_v, at_v, wh_v, wo_v, act_v, hg_v, turned_v = rest[12:23]
    send, recv, local_sem, sm_send, sm_recv = rest[23:]
    f, s, (y, zl, px, zh, core) = place()
    z = zh * 2 + zl
    coordinate = {"y": y, "z": z, "x": px}
    where = (y, zl, zh, px)
    T = CHIP_TOKENS

    def along(axis, step):
        t = dict(coordinate)
        t[axis] = (t[axis] + step) % 4
        return device(t["y"], t["z"], t["x"], core)

    plus = {a: along(a, 1) for a in "yzx"}
    minus = {a: along(a, 3) for a in "yzx"}
    same_seq = [{"fsdp": (f + k) % 8, "seq": s} for k in range(1, 8)]
    same_fsdp = [{"fsdp": f, "seq": (s + k) % 16} for k in range(1, 16)]
    zother = device(y, 2 * (1 - zh) + 1 - zl, px, core)
    sibling = device(y, z, px, 1 - core)
    sends = []

    def load(src, dst, k):
        copy = pltpu.make_async_copy(src, dst, local_sem.at[k])
        copy.start()
        return copy

    def started(src, dst, k, target):
        copy = remote(src, dst, send.at[k], recv.at[k], target)
        copy.start()
        sends.append(copy)

    def arrived(ref, k):
        remote(ref, ref, send.at[k], recv.at[k], sibling).wait_recv()

    def small_sent(src, dst, k, target):
        copy = remote(src, dst, sm_send.at[k], sm_recv.at[k], target)
        copy.start()
        sends.append(copy)

    def small_arrived(ref, k):
        remote(ref, ref, sm_send.at[k], sm_recv.at[k], sibling).wait_recv()

    def raw_copies(n, stage):
        axis = ORDERS[n][stage]
        p = coordinate[axis]

        def copy(t, h, dst, k, target):
            src = chunk(n, stage, grads[n], t % 4, h, where)
            return remote(src, dst, send.at[k], recv.at[k], target)

        if stage > 0:
            b, got = 26 * n + 3 + 3 * stage, bufs[n][1 + stage]
            return [
                copy(p + k, 0, got.at[k - 1], b + k - 1, along(axis, k)) for k in (2, 1, 3)
            ]
        opp, fin = bufs[n][0:2]
        b = 26 * n
        return [
            copy(p + 2, 0, opp.at[0], b, plus[axis]),
            copy(p + 2, 1, opp.at[1], b + 1, minus[axis]),
            copy(p + 1, 1, fin.at[0, 1], b + 2, plus[axis]),
            copy(p + 3, 0, fin.at[1, 0], b + 3, minus[axis]),
        ]

    def relay_copy(n, h):
        axis = ORDERS[n][0]
        k = 26 * n + 4 + h
        t = coordinate[axis] + 1 + 2 * h
        src = chunk(n, 0, grads[n], t % 4, h, where)
        target = (plus, minus)[h][axis]
        return src, remote(src, bufs[n][1].at[h, h], send.at[k], recv.at[k], target)

    def begin(n, stage):
        for copy in raw_copies(n, stage):
            copy.start()

    def relay(n):
        opp = bufs[n][0]
        for h in range(2):
            mid, copy = relay_copy(n, h)
            arrived(opp.at[h], 26 * n + h)
            add_into(mid, [opp.at[h]])
            copy.start()

    def finish(n, stage):
        p = coordinate[ORDERS[n][stage]]
        if stage > 0:
            b, got = 26 * n + 3 + 3 * stage, bufs[n][1 + stage]
            for k in range(3):
                arrived(got.at[k], b + k)
            mine = chunk(n, stage, grads[n], p, 0, where)
            add_into(mine, [got.at[k] for k in range(3)])
            return
        fin = bufs[n][1]
        b = 26 * n
        arrived(fin.at[0, 1], b + 2)
        arrived(fin.at[1, 0], b + 3)
        arrived(fin.at[0, 0], b + 4)
        arrived(fin.at[1, 1], b + 5)
        for h in range(2):
            add_into(chunk(n, 0, grads[n], p, h, where), [fin.at[0, h], fin.at[1, h]])

    here = pl.ds(pl.multiple_of((px * 2 + zh) * T, T), T)
    pairs = [
        (tokens_q, tq_v),
        (tokens_k, tk_v),
        (cosine.at[here], tables.at[0]),
        (sine.at[here], tables.at[1]),
        (an, an_v),
        (ct, ct_v),
        (wh, wh_v),
        (wo, wo_v),
        (x, x_v),
        (wq, wq_v),
        (wd, wd_v),
    ]
    keeps = [load(a, b, k) for k, (a, b) in enumerate(pairs)]
    barrier(same_seq + same_fsdp + [zother])
    small[...] = jnp.zeros_like(small)
    for r in range(8):
        at = slice(r * 128, r * 128 + 128)
        norms[0:4, at] = vec[r, 0:4, :]
        norms[4:5, at] = vec[r, 7:8, :] + vec[r, 12:13, :]
        for j in range(2):
            unit_bias[0:1, r * 256 + j * 128 : r * 256 + j * 128 + 128] = vec[
                r, pl.ds(8 + 2 * core + j, 1), :
            ]

    def attention_part():
        for copy in keeps[0:6]:
            copy.wait()
        low = lax.broadcasted_iota(jnp.int32, (T, 128), 1) < HEAD
        first = lax.broadcasted_iota(jnp.int32, (1, 128), 1) < HEAD
        rotary = (tables[0], tables[1])
        for pair in range(4):
            for j in range(2):
                r = 2 * pair + j
                at = slice(r * 128, r * 128 + 128)
                qk = jnp.where(low, tq_v[r].astype(F32), tk_v[r].astype(F32))
                turned = turn(qk, rotary, -1.0).astype(BF16)
                pg_v[:, at] = turned
                small[r, pl.ds(4 + core, 1), :] = jnp.sum(turned.astype(F32), axis=0, keepdims=True)
            a, b = [
                jnp.where(low, tk_v[r].astype(F32), tq_v[r].astype(F32))
                for r in (2 * pair, 2 * pair + 1)
            ]
            v = jnp.where(low, a, pltpu.roll(b, 64, 1))
            pg_v[:, 1024 + pair * 128 : 1152 + pair * 128] = v.astype(BF16)
            total = jnp.sum(v, axis=0, keepdims=True)
            moved = jnp.sum(pltpu.roll(v, 64, 1), axis=0, keepdims=True)
            zero = jnp.zeros_like(total)
            at_low = (jnp.where(first, total, zero), jnp.where(first, moved, zero))
            at_high = (jnp.where(first, zero, moved), jnp.where(first, zero, total))
            for j in range(2):
                small[2 * pair + j, 6:7, :] = jnp.where(core == 0, at_low[j], at_high[j])
            o = jnp.where(low, pltpu.roll(a, 64, 1), b)
            at_v[:, pair * 128 : pair * 128 + 128] = o.astype(BF16)

        turned_v[0:D, :] = an_v[...].T
        load_mn = load(mn, an_v, 11)

        def qkv_columns(k, _):
            at = pl.ds(pl.multiple_of(k * 512, 512), 512)
            part = jnp.dot(turned_v[0:D, :], pg_v[:, at], preferred_element_type=F32)
            g2[:, :, :, :, :, at] = part.astype(BF16).reshape(4, 2, 2, 4, 16, 512)
            return 0

        lax.fori_loop(0, 3, qkv_columns, 0)
        turned_v[0:512, :] = at_v[...].T
        for k in range(2):
            part = jnp.dot(
                turned_v[0:512, :], ct_v[:, k * 512 : k * 512 + 512], preferred_element_type=F32
            )
            g2[:, :, k, :, :, 1536:2048] = part.astype(BF16).reshape(4, 2, 4, 16, 512)
        begin(2, 0)
        return load_mn

    def attention_rows():
        for copy in keeps[8:11]:
            copy.wait()
        sums[...] = jnp.zeros_like(sums)

        def half(c, _):
            rows = pl.ds(pl.multiple_of(c * 256, 256), 256)
            grad = lax.dot_general(pg_v[rows, :], wq_v[...], NT, preferred_element_type=F32)
            normed, _ = normalised(x_v[rows, :])
            sums[0:1, :] += jnp.sum(grad * normed, axis=0, keepdims=True)
            sums[1:2, :] += jnp.sum(grad, axis=0, keepdims=True)
            weighted[rows, :] = grad * norms[0:1, :]
            branches[rows, :] = jnp.dot(at_v[rows, :], wd_v[...], preferred_element_type=F32)
            return 0

        lax.fori_loop(0, 2, half, 0)

    def unit_part(load_mn):
        load_mn.wait()
        for copy in keeps[6:8]:
            copy.wait()

        def units(r, _):
            at = pl.ds(pl.multiple_of(r * 256, 256), 256)
            h = jnp.dot(an_v[...], wh_v[:, at], preferred_element_type=F32) + unit_bias[0:1, at]
            below = 0.5 + 0.5 * lax.erf(h * math.sqrt(0.5))
            density = jnp.exp(-0.5 * h * h) * (1.0 / math.sqrt(2.0 * math.pi))
            act_v[:, at] = (h * below).astype(BF16)
            up = lax.dot_general(ct_v[...], wo_v[at, :], NT, preferred_element_type=F32)
            grad = (up * (below + h * density)).astype(BF16)
            hg_v[:, at] = grad
            total = jnp.sum(grad.astype(F32), axis=0, keepdims=True)
            small[r, pl.ds(8 + 2 * core, 1), :] = total[:, 0:128]
            small[r, pl.ds(9 + 2 * core, 1), :] = total[:, 128:256]
            return 0

        lax.fori_loop(0, 8, units, 0)
        turned_v[...] = act_v[...].T

        def output_rows(k, _):
            at = pl.ds(pl.multiple_of(k * 512, 512), 512)
            part = jnp.dot(turned_v[at, :], ct_v[...], preferred_element_type=F32)
            g1[k] = part.astype(BF16).reshape(2, 2, 4, 32, 1024)
            return 0

        lax.fori_loop(0, 4, output_rows, 0)
        begin(1, 0)
        turned_v[0:D, :] = an_v[...].T

        def hidden_columns(k, _):
            at = pl.ds(pl.multiple_of(k * 512, 512), 512)
            part = jnp.dot(turned_v[0:D, :], hg_v[:, at], preferred_element_type=F32)
            g0[:, :, :, :, :, at] = part.astype(BF16).reshape(4, 2, 2, 4, 16, 512)
            return 0

        lax.fori_loop(0, 4, hidden_columns, 0)
        begin(0, 0)

    def unit_rows():
        def half(c, _):
            rows = pl.ds(pl.multiple_of(c * 256, 256), 256)
            grad = lax.dot_general(hg_v[rows, :], wh_v[...], NT, preferred_element_type=F32)
            normed, _ = normalised(x_v[rows, :])
            sums[2:3, :] += jnp.sum(grad * normed, axis=0, keepdims=True)
            sums[3:4, :] += jnp.sum(grad, axis=0, keepdims=True)
            weighted[rows, :] += grad * norms[2:3, :]
            branches[rows, :] += jnp.dot(act_v[rows, :], wo_v[...], preferred_element_type=F32)
            return 0

        lax.fori_loop(0, 2, half, 0)

    unit_part(attention_part())
    relay(2)
    attention_rows()
    unit_rows()

    other = pl.ds(pl.multiple_of((1 - core) * 256, 256), 256)
    mine = pl.ds(pl.multiple_of(core * 256, 256), 256)
    pair_send[0] = branches[other, :].astype(BF16)
    pair_send[1] = weighted[other, :].astype(BF16)
    started(pair_send, pair_recv, 78, sibling)
    sums[4:5, :] = jnp.sum(ct_v[mine, :].astype(F32), axis=0, keepdims=True)
    for r in range(8):
        at = slice(r * 128, r * 128 + 128)
        small[r, 0:4, :] = sums[0:4, at]
        small[r, 7:8, :] = sums[4:5, at]
    for k in range(1, 8):
        small_sent(small.at[(f + k) % 8], sm_a.at[k], k, same_seq[k - 1])
    relay(1)
    relay(0)
    arrived(pair_recv, 78)
    normed, scale = normalised(x_v[mine, :])
    total = x_v[mine, :].astype(F32) + branches[mine, :] + pair_recv[0].astype(F32) + norms[4:5, :]
    outputs[...] = total.astype(BF16)
    w = weighted[mine, :] + pair_recv[1].astype(F32)
    input_grad[...] = ct_v[mine, :].astype(F32) + scale * (
        w
        - jnp.mean(w, axis=-1, keepdims=True)
        - normed * jnp.mean(w * normed, axis=-1, keepdims=True)
    )
    for k in range(1, 8):
        small_arrived(sm_a.at[k], k)
    total = small[f]
    for k in range(1, 8):
        total = total + sm_a[k]
    sm_b[0] = total
    for k in range(1, 16):
        small_sent(sm_b.at[0], sm_b.at[k], 7 + k, same_fsdp[k - 1])

    across = device(y, (z + 2) % 4, px, core)
    xp, xm = plus["x"], minus["x"]

    def at_chip(n, zz, xx):
        return bufs[n][4].at[core, zz * 4 + xx % 4]

    def spread(n):
        b = 26 * n + 18
        done = grads[n].at[y, zl, zh, px]
        place_ = at_chip(n, zh, px)
        keep = pltpu.make_async_copy(done, place_, local_sem.at[12 + n])
        keep.start()
        started(done, place_, b, across)
        started(done, place_, b + 1, xp)
        started(done, place_, b + 2, xm)
        return keep

    def spread_on(n):
        b = 26 * n + 18
        theirs = at_chip(n, 1 - zh, px)
        arrived(theirs, b)
        started(theirs, theirs, b + 3, xp)
        started(theirs, theirs, b + 4, xm)
        left, right = at_chip(n, zh, px + 3), at_chip(n, 1 - zh, px + 1)
        arrived(left, b + 1)
        started(left, left, b + 5, xp)
        arrived(right, b + 4)
        started(right, right, b + 6, xm)

    def spread_end(n, keep):
        b = 26 * n + 18
        arrived(at_chip(n, zh, px + 1), b + 2)
        arrived(at_chip(n, 1 - zh, px + 3), b + 3)
        arrived(at_chip(n, zh, px + 2), b + 5)
        arrived(at_chip(n, 1 - zh, px + 2), b + 6)
        keep.wait()
        whole = bufs[n][4].at[core]
        started(whole, whole, b + 7, sibling)

    finish(2, 0)
    begin(2, 1)
    finish(1, 0)
    begin(1, 1)
    finish(0, 0)
    begin(0, 1)
    finish(2, 1)
    begin(2, 2)
    finish(1, 1)
    begin(1, 2)
    finish(0, 1)
    begin(0, 2)
    finish(2, 2)
    keep2 = spread(2)
    finish(1, 2)
    keep1 = spread(1)
    finish(0, 2)
    keep0 = spread(0)
    spread_on(2)
    spread_end(2, keep2)
    spread_on(1)
    spread_on(0)
    spread_end(1, keep1)
    spread_end(0, keep0)
    for k in range(1, 16):
        small_arrived(sm_b.at[k], 7 + k)
    total = sm_b[0]
    for k in range(1, 16):
        total = total + sm_b[k]
    small_out[...] = total

    for n in (2, 1, 0):
        arrived(gathered[n].at[1 - core], 26 * n + 25)
    for copy in sends:
        copy.wait_send()
    for n in range(3):
        for stage in range(3):
            for copy in raw_copies(n, stage):
                copy.wait_send()
        for h in range(2):
            relay_copy(n, h)[1].wait_send()


def rest_of_block(*args):
    scratch = []
    for lead, R, C in zip(LEADS, ROWS, COLUMNS):
        for dims in (
            (2, *lead, R, C),
            (2, 2, *lead, R, C),
            (3, *((2, 2) if lead == (4, 2) else (4,)), R, C),
            (3, R, C),
        ):
            scratch.append(pltpu.VMEM(dims, BF16))
    T = CHIP_TOKENS
    return pl.pallas_call(
        rest_kernel,
        out_shape=(
            jax.ShapeDtypeStruct((256, D), BF16),
            jax.ShapeDtypeStruct((256, D), F32),
            *[jax.ShapeDtypeStruct((2, 8, R, C), BF16) for R, C in zip(ROWS, COLUMNS)],
            jax.ShapeDtypeStruct((16, 128), F32),
        ),
        in_specs=[HBM] * 10 + [VMEM, HBM, HBM],
        out_specs=(VMEM, VMEM, HBM, HBM, HBM, VMEM),
        scratch_shapes=[
            pltpu.VMEM((2, T, 128), F32),
            pltpu.VMEM((8, D), F32),
            pltpu.VMEM((8, 2048), F32),
            *[pltpu.VMEM((T, D), BF16)] * 3,
            *[pltpu.VMEM((T, D), F32)] * 2,
            pltpu.VMEM((8, D), F32),
            pltpu.VMEM((8, 16, 128), F32),
            pltpu.VMEM((8, 16, 128), F32),
            pltpu.VMEM((16, 16, 128), F32),
            *[pltpu.VMEM((2, 256, D), BF16)] * 2,
            *[pltpu.VMEM((4, 2, 2, 4, R, C), BF16) for R, C in zip(ROWS, COLUMNS)],
            *scratch,
            pltpu.VMEM((D, 1536), BF16),
            pltpu.VMEM((512, D), BF16),
            *[pltpu.VMEM((8, T, 128), BF16)] * 2,
            pltpu.VMEM((T, 1536), BF16),
            pltpu.VMEM((T, 512), BF16),
            pltpu.VMEM((D, 2048), BF16),
            pltpu.VMEM((2048, D), BF16),
            *[pltpu.VMEM((T, 2048), BF16)] * 2,
            pltpu.VMEM((2048, T), BF16),
            pltpu.SemaphoreType.DMA((79,)),
            pltpu.SemaphoreType.DMA((79,)),
            pltpu.SemaphoreType.DMA((18,)),
            pltpu.SemaphoreType.DMA((23,)),
            pltpu.SemaphoreType.DMA((23,)),
        ],
        compiler_params=pltpu.CompilerParams(
            collective_id=2, has_side_effects=True, vmem_limit_bytes=62 * MIB
        ),
    )(*args)


def position_tables():
    half = ROT // 2
    frequency = np.power(10000.0, -2.0 * np.arange(half) / ROT).astype(np.float32)
    angles = np.arange(CHIPS * CHIP_TOKENS, dtype=np.float32)[:, None] * frequency[None, :]
    angles = angles.astype(np.float64)
    cosine = np.ones((CHIPS * CHIP_TOKENS, 2 * HEAD), np.float32)
    sine = np.zeros((CHIPS * CHIP_TOKENS, 2 * HEAD), np.float32)
    for at in (0, HEAD):
        cosine[:, at : at + half] = cosine[:, at + half : at + ROT] = np.cos(angles)
        sine[:, at : at + half] = -np.sin(angles)
        sine[:, at + half : at + ROT] = np.sin(angles)
    return cosine, sine


def turn(values, tables, sign):
    lane = lax.broadcasted_iota(jnp.int32, values.shape, 1) % HEAD
    moved = jnp.where(lane < ROT // 2, pltpu.roll(values, 120, 1), pltpu.roll(values, 8, 1))
    return values * tables[0] + sign * (moved * tables[1])


def finals_kernel(
    h0, h1, h2, out_in, grad_in, sums, hidden, output, qkv, dense, out_ref, grad_ref, *rest
):
    vectors, (a0, a1, a2, sem) = rest[:7], rest[7:]
    loads = [
        pltpu.make_async_copy(a, b, sem.at[k])
        for k, (a, b) in enumerate(
            [(h2, a2), (h0, a0), (h1, a1), (out_in, out_ref), (grad_in, grad_ref)]
        )
    ]
    for copy in loads:
        copy.start()
    loads[0].wait()
    low = lax.broadcasted_iota(jnp.int32, (128, 128), 1) < HEAD
    for pair in range(4):
        at = slice(1024 + pair * 128, 1152 + pair * 128)
        v0 = a2[0, :, :, at].reshape(128, 128).astype(F32)
        v1 = a2[1, :, :, at].reshape(128, 128).astype(F32)
        for j in range(2):
            r = 2 * pair + j
            q0 = a2[0, :, :, r * 128 : r * 128 + 128].reshape(128, 128).astype(F32)
            q1 = a2[1, :, :, r * 128 : r * 128 + 128].reshape(128, 128).astype(F32)
            q1 = pltpu.roll(q1, 64, 1)
            left = v0 if j == 0 else pltpu.roll(v0, 64, 1)
            right = pltpu.roll(v1, 64, 1) if j == 0 else v1
            qkv[:, r * 384 : r * 384 + 128] = q0
            qkv[:, r * 384 + 128 : r * 384 + 256] = jnp.where(low, left, q1)
            qkv[:, r * 384 + 256 : r * 384 + 384] = jnp.where(low, q1, right)
    for c in range(2):
        for k in range(2):
            piece = a2[c, k * 4 : k * 4 + 4, :, 1536:2048].reshape(64, 512)
            dense[c * 64 : c * 64 + 64, k * 512 : k * 512 + 512] = piece.astype(F32)
    loads[1].wait()
    for c in range(2):
        for r in range(8):
            piece = a0[c, :, :, r * 256 : r * 256 + 256].reshape(128, 256)
            hidden[:, r * 512 + c * 256 : r * 512 + c * 256 + 256] = piece.astype(F32)
    loads[2].wait()
    output[...] = a1[...].reshape(512, D).astype(F32)
    loads[3].wait()
    loads[4].wait()
    for k in range(4):
        vectors[k][...] = sums[k : k + 1, :]
    first = lax.broadcasted_iota(jnp.int32, (1, 128), 1) < HEAD
    q1 = pltpu.roll(sums[5:6, :], 64, 1)
    vectors[4][:, 0:128] = sums[4:5, :]
    vectors[4][:, 128:256] = jnp.where(first, sums[6:7, :], q1)
    vectors[4][:, 256:384] = jnp.where(first, q1, sums[6:7, :])
    vectors[5][...] = sums[7:8, :]
    for k in range(4):
        vectors[6][:, k * 128 : k * 128 + 128] = sums[8 + k : 9 + k, :]


def finals(a0, a1, a2, outputs, input_grad, sums):
    widths = (128, 128, 128, 128, 384, 128, 512)
    return pl.pallas_call(
        finals_kernel,
        out_shape=(
            jax.ShapeDtypeStruct((128, FF), F32),
            jax.ShapeDtypeStruct((512, D), F32),
            jax.ShapeDtypeStruct((128, 3 * D), F32),
            jax.ShapeDtypeStruct((128, D), F32),
            jax.ShapeDtypeStruct((256, D), BF16),
            jax.ShapeDtypeStruct((256, D), F32),
            *[jax.ShapeDtypeStruct((1, w), F32) for w in widths],
        ),
        in_specs=[HBM] * 5 + [VMEM],
        out_specs=(VMEM,) * 13,
        scratch_shapes=[
            *[pltpu.VMEM((2, 8, R, C), BF16) for R, C in zip(ROWS, COLUMNS)],
            pltpu.SemaphoreType.DMA((5,)),
        ],
        compiler_params=pltpu.CompilerParams(vmem_limit_bytes=60 * MIB),
    )(a0, a1, a2, outputs, input_grad, sums)


def local(
    inputs,
    cotangent,
    ln_attn_gain,
    ln_attn_bias,
    ln_mlp_gain,
    ln_mlp_bias,
    qkv_weight,
    qkv_bias,
    dense_weight,
    dense_bias,
    hidden_weight,
    hidden_bias,
    output_weight,
    output_bias,
):
    bias = qkv_bias.reshape(2, 192)
    small = jnp.zeros((16, 128), F32)
    for k, rows in (
        (0, ln_attn_gain),
        (1, ln_attn_bias),
        (2, ln_mlp_gain),
        (3, ln_mlp_bias),
        (4, bias[:, :128]),
        (6, bias[:, 128:]),
        (7, dense_bias),
        (8, hidden_bias),
        (12, output_bias),
    ):
        rows = rows.reshape(-1, 128).astype(F32)
        small = small + jnp.pad(rows, ((k, 16 - k - rows.shape[0]), (0, 0)))
    cosine, sine = (jnp.asarray(t) for t in position_tables())
    tokens_q, tokens_k, wh, wo, wq, wd, x, ct, attn_normed, mlp_normed, vectors = attention(
        qkv_weight,
        dense_weight,
        hidden_weight,
        output_weight,
        small,
        inputs,
        cotangent,
        cosine,
        sine,
    )
    outputs, input_grad, *gathered, sums = rest_of_block(
        tokens_q,
        tokens_k,
        x.reshape(CHIP_TOKENS, D),
        ct.reshape(CHIP_TOKENS, D),
        attn_normed,
        mlp_normed,
        wq.reshape(D, 1536),
        wd.reshape(512, D),
        wh.reshape(D, 2048),
        wo.reshape(2048, D),
        vectors,
        cosine,
        sine,
    )
    hidden, output, qkv, dense, outputs, input_grad, *vectors = finals(
        *gathered, outputs, input_grad, sums
    )
    ag, ab, mg, mb, qb, db, hb = (v.reshape(v.shape[1]) for v in vectors)
    return (outputs, input_grad, ag, ab, mg, mb, qkv, qb, dense, db, hidden, hb, output, db)


def solution(mesh):
    rows = P(("fsdp", "seq"), None)
    vector = P("fsdp")
    matrix = P("fsdp", None)
    shared = (vector,) * 4 + (matrix, vector) * 4
    return jax.shard_map(
        local,
        mesh=mesh,
        in_specs=(rows, rows, *shared),
        out_specs=(rows, rows, *shared),
        check_vma=False,
    )
```

```python
import functools
import math

import jax
import jax.numpy as jnp
import numpy as np
from jax import lax
from jax.experimental import pallas as pl
from jax.experimental.pallas import tpu as pltpu
from jax.sharding import PartitionSpec as P

D = 1024
FF = 4096
HEADS = 16
HEAD = 64
ROT = 16
CHIP_TOKENS = 512
FSDP = 8
CHIPS = 8

epsilon = 1e-05
F32 = jnp.float32
BF16 = jnp.bfloat16
NT = (((1,), (1,)), ((), ()))
TN = (((0,), (0,)), ((), ()))
MIB = 2**20
HBM = pl.BlockSpec(memory_space=pl.ANY)
VMEM = pl.BlockSpec(memory_space=pltpu.VMEM)


def place():
    f = lax.axis_index("fsdp")
    s = lax.axis_index("seq")
    return f, s, (f // 2, f % 2, s // 4, (s // 2) % 2, s % 2)


def device(y, z, x, core):
    return {"fsdp": y * 2 + z % 2, "seq": x * 4 + (z // 2) * 2 + core}


def barrier(devices):
    sem = pltpu.get_barrier_semaphore()
    for d in devices:
        pl.semaphore_signal(sem, inc=1, device_id=d, device_id_type=pl.DeviceIdType.MESH)
    pl.semaphore_wait(sem, len(devices))


def remote(src, dst, send, recv, target):
    return pltpu.make_async_remote_copy(
        src_ref=src,
        dst_ref=dst,
        send_sem=send,
        recv_sem=recv,
        device_id=target,
        device_id_type=pl.DeviceIdType.MESH,
    )


class Gather:
    def __init__(self, own, full, send, recv):
        f, s, (y, zl, px, zh, core) = place()
        z = zh * 2 + zl
        self.own, self.full, self.send, self.recv = own, full, send, recv
        self.yp = device((y + 1) % 4, z, px, core)
        self.ym = device((y + 3) % 4, z, px, core)
        self.zp = device(y, (z + 1) % 4, px, core)
        self.zm = device(y, (z + 3) % 4, px, core)
        self.f = f
        self.slots = [f, (f + 6) % 8, (f + 2) % 8, (f + 4) % 8]
        flip = f + 1 - 2 * zl
        self.far = [flip, (flip + 6) % 8, (flip + 2) % 8, (flip + 4) % 8]
        self.sends = []

    def neighbours(self):
        return [self.yp, self.ym, self.zp, self.zm]

    def started(self, src, dst, k, target):
        copy = remote(src, dst, self.send.at[k], self.recv.at[k], target)
        copy.start()
        self.sends.append(copy)

    def arrived(self, ref, k):
        remote(ref, ref, self.send.at[k], self.recv.at[k], self.yp).wait_recv()

    @staticmethod
    def part(ref, h):
        rows = ref.shape[0] // 2
        return ref.at[pl.ds(h * rows, rows)]

    def own_y(self):
        for n, (o, g) in enumerate(zip(self.own, self.full)):
            for k, h, target in ((0, 0, self.yp), (3, 1, self.ym), (2, 0, self.ym), (1, 1, self.yp)):
                self.started(self.part(o, h), self.part(g.at[self.f], h), 14 * n + k, target)

    def own_z(self):
        for n, (o, g) in enumerate(zip(self.own, self.full)):
            for k, h, target in ((6, 0, self.zp), (10, 1, self.zm)):
                self.started(self.part(o, h), self.part(g.at[self.f], h), 14 * n + k, target)

    def pass_on(self, n, k, slot, h, targets):
        ref = self.part(self.full[n].at[slot], h)
        self.arrived(ref, 14 * n + k)
        for kk, target in targets:
            self.started(ref, ref, 14 * n + kk, target)

    def near_y(self):
        for n in range(len(self.full)):
            self.pass_on(n, 0, self.slots[1], 0, [(4, self.yp)])
            self.pass_on(n, 3, self.slots[2], 1, [(5, self.ym)])

    def near_z(self):
        for n, g in enumerate(self.full):
            for k, slot, h, target in ((7, 1, 0, self.zp), (12, 2, 1, self.zm)):
                ref = self.part(g.at[self.slots[slot]], h)
                self.started(ref, ref, 14 * n + k, target)
            self.pass_on(n, 2, self.slots[2], 0, [(8, self.zp)])
            self.pass_on(n, 1, self.slots[1], 1, [(11, self.zm)])

    def opposite_y(self):
        for n, g in enumerate(self.full):
            self.arrived(self.part(g.at[self.slots[3]], 0), 14 * n + 4)
            self.arrived(self.part(g.at[self.slots[3]], 1), 14 * n + 5)

    def ends_z(self):
        for k, slot in ((0, self.f), (3, self.slots[3])):
            for n, g in enumerate(self.full):
                a, b = self.part(g.at[slot], 0), self.part(g.at[slot], 1)
                if k == 0:
                    a, b = self.part(self.own[n], 0), self.part(self.own[n], 1)
                at = g.at[slot]
                self.started(a, self.part(at, 0), 14 * n + 6 + k, self.zp)
                self.started(b, self.part(at, 1), 14 * n + 10 + k, self.zm)

    def sides_y(self):
        for n in range(len(self.full)):
            self.pass_on(n, 6, self.far[0], 0, [(7, self.yp), (8, self.ym)])
            self.pass_on(n, 10, self.far[0], 1, [(11, self.yp), (12, self.ym)])

    def finish_mixed(self):
        for n, g in enumerate(self.full):
            for k, slot, h in (
                (1, self.slots[1], 1),
                (2, self.slots[2], 0),
                (7, self.far[1], 0),
                (8, self.far[2], 0),
                (11, self.far[1], 1),
                (12, self.far[2], 1),
                (9, self.far[3], 0),
                (13, self.far[3], 1),
            ):
                self.arrived(self.part(g.at[slot], h), 14 * n + k)
        for copy in self.sends:
            copy.wait_send()

    def opposite(self):
        for n in range(len(self.full)):
            self.pass_on(n, 4, self.slots[3], 0, [(9, self.zp)])
            self.pass_on(n, 5, self.slots[3], 1, [(13, self.zm)])

    def finish(self):
        for n, g in enumerate(self.full):
            for j in range(4):
                self.arrived(self.part(g.at[self.far[j]], 0), 14 * n + 6 + j)
                self.arrived(self.part(g.at[self.far[j]], 1), 14 * n + 10 + j)
        for copy in self.sends:
            copy.wait_send()


def fold(op, a):
    result = a[:, :128]
    for j in range(128, a.shape[1], 128):
        result = op(result, a[:, j : j + 128])
    return result


def attention_kernel(
    qkv_w, dense_w, hidden_w, output_w, small, x, ct, cosine, sine,
    result_q, result_k, gh, go, wq_out, wd_out, x_out, ct_out, an_out, mn_out, vectors,
    raw_q, own_q, own_h, own_o, wq, wd, x_v, ct_v, an, mn, vec, norms, bias, tables, packed,
    hd, out_q, out_k, q_s, k_s, v_s, d_s, s_s, p_s, dk_s, dv_s, mx_s, l_s, o_s, dq_s,
    in_send, in_recv, out_send, out_recv, a_send, a_recv, g_send, g_recv, local_sem,
):
    f, s, (y, zl, px, zh, core) = place()
    me = s // 2
    B = CHIP_TOKENS
    n = CHIPS
    scale = 1.0 / math.sqrt(HEAD)
    sibling = device(y, zh * 2 + zl, px, 1 - core)
    others = [{"fsdp": (f + k) % 8, "seq": s} for k in range(1, 8)]
    zother = device(y, 2 * (1 - zh) + 1 - zl, px, core)

    def chip(j):
        return {"fsdp": f, "seq": j * 2 + core}

    greeted = others + [sibling, zother] + [chip((me + k) % n) for k in range(1, n)]
    entered = pltpu.get_barrier_semaphore()
    for d in greeted:
        pl.semaphore_signal(entered, inc=1, device_id=d, device_id_type=pl.DeviceIdType.MESH)

    def load(src, dst, k):
        copy = pltpu.make_async_copy(src, dst, local_sem.at[k])
        copy.start()
        return copy

    own_d = dense_w.at[pl.ds(pl.multiple_of(core * 64, 64), 64)]
    here = pl.ds(pl.multiple_of(me * B, B), B)
    load_q = load(qkv_w, raw_q, 0)
    loads = [
        load(own_d, wd.at[f], 1),
        load(x, x_v.at[core], 2),
        load(ct, ct_v.at[core], 3),
        load(small, vec.at[f], 4),
        load(cosine.at[here], tables.at[0], 5),
        load(sine.at[here], tables.at[1], 6),
    ]
    load_o = load(output_w.at[pl.ds(pl.multiple_of(core * 256, 256), 256)], own_o, 7)
    load_h = [
        load(
            hidden_w.at[:, pl.ds(pl.multiple_of(r * 512 + core * 256, 256), 256)],
            own_h.at[:, pl.ds(r * 256, 256)],
            8 + r,
        )
        for r in range(8)
    ]
    load_q.wait()
    low = lax.broadcasted_iota(jnp.int32, (128, 128), 1) < HEAD
    even = core == 0
    held = None
    for r in range(8):
        t0, t1, t2 = [raw_q[:, r * 384 + j * 128 : r * 384 + j * 128 + 128].astype(F32) for j in range(3)]
        t2 = pltpu.roll(t2, 64, 1)
        qk = jnp.where(even, t0, jnp.where(low, pltpu.roll(t1, 64, 1), t2))
        v = jnp.where(even, t1, t2)
        own_q[:, r * 128 : r * 128 + 128] = qk.astype(BF16)
        if r % 2 == 0:
            held = v
        else:
            at = 1024 + r // 2 * 128
            own_q[:, at : at + 128] = jnp.where(low, held, pltpu.roll(v, 64, 1)).astype(BF16)
    pl.semaphore_wait(entered, len(greeted))

    heads = Gather([own_q, own_d], [wq, wd], a_send, a_recv)
    units = Gather([own_h, own_o], [gh, go], g_send, g_recv)
    heads.own_y()
    heads.started(x, x_v.at[core], 28, sibling)
    heads.started(ct, ct_v.at[core], 29, sibling)
    for k in range(1, 8):
        heads.started(small, vec.at[f], 29 + k, others[k - 1])
    heads.own_z()
    wq[f] = own_q[...]

    for copy in loads:
        copy.wait()
    heads.arrived(x_v.at[1 - core], 28)
    for k in range(1, 8):
        heads.arrived(vec.at[(f + 8 - k) % 8], 29 + k)
    heads.near_y()
    for r in range(8):
        at = slice(r * 128, r * 128 + 128)
        norms[0:4, at] = vec[r, 0:4, :]
        bias[0:1, at] = vec[r, pl.ds(4 + core, 1), :]
    first = low[0:1, :]
    for pair in range(4):
        a, b = vec[2 * pair, 6:7, :], vec[2 * pair + 1, 6:7, :]
        v_even = jnp.where(first, a, pltpu.roll(b, 64, 1))
        v_odd = jnp.where(first, pltpu.roll(a, 64, 1), b)
        at = slice(1024 + pair * 128, 1152 + pair * 128)
        bias[0:1, at] = jnp.where(even, v_even, v_odd)
    for c in range(2):
        rows = slice(c * 256, c * 256 + 256)
        normed, _ = normalised(x_v[c])
        an[rows, :] = (normed * norms[0:1, :] + norms[1:2, :]).astype(BF16)
        mn[rows, :] = (normed * norms[2:3, :] + norms[3:4, :]).astype(BF16)
        if c == 0:
            heads.near_z()
    heads.opposite()
    heads.arrived(ct_v.at[1 - core], 29)
    load_o.wait()
    for copy in load_h:
        copy.wait()
    units.own_y()
    heads.finish()

    def given(j):
        return remote(packed.at[j], hd.at[me], in_send.at[j], in_recv.at[me], chip(j))

    wide = lax.broadcasted_iota(jnp.int32, (B, 128), 1) < HEAD
    rotary = (tables[0], tables[1])
    tokens = ct_v[...].reshape(B, D)

    def project(t, _):
        pair = (px + 1 + t) % 4
        a = an[...]
        qk = pl.ds(pl.multiple_of(pair * 256, 256), 256)
        vs = pl.ds(pl.multiple_of(1024 + pair * 128, 128), 128)
        weight = wq[:, :, qk].reshape(D, 256)
        projected = jnp.dot(a, weight, preferred_element_type=F32) + bias[0:1, qk]
        for j in range(2):
            turned = turn(projected[:, j * 128 : j * 128 + 128], rotary, 1.0)
            packed[2 * pair + j, :, 0:128] = turned.astype(BF16)
        weight = wq[:, :, vs].reshape(D, 128)
        v = jnp.dot(a, weight, preferred_element_type=F32) + bias[0:1, vs]
        weight = wd[pl.ds(2 * pair, 2)].reshape(128, D)
        d = lax.dot_general(tokens, weight, NT, preferred_element_type=F32)
        packed[2 * pair, :, 128:256] = jnp.where(wide, v, pltpu.roll(d, 64, 1)).astype(BF16)
        packed[2 * pair + 1, :, 128:256] = jnp.where(wide, pltpu.roll(v, 64, 1), d).astype(BF16)
        for j in range(2):

            @pl.when(2 * pair + j != me)
            def _():
                given(2 * pair + j).start()

        return 0

    lax.fori_loop(0, 4, project, 0)
    hd[me] = packed[me]
    units.near_y()
    saves = [
        load(a, b, 16 + k)
        for k, (a, b) in enumerate(
            [
                (own_h, gh.at[f]),
                (own_o, go.at[f]),
                (wq, wq_out),
                (wd, wd_out),
                (x_v, x_out),
                (ct_v, ct_out),
                (an, an_out),
                (mn, mn_out),
                (vec, vectors),
            ]
        )
    ]
    for k in range(1, n):
        j = (me + n - k) % n
        remote(hd.at[j], hd.at[j], in_send.at[j], in_recv.at[j], chip(j)).wait_recv()
    units.opposite_y()
    units.ends_z()

    def block(i):
        return pl.ds(pl.multiple_of(i * B, B), B)

    def prepare(i, _):
        rows = block(i)
        piece = hd[i]
        q_s[rows, :] = piece[:, 0:64] * jnp.asarray(scale, BF16)
        k_s[rows, :] = piece[:, 64:128]
        v_s[rows, :] = piece[:, 128:192]
        d_s[rows, :] = piece[:, 192:256]
        return 0

    lax.fori_loop(0, n, prepare, 0)
    dk_s[...] = jnp.zeros_like(dk_s)
    dv_s[...] = jnp.zeros_like(dv_s)
    keep = lax.broadcasted_iota(jnp.int32, (B, B), 1) <= lax.broadcasted_iota(
        jnp.int32, (B, B), 0
    )

    def back_to(i, h):
        src, dst = (out_q, result_q) if h == 0 else (out_k, result_k)
        return remote(
            src.at[i], dst.at[me], out_send.at[8 * h + i], out_recv.at[8 * h + me], chip(i)
        )

    def keep_own(h):
        src, dst = (out_q, result_q) if h == 0 else (out_k, result_k)
        return pltpu.make_async_copy(src.at[me], dst.at[me], local_sem.at[25 + h])

    def in_pairs(count, body):
        def pair(k, _):
            body(2 * k)
            body(2 * k + 1)
            return 0

        def single(k, _):
            body(k)
            return 0

        lax.fori_loop(0, count // 2, pair, 0)
        lax.fori_loop(count // 2 * 2, count, single, 0)

    def query_block(t, _):
        i = (me + 1 + t) % n
        rows = block(i)
        qi = q_s[rows, :]
        mx_s[...] = jnp.full(mx_s.shape, -1e30, F32)

        def score(kb):
            return lax.dot_general(qi, k_s[block(kb), :], NT, preferred_element_type=F32)

        def first(kb):
            scores = score(kb)
            s_s[kb] = scores
            mx_s[...] = jnp.maximum(mx_s[...], fold(jnp.maximum, scores))

        in_pairs(i, first)
        scores = jnp.where(keep, score(i), -1e30)
        s_s[i] = scores
        row_max = jnp.max(
            jnp.maximum(mx_s[...], fold(jnp.maximum, scores)), axis=1, keepdims=True
        )
        l_s[...] = jnp.zeros_like(l_s)
        o_s[...] = jnp.zeros_like(o_s)
        dq_s[...] = jnp.zeros_like(dq_s)

        def second(kb):
            p = jnp.exp(s_s[kb] - row_max)
            l_s[...] += fold(jnp.add, p)
            pb = p.astype(BF16)
            p_s[kb] = pb
            o_s[...] += jnp.dot(pb, v_s[block(kb), :], preferred_element_type=F32)

        in_pairs(i + 1, second)
        inverse = 1.0 / jnp.sum(l_s[...], axis=1, keepdims=True)
        o = o_s[...] * inverse
        d = (d_s[rows, :].astype(F32) * inverse).astype(BF16)
        delta = jnp.sum(o * d.astype(F32), axis=1, keepdims=True)
        q_t = qi.T
        d_t = d.T

        def third(kb):
            cols = block(kb)
            pb = p_s[kb]
            dp = lax.dot_general(d, v_s[cols, :], NT, preferred_element_type=F32)
            ds = (pb.astype(F32) * (dp - delta)).astype(BF16)
            dq_s[...] += jnp.dot(ds, k_s[cols, :], preferred_element_type=F32)
            dk_s[:, cols] += jnp.dot(q_t, ds, preferred_element_type=F32)
            dv_s[:, cols] += jnp.dot(d_t, pb, preferred_element_type=F32)

        in_pairs(i + 1, third)
        out_q[i, :, 0:64] = (dq_s[...] * scale).astype(BF16)
        out_q[i, :, 64:128] = o.astype(BF16)

        @pl.when(i != me)
        def _():
            back_to(i, 0).start()

        return 0

    def key_block(t, _):
        i = (me + 1 + t) % n
        rows = block(i)
        out_k[i, :, 0:64] = dv_s[:, rows].T.astype(BF16)
        out_k[i, :, 64:128] = dk_s[:, rows].T.astype(BF16)

        @pl.when(i != me)
        def _():
            back_to(i, 1).start()

        return 0

    lax.fori_loop(0, 3, query_block, 0)
    units.sides_y()
    lax.fori_loop(3, n, query_block, 0)

    lax.fori_loop(0, n, key_block, 0)
    keep_own(0).start()
    keep_own(1).start()

    for k in range(1, n):
        given((me + k) % n).wait_send()
    for copy in saves:
        copy.wait()
    units.finish_mixed()
    for h, result in enumerate((result_q, result_k)):
        for k in range(1, n):
            back_to((me + k) % n, h).wait_send()
        keep_own(h).wait()
        for k in range(1, n):
            j = (me + k) % n
            ref = result.at[j]
            remote(ref, ref, out_send.at[8 * h + j], out_recv.at[8 * h + j], chip(me)).wait_recv()


def attention(*args):
    B = CHIP_TOKENS
    L = CHIPS * B

    def shape(*dims):
        return jax.ShapeDtypeStruct(dims, BF16)

    return pl.pallas_call(
        attention_kernel,
        out_shape=(
            shape(CHIPS, B, 2 * HEAD),
            shape(CHIPS, B, 2 * HEAD),
            shape(8, 128, 2048),
            shape(8, 256, 1024),
            shape(8, 128, 1536),
            shape(8, 64, 1024),
            shape(2, 256, D),
            shape(2, 256, D),
            shape(B, D),
            shape(B, D),
            jax.ShapeDtypeStruct((8, 16, 128), F32),
        ),
        in_specs=[HBM] * 9,
        out_specs=(HBM,) * 11,
        scratch_shapes=[
            pltpu.VMEM((128, 3072), BF16),
            pltpu.VMEM((128, 1536), BF16),
            pltpu.VMEM((128, 2048), BF16),
            pltpu.VMEM((256, 1024), BF16),
            pltpu.VMEM((8, 128, 1536), BF16),
            pltpu.VMEM((8, 64, 1024), BF16),
            *[pltpu.VMEM((2, 256, D), BF16)] * 2,
            *[pltpu.VMEM((B, D), BF16)] * 2,
            pltpu.VMEM((8, 16, 128), F32),
            pltpu.VMEM((8, D), F32),
            pltpu.VMEM((8, 1536), F32),
            pltpu.VMEM((2, B, 128), F32),
            *[pltpu.VMEM((CHIPS, B, 4 * HEAD), BF16)] * 2,
            *[pltpu.VMEM((CHIPS, B, 2 * HEAD), BF16)] * 2,
            *[pltpu.VMEM((L, HEAD), BF16)] * 4,
            pltpu.VMEM((L // B, B, B), F32),
            pltpu.VMEM((L // B, B, B), BF16),
            *[pltpu.VMEM((HEAD, L), F32)] * 2,
            *[pltpu.VMEM((B, 128), F32)] * 2,
            *[pltpu.VMEM((B, HEAD), F32)] * 2,
            *[pltpu.SemaphoreType.DMA((CHIPS,))] * 2,
            *[pltpu.SemaphoreType.DMA((2 * CHIPS,))] * 2,
            *[pltpu.SemaphoreType.DMA((37,))] * 2,
            *[pltpu.SemaphoreType.DMA((28,))] * 2,
            pltpu.SemaphoreType.DMA((27,)),
        ],
        compiler_params=pltpu.CompilerParams(
            collective_id=1, has_side_effects=True, vmem_limit_bytes=60 * MIB
        ),
    )(*args)


ORDERS = ("yzx", "zxy", "xyz")
LEADS = ((2, 4), (2, 4), (4, 2))
ROWS = (16, 32, 16)
COLUMNS = (2048, 1024, 2048)


def chunk(n, stage, g, t, h, where):
    y, zl, zh, px = where
    if stage == 0:
        if n == 0:
            return g.at[t, h]
        if n == 1:
            return g.at[pl.ds(2 * h, 2), t % 2, t // 2]
        return g.at[:, h, :, t]
    if stage == 1:
        return (g.at[y, t % 2, t // 2], g.at[:, zl, zh, t], g.at[t, :, :, px])[n]
    return (g.at[y, zl, zh, t], g.at[t, zl, zh, px], g.at[y, t % 2, t // 2, px])[n]


def add_into(dst, terms):
    lead = tuple(dst.shape[:-2])

    def body(k, _):
        at = []
        for extent in reversed(lead):
            at.insert(0, k % extent)
            k = k // extent
        at = (*at, slice(None), slice(None))
        total = dst[at].astype(F32)
        for t in terms:
            total = total + t[at].astype(F32)
        dst[at] = total.astype(BF16)
        return 0

    lax.fori_loop(0, math.prod(lead), body, 0)


def normalised(values):
    values = values.astype(F32)
    centered = values - jnp.mean(values, axis=-1, keepdims=True)
    variance = jnp.mean(centered * centered, axis=-1, keepdims=True)
    scale = lax.rsqrt(variance + epsilon)
    return centered * scale, scale


def rest_kernel(
    tokens_q, tokens_k, x, ct, an, mn, wq, wd, wh, wo, vec, cosine, sine,
    outputs, input_grad, gathered0, gathered1, gathered2, small_out,
    tables, norms, unit_bias, x_v, ct_v, an_v, branches, weighted, sums, small, sm_a, sm_b, pair_send, pair_recv,
    g0, g1, g2, *rest,
):
    grads = (g0, g1, g2)
    gathered = (gathered0, gathered1, gathered2)
    bufs = [(*rest[4 * n : 4 * n + 4], gathered[n]) for n in range(3)]
    wq_v, wd_v, tq_v, tk_v, pg_v, at_v, wh_v, wo_v, act_v, hg_v, turned_v = rest[12:23]
    send, recv, local_sem, sm_send, sm_recv = rest[23:]
    f, s, (y, zl, px, zh, core) = place()
    z = zh * 2 + zl
    coordinate = {"y": y, "z": z, "x": px}
    where = (y, zl, zh, px)
    T = CHIP_TOKENS

    def along(axis, step):
        t = dict(coordinate)
        t[axis] = (t[axis] + step) % 4
        return device(t["y"], t["z"], t["x"], core)

    plus = {a: along(a, 1) for a in "yzx"}
    minus = {a: along(a, 3) for a in "yzx"}
    same_seq = [{"fsdp": (f + k) % 8, "seq": s} for k in range(1, 8)]
    same_fsdp = [{"fsdp": f, "seq": (s + k) % 16} for k in range(1, 16)]
    zother = device(y, 2 * (1 - zh) + 1 - zl, px, core)
    sibling = device(y, z, px, 1 - core)
    sends = []

    def load(src, dst, k):
        copy = pltpu.make_async_copy(src, dst, local_sem.at[k])
        copy.start()
        return copy

    def started(src, dst, k, target):
        copy = remote(src, dst, send.at[k], recv.at[k], target)
        copy.start()
        sends.append(copy)

    def arrived(ref, k):
        remote(ref, ref, send.at[k], recv.at[k], sibling).wait_recv()

    def small_sent(src, dst, k, target):
        copy = remote(src, dst, sm_send.at[k], sm_recv.at[k], target)
        copy.start()
        sends.append(copy)

    def small_arrived(ref, k):
        remote(ref, ref, sm_send.at[k], sm_recv.at[k], sibling).wait_recv()

    def raw_copies(n, stage):
        axis = ORDERS[n][stage]
        p = coordinate[axis]

        def copy(t, h, dst, k, target):
            src = chunk(n, stage, grads[n], t % 4, h, where)
            return remote(src, dst, send.at[k], recv.at[k], target)

        if stage > 0:
            b, got = 26 * n + 3 + 3 * stage, bufs[n][1 + stage]
            return [
                copy(p + k, 0, got.at[k - 1], b + k - 1, along(axis, k)) for k in (2, 1, 3)
            ]
        opp, fin = bufs[n][0:2]
        b = 26 * n
        return [
            copy(p + 2, 0, opp.at[0], b, plus[axis]),
            copy(p + 2, 1, opp.at[1], b + 1, minus[axis]),
            copy(p + 1, 1, fin.at[0, 1], b + 2, plus[axis]),
            copy(p + 3, 0, fin.at[1, 0], b + 3, minus[axis]),
        ]

    def relay_copy(n, h):
        axis = ORDERS[n][0]
        k = 26 * n + 4 + h
        t = coordinate[axis] + 1 + 2 * h
        src = chunk(n, 0, grads[n], t % 4, h, where)
        target = (plus, minus)[h][axis]
        return src, remote(src, bufs[n][1].at[h, h], send.at[k], recv.at[k], target)

    def begin(n, stage):
        for copy in raw_copies(n, stage):
            copy.start()

    def relay(n):
        opp = bufs[n][0]
        for h in range(2):
            mid, copy = relay_copy(n, h)
            arrived(opp.at[h], 26 * n + h)
            add_into(mid, [opp.at[h]])
            copy.start()

    def finish(n, stage):
        p = coordinate[ORDERS[n][stage]]
        if stage > 0:
            b, got = 26 * n + 3 + 3 * stage, bufs[n][1 + stage]
            for k in range(3):
                arrived(got.at[k], b + k)
            mine = chunk(n, stage, grads[n], p, 0, where)
            add_into(mine, [got.at[k] for k in range(3)])
            return
        fin = bufs[n][1]
        b = 26 * n
        arrived(fin.at[0, 1], b + 2)
        arrived(fin.at[1, 0], b + 3)
        arrived(fin.at[0, 0], b + 4)
        arrived(fin.at[1, 1], b + 5)
        for h in range(2):
            add_into(chunk(n, 0, grads[n], p, h, where), [fin.at[0, h], fin.at[1, h]])

    here = pl.ds(pl.multiple_of((px * 2 + zh) * T, T), T)
    pairs = [
        (tokens_q, tq_v),
        (tokens_k, tk_v),
        (cosine.at[here], tables.at[0]),
        (sine.at[here], tables.at[1]),
        (an, an_v),
        (ct, ct_v),
        (wh, wh_v),
        (wo, wo_v),
        (x, x_v),
        (wq, wq_v),
        (wd, wd_v),
    ]
    keeps = [load(a, b, k) for k, (a, b) in enumerate(pairs)]
    barrier(same_seq + same_fsdp + [zother])
    small[...] = jnp.zeros_like(small)
    for r in range(8):
        at = slice(r * 128, r * 128 + 128)
        norms[0:4, at] = vec[r, 0:4, :]
        norms[4:5, at] = vec[r, 7:8, :] + vec[r, 12:13, :]
        for j in range(2):
            unit_bias[0:1, r * 256 + j * 128 : r * 256 + j * 128 + 128] = vec[
                r, pl.ds(8 + 2 * core + j, 1), :
            ]

    def attention_part():
        for copy in keeps[0:6]:
            copy.wait()
        low = lax.broadcasted_iota(jnp.int32, (T, 128), 1) < HEAD
        first = lax.broadcasted_iota(jnp.int32, (1, 128), 1) < HEAD
        rotary = (tables[0], tables[1])
        for pair in range(4):
            for j in range(2):
                r = 2 * pair + j
                at = slice(r * 128, r * 128 + 128)
                qk = jnp.where(low, tq_v[r].astype(F32), tk_v[r].astype(F32))
                turned = turn(qk, rotary, -1.0).astype(BF16)
                pg_v[:, at] = turned
                small[r, pl.ds(4 + core, 1), :] = jnp.sum(turned.astype(F32), axis=0, keepdims=True)
            a, b = [
                jnp.where(low, tk_v[r].astype(F32), tq_v[r].astype(F32))
                for r in (2 * pair, 2 * pair + 1)
            ]
            v = jnp.where(low, a, pltpu.roll(b, 64, 1))
            pg_v[:, 1024 + pair * 128 : 1152 + pair * 128] = v.astype(BF16)
            total = jnp.sum(v, axis=0, keepdims=True)
            moved = jnp.sum(pltpu.roll(v, 64, 1), axis=0, keepdims=True)
            zero = jnp.zeros_like(total)
            at_low = (jnp.where(first, total, zero), jnp.where(first, moved, zero))
            at_high = (jnp.where(first, zero, moved), jnp.where(first, zero, total))
            for j in range(2):
                small[2 * pair + j, 6:7, :] = jnp.where(core == 0, at_low[j], at_high[j])
            o = jnp.where(low, pltpu.roll(a, 64, 1), b)
            at_v[:, pair * 128 : pair * 128 + 128] = o.astype(BF16)

        turned_v[0:D, :] = an_v[...].T
        load_mn = load(mn, an_v, 11)

        def qkv_columns(k, _):
            at = pl.ds(pl.multiple_of(k * 512, 512), 512)
            part = jnp.dot(turned_v[0:D, :], pg_v[:, at], preferred_element_type=F32)
            g2[:, :, :, :, :, at] = part.astype(BF16).reshape(4, 2, 2, 4, 16, 512)
            return 0

        lax.fori_loop(0, 3, qkv_columns, 0)
        turned_v[0:512, :] = at_v[...].T
        for k in range(2):
            part = jnp.dot(
                turned_v[0:512, :], ct_v[:, k * 512 : k * 512 + 512], preferred_element_type=F32
            )
            g2[:, :, k, :, :, 1536:2048] = part.astype(BF16).reshape(4, 2, 4, 16, 512)
        begin(2, 0)
        return load_mn

    def attention_rows():
        for copy in keeps[8:11]:
            copy.wait()
        sums[...] = jnp.zeros_like(sums)

        def half(c, _):
            rows = pl.ds(pl.multiple_of(c * 256, 256), 256)
            grad = lax.dot_general(pg_v[rows, :], wq_v[...], NT, preferred_element_type=F32)
            normed, _ = normalised(x_v[rows, :])
            sums[0:1, :] += jnp.sum(grad * normed, axis=0, keepdims=True)
            sums[1:2, :] += jnp.sum(grad, axis=0, keepdims=True)
            weighted[rows, :] = grad * norms[0:1, :]
            branches[rows, :] = jnp.dot(at_v[rows, :], wd_v[...], preferred_element_type=F32)
            return 0

        lax.fori_loop(0, 2, half, 0)

    def unit_part(load_mn):
        load_mn.wait()
        for copy in keeps[6:8]:
            copy.wait()

        def units(r, _):
            at = pl.ds(pl.multiple_of(r * 256, 256), 256)
            h = jnp.dot(an_v[...], wh_v[:, at], preferred_element_type=F32) + unit_bias[0:1, at]
            below = 0.5 + 0.5 * lax.erf(h * math.sqrt(0.5))
            density = jnp.exp(-0.5 * h * h) * (1.0 / math.sqrt(2.0 * math.pi))
            act_v[:, at] = (h * below).astype(BF16)
            up = lax.dot_general(ct_v[...], wo_v[at, :], NT, preferred_element_type=F32)
            grad = (up * (below + h * density)).astype(BF16)
            hg_v[:, at] = grad
            total = jnp.sum(grad.astype(F32), axis=0, keepdims=True)
            small[r, pl.ds(8 + 2 * core, 1), :] = total[:, 0:128]
            small[r, pl.ds(9 + 2 * core, 1), :] = total[:, 128:256]
            return 0

        lax.fori_loop(0, 8, units, 0)
        turned_v[...] = act_v[...].T

        def output_rows(k, _):
            at = pl.ds(pl.multiple_of(k * 512, 512), 512)
            part = jnp.dot(turned_v[at, :], ct_v[...], preferred_element_type=F32)
            g1[k] = part.astype(BF16).reshape(2, 2, 4, 32, 1024)
            return 0

        lax.fori_loop(0, 4, output_rows, 0)
        begin(1, 0)
        turned_v[0:D, :] = an_v[...].T

        def hidden_columns(k, _):
            at = pl.ds(pl.multiple_of(k * 512, 512), 512)
            part = jnp.dot(turned_v[0:D, :], hg_v[:, at], preferred_element_type=F32)
            g0[:, :, :, :, :, at] = part.astype(BF16).reshape(4, 2, 2, 4, 16, 512)
            return 0

        lax.fori_loop(0, 4, hidden_columns, 0)
        begin(0, 0)

    def unit_rows():
        def half(c, _):
            rows = pl.ds(pl.multiple_of(c * 256, 256), 256)
            grad = lax.dot_general(hg_v[rows, :], wh_v[...], NT, preferred_element_type=F32)
            normed, _ = normalised(x_v[rows, :])
            sums[2:3, :] += jnp.sum(grad * normed, axis=0, keepdims=True)
            sums[3:4, :] += jnp.sum(grad, axis=0, keepdims=True)
            weighted[rows, :] += grad * norms[2:3, :]
            branches[rows, :] += jnp.dot(act_v[rows, :], wo_v[...], preferred_element_type=F32)
            return 0

        lax.fori_loop(0, 2, half, 0)

    unit_part(attention_part())
    relay(2)
    attention_rows()
    unit_rows()

    other = pl.ds(pl.multiple_of((1 - core) * 256, 256), 256)
    mine = pl.ds(pl.multiple_of(core * 256, 256), 256)
    pair_send[0] = branches[other, :].astype(BF16)
    pair_send[1] = weighted[other, :].astype(BF16)
    started(pair_send, pair_recv, 78, sibling)
    sums[4:5, :] = jnp.sum(ct_v[mine, :].astype(F32), axis=0, keepdims=True)
    for r in range(8):
        at = slice(r * 128, r * 128 + 128)
        small[r, 0:4, :] = sums[0:4, at]
        small[r, 7:8, :] = sums[4:5, at]
    for k in range(1, 8):
        small_sent(small.at[(f + k) % 8], sm_a.at[k], k, same_seq[k - 1])
    relay(1)
    relay(0)
    arrived(pair_recv, 78)
    normed, scale = normalised(x_v[mine, :])
    total = x_v[mine, :].astype(F32) + branches[mine, :] + pair_recv[0].astype(F32) + norms[4:5, :]
    outputs[...] = total.astype(BF16)
    w = weighted[mine, :] + pair_recv[1].astype(F32)
    input_grad[...] = ct_v[mine, :].astype(F32) + scale * (
        w
        - jnp.mean(w, axis=-1, keepdims=True)
        - normed * jnp.mean(w * normed, axis=-1, keepdims=True)
    )
    for k in range(1, 8):
        small_arrived(sm_a.at[k], k)
    total = small[f]
    for k in range(1, 8):
        total = total + sm_a[k]
    sm_b[0] = total
    for k in range(1, 16):
        small_sent(sm_b.at[0], sm_b.at[k], 7 + k, same_fsdp[k - 1])

    across = device(y, (z + 2) % 4, px, core)
    xp, xm = plus["x"], minus["x"]

    def at_chip(n, zz, xx):
        return bufs[n][4].at[core, zz * 4 + xx % 4]

    def spread(n):
        b = 26 * n + 18
        done = grads[n].at[y, zl, zh, px]
        place_ = at_chip(n, zh, px)
        keep = pltpu.make_async_copy(done, place_, local_sem.at[12 + n])
        keep.start()
        started(done, place_, b, across)
        started(done, place_, b + 1, xp)
        started(done, place_, b + 2, xm)
        return keep

    def spread_on(n):
        b = 26 * n + 18
        theirs = at_chip(n, 1 - zh, px)
        arrived(theirs, b)
        started(theirs, theirs, b + 3, xp)
        started(theirs, theirs, b + 4, xm)
        left, right = at_chip(n, zh, px + 3), at_chip(n, 1 - zh, px + 1)
        arrived(left, b + 1)
        started(left, left, b + 5, xp)
        arrived(right, b + 4)
        started(right, right, b + 6, xm)

    def spread_end(n, keep):
        b = 26 * n + 18
        arrived(at_chip(n, zh, px + 1), b + 2)
        arrived(at_chip(n, 1 - zh, px + 3), b + 3)
        arrived(at_chip(n, zh, px + 2), b + 5)
        arrived(at_chip(n, 1 - zh, px + 2), b + 6)
        keep.wait()
        whole = bufs[n][4].at[core]
        started(whole, whole, b + 7, sibling)

    finish(2, 0)
    begin(2, 1)
    finish(1, 0)
    begin(1, 1)
    finish(0, 0)
    begin(0, 1)
    finish(2, 1)
    begin(2, 2)
    finish(1, 1)
    begin(1, 2)
    finish(0, 1)
    begin(0, 2)
    finish(2, 2)
    keep2 = spread(2)
    finish(1, 2)
    keep1 = spread(1)
    finish(0, 2)
    keep0 = spread(0)
    spread_on(2)
    spread_end(2, keep2)
    spread_on(1)
    spread_on(0)
    spread_end(1, keep1)
    spread_end(0, keep0)
    for k in range(1, 16):
        small_arrived(sm_b.at[k], 7 + k)
    total = sm_b[0]
    for k in range(1, 16):
        total = total + sm_b[k]
    small_out[...] = total

    for n in (2, 1, 0):
        arrived(gathered[n].at[1 - core], 26 * n + 25)
    for copy in sends:
        copy.wait_send()
    for n in range(3):
        for stage in range(3):
            for copy in raw_copies(n, stage):
                copy.wait_send()
        for h in range(2):
            relay_copy(n, h)[1].wait_send()


def rest_of_block(*args):
    scratch = []
    for lead, R, C in zip(LEADS, ROWS, COLUMNS):
        for dims in (
            (2, *lead, R, C),
            (2, 2, *lead, R, C),
            (3, *((2, 2) if lead == (4, 2) else (4,)), R, C),
            (3, R, C),
        ):
            scratch.append(pltpu.VMEM(dims, BF16))
    T = CHIP_TOKENS
    return pl.pallas_call(
        rest_kernel,
        out_shape=(
            jax.ShapeDtypeStruct((256, D), BF16),
            jax.ShapeDtypeStruct((256, D), F32),
            *[jax.ShapeDtypeStruct((2, 8, R, C), BF16) for R, C in zip(ROWS, COLUMNS)],
            jax.ShapeDtypeStruct((16, 128), F32),
        ),
        in_specs=[HBM] * 10 + [VMEM, HBM, HBM],
        out_specs=(VMEM, VMEM, HBM, HBM, HBM, VMEM),
        scratch_shapes=[
            pltpu.VMEM((2, T, 128), F32),
            pltpu.VMEM((8, D), F32),
            pltpu.VMEM((8, 2048), F32),
            *[pltpu.VMEM((T, D), BF16)] * 3,
            *[pltpu.VMEM((T, D), F32)] * 2,
            pltpu.VMEM((8, D), F32),
            pltpu.VMEM((8, 16, 128), F32),
            pltpu.VMEM((8, 16, 128), F32),
            pltpu.VMEM((16, 16, 128), F32),
            *[pltpu.VMEM((2, 256, D), BF16)] * 2,
            *[pltpu.VMEM((4, 2, 2, 4, R, C), BF16) for R, C in zip(ROWS, COLUMNS)],
            *scratch,
            pltpu.VMEM((D, 1536), BF16),
            pltpu.VMEM((512, D), BF16),
            *[pltpu.VMEM((8, T, 128), BF16)] * 2,
            pltpu.VMEM((T, 1536), BF16),
            pltpu.VMEM((T, 512), BF16),
            pltpu.VMEM((D, 2048), BF16),
            pltpu.VMEM((2048, D), BF16),
            *[pltpu.VMEM((T, 2048), BF16)] * 2,
            pltpu.VMEM((2048, T), BF16),
            pltpu.SemaphoreType.DMA((79,)),
            pltpu.SemaphoreType.DMA((79,)),
            pltpu.SemaphoreType.DMA((18,)),
            pltpu.SemaphoreType.DMA((23,)),
            pltpu.SemaphoreType.DMA((23,)),
        ],
        compiler_params=pltpu.CompilerParams(
            collective_id=2, has_side_effects=True, vmem_limit_bytes=62 * MIB
        ),
    )(*args)


def position_tables():
    half = ROT // 2
    frequency = np.power(10000.0, -2.0 * np.arange(half) / ROT).astype(np.float32)
    angles = np.arange(CHIPS * CHIP_TOKENS, dtype=np.float32)[:, None] * frequency[None, :]
    angles = angles.astype(np.float64)
    cosine = np.ones((CHIPS * CHIP_TOKENS, 2 * HEAD), np.float32)
    sine = np.zeros((CHIPS * CHIP_TOKENS, 2 * HEAD), np.float32)
    for at in (0, HEAD):
        cosine[:, at : at + half] = cosine[:, at + half : at + ROT] = np.cos(angles)
        sine[:, at : at + half] = -np.sin(angles)
        sine[:, at + half : at + ROT] = np.sin(angles)
    return cosine, sine


def turn(values, tables, sign):
    lane = lax.broadcasted_iota(jnp.int32, values.shape, 1) % HEAD
    moved = jnp.where(lane < ROT // 2, pltpu.roll(values, 120, 1), pltpu.roll(values, 8, 1))
    return values * tables[0] + sign * (moved * tables[1])


def finals_kernel(
    h0, h1, h2, out_in, grad_in, sums, hidden, output, qkv, dense, out_ref, grad_ref, *rest
):
    vectors, (a0, a1, a2, sem) = rest[:8], rest[8:]
    loads = [
        pltpu.make_async_copy(a, b, sem.at[k])
        for k, (a, b) in enumerate(
            [(h2, a2), (h0, a0), (h1, a1), (out_in, out_ref), (grad_in, grad_ref)]
        )
    ]
    for copy in loads:
        copy.start()
    loads[0].wait()
    low = lax.broadcasted_iota(jnp.int32, (128, 128), 1) < HEAD
    for pair in range(4):
        at = slice(1024 + pair * 128, 1152 + pair * 128)
        v0 = a2[0, :, :, at].reshape(128, 128).astype(F32)
        v1 = a2[1, :, :, at].reshape(128, 128).astype(F32)
        for j in range(2):
            r = 2 * pair + j
            q0 = a2[0, :, :, r * 128 : r * 128 + 128].reshape(128, 128).astype(F32)
            q1 = a2[1, :, :, r * 128 : r * 128 + 128].reshape(128, 128).astype(F32)
            q1 = pltpu.roll(q1, 64, 1)
            left = v0 if j == 0 else pltpu.roll(v0, 64, 1)
            right = pltpu.roll(v1, 64, 1) if j == 0 else v1
            qkv[:, r * 384 : r * 384 + 128] = q0
            qkv[:, r * 384 + 128 : r * 384 + 256] = jnp.where(low, left, q1)
            qkv[:, r * 384 + 256 : r * 384 + 384] = jnp.where(low, q1, right)
    for c in range(2):
        for k in range(2):
            piece = a2[c, k * 4 : k * 4 + 4, :, 1536:2048].reshape(64, 512)
            dense[c * 64 : c * 64 + 64, k * 512 : k * 512 + 512] = piece.astype(F32)
    loads[1].wait()
    for c in range(2):
        for r in range(8):
            piece = a0[c, :, :, r * 256 : r * 256 + 256].reshape(128, 256)
            hidden[:, r * 512 + c * 256 : r * 512 + c * 256 + 256] = piece.astype(F32)
    loads[2].wait()
    output[...] = a1[...].reshape(512, D).astype(F32)
    loads[3].wait()
    loads[4].wait()
    for k in range(4):
        vectors[k][...] = sums[k : k + 1, :]
    first = lax.broadcasted_iota(jnp.int32, (1, 128), 1) < HEAD
    q1 = pltpu.roll(sums[5:6, :], 64, 1)
    vectors[4][:, 0:128] = sums[4:5, :]
    vectors[4][:, 128:256] = jnp.where(first, sums[6:7, :], q1)
    vectors[4][:, 256:384] = jnp.where(first, q1, sums[6:7, :])
    vectors[5][...] = sums[7:8, :]
    vectors[7][...] = sums[7:8, :]
    for k in range(4):
        vectors[6][:, k * 128 : k * 128 + 128] = sums[8 + k : 9 + k, :]


def finals(a0, a1, a2, outputs, input_grad, sums):
    widths = (128, 128, 128, 128, 384, 128, 512, 128)
    return pl.pallas_call(
        finals_kernel,
        out_shape=(
            jax.ShapeDtypeStruct((128, FF), F32),
            jax.ShapeDtypeStruct((512, D), F32),
            jax.ShapeDtypeStruct((128, 3 * D), F32),
            jax.ShapeDtypeStruct((128, D), F32),
            jax.ShapeDtypeStruct((256, D), BF16),
            jax.ShapeDtypeStruct((256, D), F32),
            *[jax.ShapeDtypeStruct((1, w), F32) for w in widths],
        ),
        in_specs=[HBM] * 5 + [VMEM],
        out_specs=(VMEM,) * 14,
        scratch_shapes=[
            *[pltpu.VMEM((2, 8, R, C), BF16) for R, C in zip(ROWS, COLUMNS)],
            pltpu.SemaphoreType.DMA((5,)),
        ],
        compiler_params=pltpu.CompilerParams(vmem_limit_bytes=60 * MIB),
    )(a0, a1, a2, outputs, input_grad, sums)


def local(
    inputs,
    cotangent,
    ln_attn_gain,
    ln_attn_bias,
    ln_mlp_gain,
    ln_mlp_bias,
    qkv_weight,
    qkv_bias,
    dense_weight,
    dense_bias,
    hidden_weight,
    hidden_bias,
    output_weight,
    output_bias,
):
    bias = qkv_bias.reshape(2, 192)
    small = jnp.zeros((16, 128), F32)
    for k, rows in (
        (0, ln_attn_gain),
        (1, ln_attn_bias),
        (2, ln_mlp_gain),
        (3, ln_mlp_bias),
        (4, bias[:, :128]),
        (6, bias[:, 128:]),
        (7, dense_bias),
        (8, hidden_bias),
        (12, output_bias),
    ):
        rows = rows.reshape(-1, 128).astype(F32)
        small = small + jnp.pad(rows, ((k, 16 - k - rows.shape[0]), (0, 0)))
    cosine, sine = (jnp.asarray(t) for t in position_tables())
    tokens_q, tokens_k, wh, wo, wq, wd, x, ct, attn_normed, mlp_normed, vectors = attention(
        qkv_weight,
        dense_weight,
        hidden_weight,
        output_weight,
        small,
        inputs,
        cotangent,
        cosine,
        sine,
    )
    outputs, input_grad, *gathered, sums = rest_of_block(
        tokens_q,
        tokens_k,
        x.reshape(CHIP_TOKENS, D),
        ct.reshape(CHIP_TOKENS, D),
        attn_normed,
        mlp_normed,
        wq.reshape(D, 1536),
        wd.reshape(512, D),
        wh.reshape(D, 2048),
        wo.reshape(2048, D),
        vectors,
        cosine,
        sine,
    )
    hidden, output, qkv, dense, outputs, input_grad, *vectors = finals(
        *gathered, outputs, input_grad, sums
    )
    ag, ab, mg, mb, qb, db, hb, ob = (v.reshape(v.shape[1]) for v in vectors)
    return (outputs, input_grad, ag, ab, mg, mb, qkv, qb, dense, db, hidden, hb, output, ob)


def solution(mesh):
    rows = P(("fsdp", "seq"), None)
    vector = P("fsdp")
    matrix = P("fsdp", None)
    shared = (vector,) * 4 + (matrix, vector) * 4
    return jax.shard_map(
        local,
        mesh=mesh,
        in_specs=(rows, rows, *shared),
        out_specs=(rows, rows, *shared),
        check_vma=False,
    )
```
